512 devices in a mesh: member: 16 (over y, z_hi, core), gx: 32 (over x, z_lo).
Axes of the slice: x: 4, y: 4, z: 16 (z_hi: 2, z_lo: 8; z = z_hi * 8 + z_lo), core: 2. Of those that a mesh axis runs over, the one named last changes fastest.
Arguments:
- features: bfloat16 [16, 64, 8, 32, 128], P('member', 'gx'), may hold values from -6 to 6
- cotangent: bfloat16 [16, 64, 8, 32, 128], P('member', 'gx'), may hold values from -6 to 6
- keep_flags: int32 [16, 3], P('member'), may hold values from 0 to 1, as said below
- conv_a: bfloat16 [27, 128, 128], replicated, may hold values from -0.109375 to 0.109375
- conv_b: bfloat16 [27, 128, 128], replicated, may hold values from -0.109375 to 0.109375
- conv_c: bfloat16 [27, 512, 512], P(None, None, 'gx'), may hold values from -0.1875 to 0.1875
- lift_one: bfloat16 [128, 128], replicated, may hold values from -0.5 to 0.5
- lift_two: bfloat16 [128, 512], replicated, may hold values from -0.5 to 0.5
- lower_two: bfloat16 [512, 128], replicated, may hold values from -0.25 to 0.25
- lower_one: bfloat16 [128, 128], replicated, may hold values from -0.5 to 0.5
Outputs:
- result: bfloat16 [16, 64, 8, 32, 128], P('member', 'gx')
- grad_conv_a: float32 [27, 128, 128], P(None, None, 'gx')
- grad_conv_b: float32 [27, 128, 128], P(None, None, 'gx')
- grad_conv_c: float32 [27, 512, 512], P(None, None, 'gx')
The draws below stay inside these ranges and needn't reach their ends.
Inputs may be any that keep to these rules, and one draw needn't show every extreme that they name: `keep_flags`: 1 where the member keeps the block, 0 where it is dropped; every block is kept by at least one member.
All inputs are finite; a program needn't handle non-finite values.
Results may differ from the reference program's by a relative error of at most 0.024.
Values may be sent and summed in bfloat16 or wider, within the bound.
A program may use at most 64 MiB of HBM per device.

```python
import jax
import jax.numpy as jnp
from jax import lax

C1 = 128
C2 = 128
C3 = 512
Y = 8
Z = 32
NX = 64
MEMBERS = 16


def draw_keep_flags(key, part):
    key = jax.random.fold_in(key, 7)
    first_key, second_key = jax.random.split(key)
    rolls = jax.random.randint(first_key, (MEMBERS, 3), 0, 10)
    limits = jnp.array([9, 8, 7], jnp.int32)
    kept = (rolls < limits[None, :]).astype(jnp.int32)
    chosen = jax.random.randint(second_key, (3,), 0, MEMBERS)
    forced = (jnp.arange(MEMBERS)[:, None] == chosen[None, :]).astype(jnp.int32)
    return jnp.maximum(kept, forced)


def spiked(values, stream_key, source, target, parts, factor):
    owner, partner = [(jnp.arange(values.shape[dim]) // (values.shape[dim] // parts)).reshape([-1 if axis == dim else 1 for axis in range(values.ndim)]) for dim in (source, target)]
    chosen = jax.random.permutation(stream_key, parts)[partner]
    strong = (owner == chosen) | (owner == (partner + parts // 2) % parts)
    return jnp.where(strong, factor * values, values)


def block_scale(key, extent, shards, low, top_value):
    level = 1.0
    for dim, parts in shards:
        steps = jax.random.uniform(jax.random.fold_in(jax.random.fold_in(key, 6), dim), (parts,), jnp.float32, low / len(shards), top_value / len(shards))
        level = level * jnp.repeat(jnp.exp(steps), extent[dim] // parts).reshape((-1,) + (1,) * (len(extent) - 1 - dim))
    return level


def scatter_about(rng, shape, width, most, shards=(), held_as=jnp.bfloat16):
    drawn = jax.random.normal(rng, shape, jnp.float32) * width
    if len(shards) > 0:
        drawn = block_scale(rng, shape, shards, -0.22, 0.18) * drawn
    return jnp.clip(drawn, min=-most, max=most).astype(held_as)


def bell_draw_with(own_key, shape, deviation, limit, cuts, heavy, held_as=jnp.bfloat16):
    drawn = deviation * jax.random.normal(own_key, shape, jnp.float32)
    if cuts:
        drawn = drawn * block_scale(own_key, shape, cuts, -0.22, 0.18)
    return jnp.clip(spiked(drawn, jax.random.fold_in(own_key, 3), *heavy), -limit, limit).astype(held_as)


def setup_inputs(seed: int = 0) -> dict:
    splits = jax.random.split(jax.random.key(seed), 11)
    return {
        "features": scatter_about(splits[0], (MEMBERS, NX, Y, Z, C1), 1.0, 6.0, ((0, 16), (1, 32))),
        "cotangent": bell_draw_with(splits[1], (MEMBERS, NX, Y, Z, C1), 1.0, 6.0, ((0, 16), (1, 32)), (1, 4, 32, 2.75)),
        "keep_flags": draw_keep_flags(jax.random.fold_in(splits[10], 71), 0),
        "conv_a": scatter_about(splits[3], (27, C1, C1), (27 * C1) ** -0.5, 0.109375),
        "conv_b": scatter_about(splits[4], (27, C2, C2), (27 * C2) ** -0.5, 0.109375),
        "conv_c": scatter_about(splits[5], (27, C3, C3), (2 * C3) ** -0.5, 0.1875, ((2, 32),)),
        "lift_one": scatter_about(splits[6], (C1, C2), C1 ** -0.5, 0.5),
        "lift_two": scatter_about(splits[7], (C2, C3), C2 ** -0.5, 0.5),
        "lower_two": scatter_about(splits[8], (C3, C2), C3 ** -0.5, 0.25),
        "lower_one": scatter_about(splits[9], (C2, C1), C2 ** -0.5, 0.5),
    }


survival = (0.9, 0.8, 0.7)


def offsets(position):
    return position // 9 - 1, (position // 3) % 3 - 1, position % 3 - 1


def padded3(field_in):
    return jnp.pad(field_in, ((1, 1), (1, 1), (1, 1), (0, 0)))


def window(padded, grid_shape, shift_x, shift_y, shift_z):
    return padded[1 + shift_x:1 + shift_x + grid_shape[0], 1 + shift_y:1 + shift_y + grid_shape[1], 1 + shift_z:1 + shift_z + grid_shape[2], :]


def flatten(field_in):
    return field_in.reshape(-1, field_in.shape[-1])


def project(field_in, matrix):
    return jnp.dot(flatten(field_in), matrix, preferred_element_type=jnp.float32).reshape(field_in.shape[:-1] + (matrix.shape[1],))


def convolve(hidden, weight):
    padded = padded3(hidden)
    running = jnp.zeros(hidden.shape[:3] + (weight.shape[2],), jnp.float32)
    for position in range(27):
        shift_x, shift_y, shift_z = offsets(position)
        window_piece = window(padded, hidden.shape, shift_x, shift_y, shift_z)
        running = running + project(window_piece, weight[position])
    return running


def convolve_back(gradient, weight):
    padded = padded3(gradient)
    running = jnp.zeros(gradient.shape[:3] + (weight.shape[1],), jnp.float32)
    for position in range(27):
        shift_x, shift_y, shift_z = offsets(position)
        window_piece = window(padded, gradient.shape, -shift_x, -shift_y, -shift_z)
        running = running + project(window_piece, weight[position].T)
    return running


def weight_grads(hidden, gradient):
    padded = padded3(hidden)
    results = []
    for position in range(27):
        shift_x, shift_y, shift_z = offsets(position)
        window_piece = window(padded, hidden.shape, shift_x, shift_y, shift_z)
        results.append(jnp.dot(flatten(window_piece).T, flatten(gradient), preferred_element_type=jnp.float32))
    return jnp.stack(results, axis=0)


def slope(value):
    logistic = jax.nn.sigmoid(value)
    return logistic * (1.0 + value * (1.0 - logistic))


def mean_yz(field_in):
    sizes_now = field_in.shape
    return field_in.astype(jnp.float32).reshape(sizes_now[0], sizes_now[1] // 2, 2, sizes_now[2] // 2, 2, sizes_now[3]).mean(axis=(2, 4))


def sum_yz(field_in):
    sizes_now = field_in.shape
    return field_in.astype(jnp.float32).reshape(sizes_now[0], sizes_now[1] // 2, 2, sizes_now[2] // 2, 2, sizes_now[3]).sum(axis=(2, 4))


def mean_pairs(field_in):
    sizes_now = field_in.shape
    return field_in.astype(jnp.float32).reshape((sizes_now[0] // 2, 2) + sizes_now[1:]).mean(axis=1)


def sum_pairs(field_in):
    sizes_now = field_in.shape
    return field_in.astype(jnp.float32).reshape((sizes_now[0] // 2, 2) + sizes_now[1:]).sum(axis=1)


def mean_cubes(field_in):
    sizes_now = field_in.shape
    return field_in.astype(jnp.float32).reshape(sizes_now[0] // 2, 2, sizes_now[1] // 2, 2, sizes_now[2] // 2, 2, sizes_now[3]).mean(axis=(1, 3, 5))


def sum_cubes(field_in):
    sizes_now = field_in.shape
    return field_in.astype(jnp.float32).reshape(sizes_now[0] // 2, 2, sizes_now[1] // 2, 2, sizes_now[2] // 2, 2, sizes_now[3]).sum(axis=(1, 3, 5))


def grow_cubes(field_in):
    return jnp.repeat(jnp.repeat(jnp.repeat(field_in, 2, axis=0), 2, axis=1), 2, axis=2)


def reference(features, cotangent, keep_flags, conv_a, conv_b, conv_c, lift_one, lift_two, lower_two, lower_one):
    bf16 = jnp.bfloat16
    f32 = jnp.float32

    def one_member(totals, inputs):
        feature, upstream, keep_row = inputs
        scales = keep_row.astype(f32) / jnp.array(survival, f32)
        hidden_a = jax.nn.silu(feature.astype(f32)).astype(bf16)
        level_a = feature.astype(f32) + scales[0] * convolve(hidden_a, conv_a)
        pooled_one = mean_cubes(level_a).astype(bf16)
        level_in_b = project(pooled_one, lift_one).astype(bf16)
        hidden_b = jax.nn.silu(level_in_b.astype(f32)).astype(bf16)
        level_b = level_in_b.astype(f32) + scales[1] * convolve(hidden_b, conv_b)
        halves_b = mean_yz(level_b)
        pooled_two = mean_pairs(halves_b).astype(bf16)
        level_in_c = project(pooled_two, lift_two).astype(bf16)
        hidden_c = jax.nn.silu(level_in_c.astype(f32)).astype(bf16)
        level_c = (level_in_c.astype(f32) + scales[2] * convolve(hidden_c, conv_c)).astype(bf16)
        level_d = (level_b + grow_cubes(project(level_c, lower_two))).astype(bf16)
        result = (level_a + grow_cubes(project(level_d, lower_one))).astype(bf16)
        grad_e1 = sum_cubes(upstream).astype(bf16)
        grad_d = project(grad_e1, lower_one.T).astype(bf16)
        grad_halves = sum_yz(grad_d)
        grad_e2 = sum_pairs(grad_halves).astype(bf16)
        grad_c = project(grad_e2, lower_two.T).astype(bf16)
        weight_c = scales[2] * weight_grads(hidden_c, grad_c)
        back_c = convolve_back(grad_c, conv_c)
        grad_q = (grad_c.astype(f32) + scales[2] * slope(level_in_c.astype(f32)) * back_c).astype(bf16)
        grad_m2 = project(grad_q, lift_two.T).astype(bf16)
        grad_b = (grad_d.astype(f32) + grow_cubes(grad_m2.astype(f32)) / 8.0).astype(bf16)
        weight_b = scales[1] * weight_grads(hidden_b, grad_b)
        back_b = convolve_back(grad_b, conv_b)
        grad_p = (grad_b.astype(f32) + scales[1] * slope(level_in_b.astype(f32)) * back_b).astype(bf16)
        grad_m1 = project(grad_p, lift_one.T).astype(bf16)
        grad_a = (upstream.astype(f32) + grow_cubes(grad_m1.astype(f32)) / 8.0).astype(bf16)
        weight_a = scales[0] * weight_grads(hidden_a, grad_a)
        return (totals[0] + weight_a, totals[1] + weight_b, totals[2] + weight_c), result

    initial = (jnp.zeros(conv_a.shape, f32), jnp.zeros(conv_b.shape, f32), jnp.zeros(conv_c.shape, f32))
    totals, results = lax.scan(one_member, initial, (features, cotangent, keep_flags))
    return results, totals[0], totals[1], totals[2]
```

```python
import jax
import jax.numpy as jnp
from jax import lax
from jax.experimental import pallas as pl
from jax.experimental.pallas import tpu as pltpu
from jax.sharding import PartitionSpec as P

f32 = jnp.float32
bf16 = jnp.bfloat16
MESH = pl.DeviceIdType.MESH

NY, NZH, NCORE, NXC, NZL = 4, 2, 2, 4, 8
NZ = NZH * NZL
SURVIVAL = (0.9, 0.8, 0.7)

COPIES = dict(
    halo_a=2,
    halo_b=2,
    halo_d=2,
    bz=7,
    bx=3,
    fz=7,
    fx=3,
    cot=4,
    cot_f=3,
    hid=4,
    hid_f=3,
    hb=7,
    gb=7,
    m1=7,
    rxb=3,
    rxf=3,
    rzb=7,
    rzf=7,
    a_x=3,
    a_z=15,
    a_all=7,
    b_x=3,
    b_z=15,
    b_all=7,
    c_core=1,
    c_y=3,
    c_zh=1,
    c_ay=3,
    c_ac=1,
)


class S:
    pass


TOTAL = 0
for _name, _count in COPIES.items():
    setattr(S, _name, TOTAL)
    TOTAL += _count
KINDS = ((S.a_x, S.a_z, S.a_all), (S.b_x, S.b_z, S.b_all))

NN = (((1,), (0,)), ((), ()))
NT = (((1,), (1,)), ((), ()))
TN = (((0,), (0,)), ((), ()))


def mm(a, b, dims=NN):
    return lax.dot_general(a, b, dims, preferred_element_type=f32)


def silu(v):
    return v * jax.nn.sigmoid(v)


def slope(v):
    s = jax.nn.sigmoid(v)
    return s * (1.0 + v * (1.0 - s))


SCRATCH = dict(
    fv=((2, 8, 32, 128), bf16),
    cv=((2, 8, 32, 128), bf16),
    kv=((1, 3), jnp.int32),
    wa=((9, 384, 128), bf16),
    wb=((9, 384, 128), bf16),
    wc=((432, 512), bf16),
    l1=((128, 128), bf16),
    l2=((128, 512), bf16),
    w2=((512, 128), bf16),
    w1=((128, 128), bf16),
    rv=((2, 8, 32, 128), bf16),
    halo_a=((2, 8, 32, 128), bf16),
    hraw=((8, 4, 8, 32, 128), bf16),
    hs=((8, 3, 4, 10, 32, 128), bf16),
    la=((2, 256, 128), f32),
    pool_s=((128, 128), f32),
    grow_s=((128, 128), f32),
    hb_own=((64, 128), bf16),
    halo_b=((2, 64, 128), bf16),
    hbraw=((8, 3, 64, 128), bf16),
    hsb=((8, 3, 3, 6, 16, 128), bf16),
    small_s=((32, 128), f32),
    gd_own=((64, 128), bf16),
    halo_d=((2, 64, 128), bf16),
    bz_buf=((8, 16, 128), bf16),
    ge=((18, 16, 128), bf16),
    fz_buf=((8, 16, 128), bf16),
    fx_buf=((4, 4, 16, 128), bf16),
    st=((448, 256), bf16),
    mp=((18, 16, 128), bf16),
    up=((16, 16, 128), bf16),
    rxb=((3, 6, 16, 128), bf16),
    rxf=((3, 4, 16, 128), bf16),
    sb=((6, 16, 128), bf16),
    sf=((4, 16, 128), bf16),
    rzb=((7, 2, 16, 128), bf16),
    rzf=((7, 16, 128), bf16),
    gbs=((3, 3, 6, 16, 128), bf16),
    cq=((8, 128, 512), bf16),
    gbq=((8, 64, 128), bf16),
    m1q=((8, 64, 128), bf16),
    gt=((8, 128, 512), bf16),
    xs=((2, 4, 4, 32, 128), bf16),
    xr=((2, 3, 4, 32, 128), bf16),
    zs=((2, 8, 16, 128), bf16),
    zr=((2, 16, 16, 128), bf16),
    zt=((2, 16, 128), f32),
    c_own=((224, 128), bf16),
    dc=((2, 4, 224, 128), bf16),
    c_cr=((4, 224, 128), bf16),
    c_ys=((4, 224, 128), bf16),
    c_yr=((3, 224, 128), bf16),
    c_zs=((224, 128), bf16),
    c_zr=((224, 128), bf16),
)


class Bufs:
    pass


def kernel(
    feat_h,
    cot_h,
    keep_h,
    wa_h,
    wb_h,
    wc_h,
    l1_h,
    l2_h,
    w2_h,
    w1_h,
    res,
    fga,
    fgb,
    fgc,
    *scratch,
):
    b = Bufs()
    for name, ref in zip(SCRATCH, scratch):
        setattr(b, name, ref)
    local_sem, send_sem, recv_sem = scratch[len(SCRATCH) :]

    m = lax.axis_index("member")
    g = lax.axis_index("gx")
    x, z = g // NZL, g % NZL
    core, zh, y = m % NCORE, (m // NCORE) % NZH, m // (NCORE * NZH)
    z16 = zh * NZL + z
    q = y * 2 + core

    def dev(dy=None, dzh=None, dcore=None, dx=None, dz=None):
        yy = y if dy is None else dy
        hh = zh if dzh is None else dzh
        cc = core if dcore is None else dcore
        xx = x if dx is None else dx
        zz = z if dz is None else dz
        return ((yy * NZH + hh) * NCORE + cc, xx * NZL + zz)

    nxt = (m, (g + 1) % (NXC * NZL))
    prv = (m, (g + NXC * NZL - 1) % (NXC * NZL))
    x_of = [(x + k) % NXC for k in range(NXC)]
    z_of = [(z + k) % NZL for k in range(NZL)]
    y_of = [(y + k) % NY for k in range(NY)]
    y_from = [(y + NY - k) % NY for k in range(NY)]
    z16_of = [(z16 + k) % NZ for k in range(NZ)]
    group_of = [(y_of[k // 2], (core + k) % 2) for k in range(8)]
    group_dev = [dev(dy=yy, dcore=cc) for yy, cc in group_of]
    sibling = dev(dcore=1 - core)

    barrier = pltpu.get_barrier_semaphore()
    targets = [prv, nxt]
    targets += [dev(dx=x_of[k]) for k in range(1, NXC)]
    targets += [dev(dzh=z16_of[k] // NZL, dz=z16_of[k] % NZL) for k in range(1, NZ)]
    targets += group_dev[1:]
    for target in targets:
        pl.semaphore_signal(barrier, inc=1, device_id=target, device_id_type=MESH)

    started = []

    def finish(count):
        for copy in started[:count]:
            copy.wait_send()
        del started[:count]

    def send(name, k, src, dst, target):
        index = name + k
        copy = pltpu.make_async_remote_copy(
            src_ref=src,
            dst_ref=dst,
            send_sem=send_sem.at[index],
            recv_sem=recv_sem.at[index],
            device_id=target,
            device_id_type=MESH,
        )
        copy.start()
        started.append(copy)
        return copy

    def arrived(copies):
        for copy in copies:
            copy.wait_recv()

    loads = Bufs()

    def load_all(first, **sources):
        for k, (name, src) in enumerate(sources.items()):
            load = pltpu.make_async_copy(src, getattr(b, name), local_sem.at[first + k])
            load.start()
            setattr(loads, name, load)

    load_all(0, fv=feat_h.at[0], wa=wa_h)
    pl.semaphore_wait(barrier, len(targets))
    halo_a_copies = [
        send(S.halo_a, 0, feat_h.at[0, 1], b.halo_a.at[0], nxt),
        send(S.halo_a, 1, feat_h.at[0, 0], b.halo_a.at[1], prv),
    ]
    load_all(2, cv=cot_h.at[0], w1=w1_h, kv=keep_h, l1=l1_h, wb=wb_h, w2=w2_h, wc=wc_h, l2=l2_h)

    has_prev = (g > 0).astype(f32)
    has_next = (g < NXC * NZL - 1).astype(f32)

    def z_shifts(h, length):
        rows = h.shape[0]
        pos = lax.broadcasted_iota(jnp.int32, h.shape, 0) % length
        before = jnp.where(pos == 0, 0.0, pltpu.roll(h, 1, 0))
        after = jnp.where(pos == length - 1, 0.0, pltpu.roll(h, rows - 1, 0))
        return before, h, after

    def put(cat, plane, h, grid_y, grid_z):
        for k, piece in enumerate(z_shifts(h, grid_z)):
            cat[k, plane, 1 : 1 + grid_y] = piece.astype(bf16).reshape(grid_y, grid_z, 128)

    def pool_yz(v, grid_y, grid_z, scratch_ref):
        half = v.reshape(grid_y // 2, 2, grid_z, 128).sum(axis=1)
        n = grid_y // 2 * grid_z
        scratch_ref[0:n, :] = half.reshape(n, 128)
        even = scratch_ref[pl.ds(0, n // 2, stride=2), :]
        return even + scratch_ref[pl.ds(1, n // 2, stride=2), :]

    def grow_yz(v, grid_y, grid_z, scratch_ref):
        n = grid_y * grid_z
        scratch_ref[pl.ds(0, n, stride=2), :] = v
        scratch_ref[pl.ds(1, n, stride=2), :] = v
        wide = scratch_ref[0 : 2 * n, :].reshape(grid_y, 1, 2 * grid_z, 128)
        return jnp.broadcast_to(wide, (grid_y, 2, 2 * grid_z, 128)).reshape(4 * n, 128)

    def wide_field(cat, plane, first, grid_y, grid_z, turned=False):
        order = (2, 1, 0) if turned else (0, 1, 2)
        pieces = [
            cat[k, plane, first : first + grid_y].reshape(grid_y * grid_z, 128) for k in order
        ]
        return jnp.concatenate(pieces, axis=1)

    row = lax.broadcasted_iota(jnp.int32, (128, 128), 0)
    col = lax.broadcasted_iota(jnp.int32, (128, 128), 1)
    unit = (row == col).astype(f32).astype(bf16)

    def clear(i, carry):
        for k in range(3):
            for p in range(4):
                b.hs[i, k, p, 0] = jnp.zeros((32, 128), bf16)
                b.hs[i, k, p, 9] = jnp.zeros((32, 128), bf16)
            for p in range(3):
                b.hsb[i, k, p, 0] = jnp.zeros((16, 128), bf16)
                b.hsb[i, k, p, 5] = jnp.zeros((16, 128), bf16)
        return carry

    clear(q, 0)
    for ref in (b.ge, b.mp):
        ref[0] = jnp.zeros((16, 128), bf16)
        ref[17] = jnp.zeros((16, 128), bf16)

    hs_own = b.hs.at[q]
    hsb_own = b.hsb.at[q]

    def put_a(plane, h):
        put(hs_own, plane, h, 8, 32)
        b.hraw[q, plane] = h.astype(bf16).reshape(8, 32, 128)

    loads.fv.wait()
    for p in range(2):
        put_a(1 + p, silu(b.fv[p].astype(f32).reshape(256, 128)))

    def taps_a(acc, p, dx):
        for dy in range(3):
            acc = acc + mm(wide_field(hs_own, p + dx, dy, 8, 32), b.wa[3 * dx + dy])
        return acc

    loads.wa.wait()
    acc_a = [jnp.zeros((256, 128), f32), jnp.zeros((256, 128), f32)]
    acc_a[0] = taps_a(taps_a(acc_a[0], 0, 1), 0, 2)
    acc_a[1] = taps_a(taps_a(acc_a[1], 1, 1), 1, 0)
    for p in range(2):
        b.la[p] = acc_a[p]

    loads.cv.wait()
    loads.w1.wait()
    loads.kv.wait()
    flags = b.kv[...].astype(f32)
    flag = [flags[0:1, j : j + 1] for j in range(3)]
    scale = [flag[j] * f32(1.0 / SURVIVAL[j]) for j in range(3)]
    up32 = [b.cv[p].astype(f32).reshape(256, 128) for p in range(2)]
    grad_e1 = pool_yz(up32[0] + up32[1], 8, 32, b.pool_s).astype(bf16)
    grad_d = mm(grad_e1, b.w1[...], NT).astype(bf16)
    b.gd_own[...] = grad_d
    b.bz_buf[z] = pool_yz(grad_d.astype(f32), 4, 16, b.small_s).astype(bf16)
    bz_copies = [
        send(S.bz, k - 1, b.bz_buf.at[z], b.bz_buf.at[z], dev(dz=z_of[k]))
        for k in range(1, NZL)
    ]
    halo_d_copies = [
        send(S.halo_d, 0, b.gd_own, b.halo_d.at[0], nxt),
        send(S.halo_d, 1, b.gd_own, b.halo_d.at[1], prv),
    ]
    for p in range(2):
        turned = mm(unit, (up32[p] * flag[0]).astype(bf16), NT).astype(bf16)
        b.cq[q, :, 256 * p : 256 * p + 256] = turned
    peers = [sibling] + [dev(dy=y_of[k]) for k in range(1, NY)]

    def whole(ref, slot, to_y):
        return ref.at[slot]

    def some(count):
        return lambda ref, slot, to_y: ref.at[slot, pl.ds(to_y // 2, count)]

    def spread(name, ref, part=whole):
        result = []
        for k in range(4):
            piece = part(ref, q, y_of[k])
            result.append(send(name, k, piece, piece, peers[k]))
        return result

    def forward(name, ref, copies, part=whole):
        result = []
        for k in range(1, NY):
            piece = part(ref, y_from[k] * 2 + core, y)
            pltpu.make_async_remote_copy(
                src_ref=piece,
                dst_ref=piece,
                send_sem=send_sem.at[0],
                recv_sem=recv_sem.at[copies[k]],
                device_id=sibling,
                device_id_type=MESH,
            ).wait_recv()
            result.append(send(name, k - 1, piece, piece, sibling))
        return result

    def to_group(name, ref, part=whole):
        result = []
        for k in range(1, 8):
            piece = part(ref, q, group_of[k][0])
            result.append(send(name, k - 1, piece, piece, group_dev[k]))
        return result

    cot_copies = spread(S.cot, b.cq)
    cot_sems = [S.cot + k for k in range(4)]
    hid_sems = [S.hid + k for k in range(4)]

    arrived(halo_a_copies)
    put_a(0, silu(b.halo_a[0].astype(f32).reshape(256, 128)) * has_prev)
    put_a(3, silu(b.halo_a[1].astype(f32).reshape(256, 128)) * has_next)
    hid_copies = spread(S.hid, b.hraw, some(3))
    acc_a[0] = taps_a(b.la[0], 0, 0)
    acc_a[1] = taps_a(b.la[1], 1, 2)
    level_a = []
    for p in range(2):
        value = b.fv[p].astype(f32).reshape(256, 128) + scale[0] * acc_a[p]
        b.la[p] = value
        level_a.append(value)
    pooled = (pool_yz(level_a[0] + level_a[1], 8, 32, b.pool_s) * 0.125).astype(bf16)
    loads.l1.wait()
    lb = mm(pooled, b.l1[...]).astype(bf16).astype(f32)

    hidden_b = silu(lb)
    b.hb_own[...] = hidden_b.astype(bf16)
    halo_b_copies = [
        send(S.halo_b, 0, b.hb_own, b.halo_b.at[0], nxt),
        send(S.halo_b, 1, b.hb_own, b.halo_b.at[1], prv),
    ]

    def put_b(plane, h):
        put(hsb_own, plane, h, 4, 16)
        b.hbraw[q, plane] = h.astype(bf16)

    put_b(1, hidden_b)

    arrived(bz_copies)
    for k in range(4):
        both = b.bz_buf[2 * k].astype(f32) + b.bz_buf[2 * k + 1].astype(f32)
        b.ge[1 + 4 * x + k] = both.astype(bf16)
    own_ge = b.ge.at[pl.ds(1 + 4 * x, 4)]
    bx_copies = [send(S.bx, k - 1, own_ge, own_ge, dev(dx=x_of[k])) for k in range(1, NXC)]

    def taps_b(acc, dx):
        for dy in range(3):
            acc = acc + mm(wide_field(hsb_own, dx, dy, 4, 16), b.wb[3 * dx + dy])
        return acc

    loads.wb.wait()
    acc_b = taps_b(jnp.zeros((64, 128), f32), 1)
    arrived(halo_b_copies)
    put_b(0, b.halo_b[0].astype(f32) * has_prev)
    put_b(2, b.halo_b[1].astype(f32) * has_next)
    acc_b = taps_b(taps_b(acc_b, 0), 2)
    level_b = lb + scale[1] * acc_b
    b.fz_buf[z] = (pool_yz(level_b, 4, 16, b.small_s) * 0.25).astype(bf16)
    fz_copies = [
        send(S.fz, k - 1, b.fz_buf.at[z], b.fz_buf.at[z], dev(dz=z_of[k]))
        for k in range(1, NZL)
    ]

    for k in range(3):
        for p in range(3):
            b.gbs[k, p, 0] = jnp.zeros((16, 128), bf16)
            b.gbs[k, p, 5] = jnp.zeros((16, 128), bf16)
    lax.fori_loop(1, 8, lambda k, carry: clear(lax.rem(q + k, 8), carry), 0)
    for load in (loads.w2, loads.wc, loads.l2):
        load.wait()
    arrived(bx_copies)
    grad_e2 = b.ge[1:17].reshape(256, 128)
    own_rows = b.w2[pl.ds(pl.multiple_of(g * 16, 16), 16), :]
    grad_t = mm(own_rows, grad_e2, NT).astype(bf16).astype(f32)
    lane = lax.broadcasted_iota(jnp.int32, (16, 256), 1)
    pos_p, pos_y, pos_z = lane // 16, (lane // 8) % 2, lane % 8

    def moved(v, pos, length, step, d):
        if d == 0:
            return v
        ok = (pos + d >= 0) & (pos + d < length)
        return jnp.where(ok, pltpu.roll(v, (-d * step) % 256, 1), 0.0)

    for dx in range(3):
        vx = moved(grad_t, pos_p, 16, 16, 1 - dx)
        for dy in range(3):
            vy = moved(vx, pos_y, 2, 8, 1 - dy)
            for dz in range(3):
                tap = 9 * dx + 3 * dy + dz
                b.st[16 * tap : 16 * tap + 16, :] = moved(vy, pos_z, 8, 1, 1 - dz).astype(bf16)
    b.st[432:448, :] = jnp.zeros((16, 256), bf16)
    back_part = mm(b.st[0:432, :], b.wc[...], TN)
    start = z // 2 + z % 2
    two_e2 = b.ge[pl.ds(4 * x + start, 2)].reshape(32, 128)
    two_c = mm(two_e2, b.w2[...], NT).astype(bf16)
    two_m2 = mm(two_c, b.l2[...], NT)

    arrived(fz_copies)
    for k in range(4):
        both = b.fz_buf[2 * k].astype(f32) + b.fz_buf[2 * k + 1].astype(f32)
        b.fx_buf[x, k] = (both * 0.5).astype(bf16)
    fx_copies = [
        send(S.fx, k - 1, b.fx_buf.at[x], b.fx_buf.at[x], dev(dx=x_of[k]))
        for k in range(1, NXC)
    ]
    hb_copies = to_group(S.hb, b.hbraw, some(2))
    cot_forward = forward(S.cot_f, b.cq, cot_sems)
    arrived(fx_copies)
    pooled_two = b.fx_buf[...].reshape(256, 128)
    lc_b = mm(pooled_two, b.l2[...]).astype(bf16)
    lc = lc_b.astype(f32)
    sig = jax.nn.sigmoid(lc)
    hidden_c = (lc * sig).astype(bf16)
    weighted = (scale[2] * (sig * (1.0 + lc * (1.0 - sig))) * back_part).astype(bf16)
    b.mp[1:17] = mm(weighted, b.l2[...], NT).astype(bf16).reshape(16, 16, 128)
    rxb_copies = [
        send(S.rxb, k - 1, b.mp.at[pl.ds(4 * x_of[k], 6)], b.rxb.at[k - 1], dev(dx=x_of[k]))
        for k in range(1, NXC)
    ]
    taps = mm(b.wc[...], hidden_c, NT).reshape(9, 3, 16, 256)

    def folded(v, pos, length, step):
        total = v[:, 1]
        for d in (-1, 1):
            ok = (pos + d >= 0) & (pos + d < length)
            piece = v[:, 1 + d]
            turned = pltpu.roll(piece.reshape(-1, 256), (-d * step) % 256, 1)
            total = total + jnp.where(ok[None], turned.reshape(piece.shape), 0.0)
        return total

    conv_t = folded(taps, pos_z, 8, 1).reshape(3, 3, 16, 256)
    conv_t = folded(conv_t, pos_y, 2, 8).reshape(1, 3, 16, 256)
    conv_t = folded(conv_t, pos_p, 16, 16).reshape(16, 256)
    row16 = lax.broadcasted_iota(jnp.int32, (16, 512), 0)
    lane16 = lax.broadcasted_iota(jnp.int32, (16, 512), 1)
    pick = (lane16 == row16 + g * 16).astype(f32).astype(bf16)
    own_lc = mm(pick, lc_b, NT)
    level_c = (own_lc + scale[2] * conv_t).astype(bf16)
    b.up[...] = mm(level_c, own_rows, TN).astype(bf16).reshape(16, 16, 128)
    rxf_copies = [
        send(S.rxf, k - 1, b.up.at[pl.ds(4 * x_of[k], 4)], b.rxf.at[k - 1], dev(dx=x_of[k]))
        for k in range(1, NXC)
    ]

    arrived(rxb_copies)
    both = b.mp[pl.ds(4 * x, 6)].astype(f32)
    for k in range(3):
        both = both + b.rxb[k].astype(f32)
    b.sb[...] = both.astype(bf16)
    rzb_copies = []
    for k in range(1, NZL):
        first = z_of[k] // 2 + z_of[k] % 2
        rzb_copies.append(
            send(S.rzb, k - 1, b.sb.at[pl.ds(first, 2)], b.rzb.at[k - 1], dev(dz=z_of[k]))
        )
    arrived(rxf_copies)
    both = b.up[pl.ds(4 * x, 4)].astype(f32)
    for k in range(3):
        both = both + b.rxf[k].astype(f32)
    b.sf[...] = both.astype(bf16)
    rzf_copies = [
        send(S.rzf, k - 1, b.sf.at[z_of[k] // 2], b.rzf.at[k - 1], dev(dz=z_of[k]))
        for k in range(1, NZL)
    ]

    grad_w = (scale[2] * mm(b.st[...], hidden_c)).astype(bf16)
    for cc in range(2):
        for yy in range(NY):
            b.dc[cc, yy] = grad_w[224 * cc : 224 * cc + 224, 128 * yy : 128 * yy + 128]
    hid_forward = forward(S.hid_f, b.hraw, hid_sems, some(3))
    c_core = send(S.c_core, 0, b.dc.at[1 - core], b.c_cr, sibling)

    def prepare(slot):
        def one(p, carry):
            put(b.hs.at[slot], p, b.hraw[slot, p].astype(f32).reshape(256, 128), 8, 32)
            return carry

        lax.fori_loop(y // 2, y // 2 + 3, one, 0)

    hid_copies[0].wait_recv()
    prepare(y * 2 + 1 - core)
    for k in range(1, NY):
        prepare(y_of[k] * 2 + core)

    c_core.wait_recv()
    for yy in range(NY):
        b.c_ys[yy] = (b.dc[core, yy].astype(f32) + b.c_cr[yy].astype(f32)).astype(bf16)
    c_y = [
        send(S.c_y, k - 1, b.c_ys.at[y_of[k]], b.c_yr.at[k - 1], dev(dy=y_of[k]))
        for k in range(1, NY)
    ]

    arrived(rzb_copies)
    both = b.sb[pl.ds(start, 2)].astype(f32)
    for k in range(7):
        both = both + b.rzb[k].astype(f32)
    two_m2 = (two_m2.reshape(2, 16, 128) + both).astype(bf16).astype(f32)
    even = (z % 2 == 0).astype(f32)
    lo, hi = two_m2[0], two_m2[1]
    own_m2 = hi * even + lo * (1.0 - even)
    arrived(halo_d_copies)

    def grad_plane(field, m2):
        return (field.astype(f32) + grow_yz(m2, 2, 8, b.small_s) * 0.125).astype(bf16)

    grad_b = grad_plane(b.gd_own[...], own_m2)
    grad_b32 = grad_b.astype(f32)
    b.gbq[q] = (grad_b32 * flag[1]).astype(bf16)
    gb_copies = to_group(S.gb, b.gbq)
    put(b.gbs, 1, grad_b32, 4, 16)
    put(b.gbs, 0, grad_plane(b.halo_d[0], lo).astype(f32) * has_prev, 4, 16)
    put(b.gbs, 2, grad_plane(b.halo_d[1], hi).astype(f32) * has_next, 4, 16)
    back_b = jnp.zeros((64, 128), f32)
    for t in range(9):
        dx, dy = t // 3, t % 3
        for dz in range(3):
            part = b.gbs[2 - dz, 2 - dx, 2 - dy : 6 - dy].reshape(64, 128)
            back_b = back_b + mm(part, b.wb[t, 128 * dz : 128 * dz + 128, :], NT)
    grad_p = (grad_b32 + scale[1] * slope(lb) * back_b).astype(bf16)
    grad_m1 = mm(grad_p, b.l1[...], NT).astype(bf16).astype(f32)
    b.m1q[q] = (grad_m1 * flag[0]).astype(bf16)
    m1_copies = to_group(S.m1, b.m1q)
    early = len(started)

    arrived(c_y)
    total = b.c_ys[y].astype(f32)
    for k in range(3):
        total = total + b.c_yr[k].astype(f32)
    b.c_zs[...] = total.astype(bf16)
    c_zh = send(S.c_zh, 0, b.c_zs, b.c_zr, dev(dzh=1 - zh))
    arrived(hb_copies)
    for k in range(1, 8):
        slot = group_of[k][0] * 2 + group_of[k][1]
        for p in range(2):
            plane = y // 2 + p
            put(b.hsb.at[slot], plane, b.hbraw[slot, plane].astype(f32), 4, 16)
    arrived(gb_copies)
    numbers = [jnp.minimum(4 * q + i, 26) for i in range(4)]
    where = [(t // 9, (t // 3) % 3, t % 3) for t in numbers]

    def keep_sum(kind, i, value):
        for k in range(NXC):
            b.xs[kind, k, i] = value[32 * k : 32 * k + 32].astype(bf16)

    def along_x(kind):
        return [
            send(
                KINDS[kind][0],
                k - 1,
                b.xs.at[kind, x_of[k]],
                b.xr.at[kind, k - 1],
                dev(dx=x_of[k]),
            )
            for k in range(1, NXC)
        ]

    source = ((row // 4) % 4) * 32 + (row // 16) * 4 + row % 4
    shuffle = (col == source).astype(f32).astype(bf16)

    def along_z(kind):
        total = b.xs[kind, x].astype(f32)
        for k in range(3):
            total = total + b.xr[kind, k].astype(f32)
        pieces = mm(shuffle, total.astype(bf16).reshape(128, 128)).astype(bf16)
        b.zs[kind] = pieces.reshape(8, 16, 128)
        copies = []
        for k in sorted(range(1, NZ), key=lambda k: abs(k - NZ // 2)):
            target = dev(dzh=z16_of[k] // NZL, dz=z16_of[k] % NZL)
            src = b.zs.at[kind, z16_of[k] % NZL]
            copies.append(send(KINDS[kind][1], k - 1, src, b.zr.at[kind, z16], target))
        b.zr[kind, z16] = b.zs[kind, z]
        return copies

    def to_all(kind):
        total = b.zr[kind, 0].astype(f32)
        for k in range(1, NZ):
            total = total + b.zr[kind, k].astype(f32)
        b.zt[kind] = total
        own = (fga, fgb)[kind].at[q]
        copies = [
            send(KINDS[kind][2], k - 1, b.zt.at[kind], own, group_dev[k]) for k in range(1, 8)
        ]
        stores.append(pltpu.make_async_copy(b.zt.at[kind], own, local_sem.at[11 + kind]))
        stores[-1].start()
        return copies

    turned_b = mm(unit, b.gbq[...].reshape(512, 128), NT).astype(bf16)
    for i, (dx, dy, dz) in enumerate(where):
        field = b.hsb[:, dz, dx, pl.ds(dy, 4)].reshape(512, 128)
        keep_sum(1, i, mm(turned_b, field) * f32(1.0 / SURVIVAL[1]))
    b_x = along_x(1)
    arrived(rzf_copies)
    both = b.sf[z // 2].astype(f32)
    for k in range(7):
        both = both + b.rzf[k].astype(f32)
    level_d = (level_b + grow_yz(both, 2, 8, b.small_s)).astype(bf16)
    wide = grow_yz(mm(level_d, b.w1[...]), 4, 16, b.grow_s)
    for p in range(2):
        b.rv[p] = (b.la[p] + wide).astype(bf16).reshape(8, 32, 128)
    stores = [pltpu.make_async_copy(b.rv, res.at[0], local_sem.at[10])]
    stores[0].start()
    for k in range(1, NY):
        hid_forward[k - 1].wait_recv()
        prepare(y_from[k] * 2 + 1 - core)
    arrived(b_x)
    b_z = along_z(1)
    cot_copies[0].wait_recv()
    arrived(cot_forward)

    coarse = lax.broadcasted_iota(jnp.int32, (64, 512), 0)
    fine = lax.broadcasted_iota(jnp.int32, (64, 512), 1)
    above = ((fine // 64) % 4) * 16 + (fine % 32) // 2
    grow = jnp.where(coarse == above, 0.125, 0.0).astype(bf16)
    arrived(m1_copies)
    for j in range(8):
        b.gt[j] = (b.cq[j].astype(f32) + mm(b.m1q[j], grow, TN)).astype(bf16)
    for pair in range(2):
        acc = jnp.zeros((128, 256), f32)
        for j in range(8):
            pieces = []
            for i in (2 * pair, 2 * pair + 1):
                dx, dy, dz = where[i]
                pieces.append(b.hs[j, dz, pl.ds(dx, 2), pl.ds(dy, 8)].reshape(512, 128))
            acc = acc + mm(b.gt[j], jnp.concatenate(pieces, axis=1))
        acc = acc * f32(1.0 / SURVIVAL[0])
        keep_sum(0, 2 * pair, acc[:, 0:128])
        keep_sum(0, 2 * pair + 1, acc[:, 128:256])
    a_x = along_x(0)

    arrived(b_z)
    b_all = to_all(1)
    arrived(a_x)
    a_z = along_z(0)
    finish(early)
    c_zh.wait_recv()
    b.c_own[...] = (b.c_zs[...].astype(f32) + b.c_zr[...].astype(f32)).astype(bf16)
    rows_c = pl.ds(pl.multiple_of(core * 224, 16), 224)
    lanes_y = pl.ds(pl.multiple_of(y * 128, 128), 128)
    own_c = fgc.at[rows_c, lanes_y]
    c_ay = [send(S.c_ay, k - 1, b.c_own, own_c, dev(dy=y_of[k])) for k in range(1, NY)]
    stores.append(pltpu.make_async_copy(b.c_own, own_c, local_sem.at[13]))
    stores[-1].start()
    arrived(a_z)
    a_all = to_all(0)
    arrived(c_ay)
    for copy in stores:
        copy.wait()
    half_c = fgc.at[rows_c]
    c_ac = send(S.c_ac, 0, half_c, half_c, sibling)
    finish(len(started) - 8)
    arrived(b_all)
    arrived(a_all)
    c_ac.wait_recv()
    finish(len(started))


def finalize(
    res, fga, fgb, fgc, out, out_a, out_b, out_c, res_v, fg_v, fgc_v, tables, wide, sems
):
    loads = [
        pltpu.make_async_copy(fgc, fgc_v, sems.at[0]),
        pltpu.make_async_copy(fga, fg_v.at[0], sems.at[1]),
        pltpu.make_async_copy(fgb, fg_v.at[1], sems.at[2]),
        pltpu.make_async_copy(res, res_v, sems.at[9]),
    ]
    copies = [pltpu.make_async_copy(res_v, out, sems.at[3])]
    for load in loads:
        load.start()
    loads[3].wait()
    copies[0].start()
    for kind, target in enumerate((out_a, out_b)):
        loads[1 + kind].wait()
        for t in range(27):
            first = 4 * (t % 4)
            tables[kind, t] = fg_v[kind, t // 4, first : first + 4]
        copies.append(pltpu.make_async_copy(tables.at[kind], target, sems.at[4 + kind]))
        copies[-1].start()
    loads[0].wait()
    for part in range(3):
        rows = pl.ds(144 * part, 144)
        wide[rows] = fgc_v[rows].astype(f32)
        copies.append(pltpu.make_async_copy(wide.at[rows], out_c.at[rows], sems.at[6 + part]))
        copies[-1].start()
    for copy in copies:
        copy.wait()


def body(
    features,
    cotangent,
    keep_flags,
    conv_a,
    conv_b,
    conv_c,
    lift_one,
    lift_two,
    lower_two,
    lower_one,
):
    hbm = pl.BlockSpec(memory_space=pltpu.HBM)
    result, fga, fgb, fgc = pl.pallas_call(
        kernel,
        out_shape=(
            jax.ShapeDtypeStruct(features.shape, bf16),
            jax.ShapeDtypeStruct((8, 16, 128), f32),
            jax.ShapeDtypeStruct((8, 16, 128), f32),
            jax.ShapeDtypeStruct((448, 512), bf16),
        ),
        in_specs=[hbm] * 10,
        out_specs=(hbm,) * 4,
        scratch_shapes=[pltpu.VMEM(shape, dtype) for shape, dtype in SCRATCH.values()]
        + [
            pltpu.SemaphoreType.DMA((14,)),
            pltpu.SemaphoreType.DMA((TOTAL,)),
            pltpu.SemaphoreType.DMA((TOTAL,)),
        ],
        compiler_params=pltpu.CompilerParams(
            collective_id=0, has_side_effects=True, vmem_limit_bytes=60 * 1024 * 1024
        ),
        cost_estimate=pl.CostEstimate(
            flops=1_400_000_000, bytes_accessed=5_000_000, transcendentals=600_000
        ),
    )(
        features,
        cotangent,
        keep_flags,
        conv_a.reshape(9, 384, 128),
        conv_b.reshape(9, 384, 128),
        conv_c.transpose(0, 2, 1).reshape(432, 512),
        lift_one,
        lift_two,
        lower_two,
        lower_one,
    )

    result, grad_a, grad_b, grad_c = pl.pallas_call(
        finalize,
        out_shape=(
            jax.ShapeDtypeStruct(features.shape, bf16),
            jax.ShapeDtypeStruct((27, 4, 128), f32),
            jax.ShapeDtypeStruct((27, 4, 128), f32),
            jax.ShapeDtypeStruct((432, 512), f32),
        ),
        in_specs=[hbm] * 4,
        out_specs=(hbm,) * 4,
        scratch_shapes=[
            pltpu.VMEM(features.shape, bf16),
            pltpu.VMEM((2, 8, 16, 128), f32),
            pltpu.VMEM((448, 512), bf16),
            pltpu.VMEM((2, 27, 4, 128), f32),
            pltpu.VMEM((432, 512), f32),
            pltpu.SemaphoreType.DMA((10,)),
        ],
        compiler_params=pltpu.CompilerParams(vmem_limit_bytes=60 * 1024 * 1024),
    )(result, fga, fgb, fgc)
    return (
        result,
        grad_a.transpose(0, 2, 1),
        grad_b.transpose(0, 2, 1),
        grad_c.reshape(27, 16, 512).transpose(0, 2, 1),
    )


def solution(mesh):
    return jax.shard_map(
        body,
        mesh=mesh,
        in_specs=(
            P("member", "gx", None, None, None),
            P("member", "gx", None, None, None),
            P("member", None),
            P(),
            P(),
            P(None, None, "gx"),
            P(),
            P(),
            P(),
            P(),
        ),
        out_specs=(
            P("member", "gx", None, None, None),
            P(None, None, "gx"),
            P(None, None, "gx"),
            P(None, None, "gx"),
        ),
        check_vma=False,
    )
```

```python
import jax
import jax.numpy as jnp
from jax import lax
from jax.experimental import pallas as pl
from jax.experimental.pallas import tpu as pltpu
from jax.sharding import PartitionSpec as P

f32 = jnp.float32
bf16 = jnp.bfloat16
MESH = pl.DeviceIdType.MESH

NY, NZH, NCORE, NXC, NZL = 4, 2, 2, 4, 8
NZ = NZH * NZL
SURVIVAL = (0.9, 0.8, 0.7)

COPIES = dict(
    halo_a=2,
    halo_b=2,
    halo_d=2,
    bz=7,
    bx=3,
    fz=7,
    fx=3,
    cot=4,
    cot_f=3,
    hid=4,
    hid_f=3,
    hb=7,
    gb=7,
    m1=7,
    rxb=3,
    rxf=3,
    rzb=7,
    rzf=7,
    a_x=3,
    a_z=15,
    a_all=7,
    b_x=3,
    b_z=15,
    b_all=7,
    c_core=1,
    c_y=3,
    c_zh=1,
    c_ay=3,
    c_ac=1,
)


class S:
    pass


TOTAL = 0
for _name, _count in COPIES.items():
    setattr(S, _name, TOTAL)
    TOTAL += _count
KINDS = ((S.a_x, S.a_z, S.a_all), (S.b_x, S.b_z, S.b_all))

NN = (((1,), (0,)), ((), ()))
NT = (((1,), (1,)), ((), ()))
TN = (((0,), (0,)), ((), ()))


def mm(a, b, dims=NN):
    return lax.dot_general(a, b, dims, preferred_element_type=f32)


def silu(v):
    return v * jax.nn.sigmoid(v)


def slope(v):
    s = jax.nn.sigmoid(v)
    return s * (1.0 + v * (1.0 - s))


SCRATCH = dict(
    fv=((2, 8, 32, 128), bf16),
    cv=((2, 8, 32, 128), bf16),
    kv=((1, 3), jnp.int32),
    wa=((9, 384, 128), bf16),
    wb=((9, 384, 128), bf16),
    wc=((432, 512), bf16),
    l1=((128, 128), bf16),
    l2=((128, 512), bf16),
    w2=((512, 128), bf16),
    w1=((128, 128), bf16),
    rv=((2, 8, 32, 128), bf16),
    halo_a=((2, 8, 32, 128), bf16),
    hraw=((8, 4, 8, 32, 128), bf16),
    hs=((8, 3, 4, 10, 32, 128), bf16),
    la=((2, 256, 128), f32),
    pool_s=((128, 128), f32),
    grow_s=((128, 128), f32),
    hb_own=((64, 128), bf16),
    halo_b=((2, 64, 128), bf16),
    hbraw=((8, 3, 64, 128), bf16),
    hsb=((8, 3, 3, 6, 16, 128), bf16),
    small_s=((32, 128), f32),
    gd_own=((64, 128), bf16),
    halo_d=((2, 64, 128), bf16),
    bz_buf=((8, 16, 128), bf16),
    ge=((18, 16, 128), bf16),
    fz_buf=((8, 16, 128), bf16),
    fx_buf=((4, 4, 16, 128), bf16),
    st=((448, 256), bf16),
    mp=((18, 16, 128), bf16),
    up=((16, 16, 128), bf16),
    rxb=((3, 6, 16, 128), bf16),
    rxf=((3, 4, 16, 128), bf16),
    sb=((6, 16, 128), bf16),
    sf=((4, 16, 128), bf16),
    rzb=((7, 2, 16, 128), bf16),
    rzf=((7, 16, 128), bf16),
    gbs=((3, 3, 6, 16, 128), bf16),
    cq=((8, 128, 512), bf16),
    gbq=((8, 64, 128), bf16),
    m1q=((8, 64, 128), bf16),
    gt=((8, 128, 512), bf16),
    xs=((2, 4, 4, 32, 128), bf16),
    xr=((2, 3, 4, 32, 128), bf16),
    zs=((2, 8, 16, 128), bf16),
    zr=((2, 16, 16, 128), bf16),
    zt=((2, 16, 128), f32),
    fc=((4, 224, 128), bf16),
    dc=((2, 4, 224, 128), bf16),
    c_cr=((4, 224, 128), bf16),
    c_ys=((4, 224, 128), bf16),
    c_yr=((3, 224, 128), bf16),
    c_zs=((224, 128), bf16),
    c_zr=((224, 128), bf16),
)


class Bufs:
    pass


def kernel(
    feat_h,
    cot_h,
    keep_h,
    wa_h,
    wb_h,
    wc_h,
    l1_h,
    l2_h,
    w2_h,
    w1_h,
    res,
    fga,
    fgb,
    fgc,
    *scratch,
):
    b = Bufs()
    for name, ref in zip(SCRATCH, scratch):
        setattr(b, name, ref)
    local_sem, send_sem, recv_sem = scratch[len(SCRATCH) :]

    m = lax.axis_index("member")
    g = lax.axis_index("gx")
    x, z = g // NZL, g % NZL
    core, zh, y = m % NCORE, (m // NCORE) % NZH, m // (NCORE * NZH)
    z16 = zh * NZL + z
    q = y * 2 + core

    def dev(dy=None, dzh=None, dcore=None, dx=None, dz=None):
        yy = y if dy is None else dy
        hh = zh if dzh is None else dzh
        cc = core if dcore is None else dcore
        xx = x if dx is None else dx
        zz = z if dz is None else dz
        return ((yy * NZH + hh) * NCORE + cc, xx * NZL + zz)

    nxt = (m, (g + 1) % (NXC * NZL))
    prv = (m, (g + NXC * NZL - 1) % (NXC * NZL))
    x_of = [(x + k) % NXC for k in range(NXC)]
    z_of = [(z + k) % NZL for k in range(NZL)]
    y_of = [(y + k) % NY for k in range(NY)]
    y_from = [(y + NY - k) % NY for k in range(NY)]
    z16_of = [(z16 + k) % NZ for k in range(NZ)]
    group_of = [(y_of[k // 2], (core + k) % 2) for k in range(8)]
    group_dev = [dev(dy=yy, dcore=cc) for yy, cc in group_of]
    sibling = dev(dcore=1 - core)

    barrier = pltpu.get_barrier_semaphore()
    targets = [prv, nxt]
    targets += [dev(dx=x_of[k]) for k in range(1, NXC)]
    targets += [dev(dzh=z16_of[k] // NZL, dz=z16_of[k] % NZL) for k in range(1, NZ)]
    targets += group_dev[1:]
    for target in targets:
        pl.semaphore_signal(barrier, inc=1, device_id=target, device_id_type=MESH)

    started = []

    def finish(count):
        for copy in started[:count]:
            copy.wait_send()
        del started[:count]

    def send(name, k, src, dst, target):
        index = name + k
        copy = pltpu.make_async_remote_copy(
            src_ref=src,
            dst_ref=dst,
            send_sem=send_sem.at[index],
            recv_sem=recv_sem.at[index],
            device_id=target,
            device_id_type=MESH,
        )
        copy.start()
        started.append(copy)
        return copy

    def arrived(copies):
        for copy in copies:
            copy.wait_recv()

    loads = Bufs()

    def load_all(first, **sources):
        for k, (name, src) in enumerate(sources.items()):
            load = pltpu.make_async_copy(src, getattr(b, name), local_sem.at[first + k])
            load.start()
            setattr(loads, name, load)

    load_all(0, fv=feat_h.at[0], wa=wa_h)
    pl.semaphore_wait(barrier, len(targets))
    halo_a_copies = [
        send(S.halo_a, 0, feat_h.at[0, 1], b.halo_a.at[0], nxt),
        send(S.halo_a, 1, feat_h.at[0, 0], b.halo_a.at[1], prv),
    ]
    load_all(2, cv=cot_h.at[0], w1=w1_h, kv=keep_h, l1=l1_h, wb=wb_h, w2=w2_h, wc=wc_h, l2=l2_h)

    has_prev = (g > 0).astype(f32)
    has_next = (g < NXC * NZL - 1).astype(f32)

    def z_shifts(h, length):
        rows = h.shape[0]
        pos = lax.broadcasted_iota(jnp.int32, h.shape, 0) % length
        before = jnp.where(pos == 0, 0.0, pltpu.roll(h, 1, 0))
        after = jnp.where(pos == length - 1, 0.0, pltpu.roll(h, rows - 1, 0))
        return before, h, after

    def put(cat, plane, h, grid_y, grid_z):
        for k, piece in enumerate(z_shifts(h, grid_z)):
            cat[k, plane, 1 : 1 + grid_y] = piece.astype(bf16).reshape(grid_y, grid_z, 128)

    def pool_yz(v, grid_y, grid_z, scratch_ref):
        half = v.reshape(grid_y // 2, 2, grid_z, 128).sum(axis=1)
        n = grid_y // 2 * grid_z
        scratch_ref[0:n, :] = half.reshape(n, 128)
        even = scratch_ref[pl.ds(0, n // 2, stride=2), :]
        return even + scratch_ref[pl.ds(1, n // 2, stride=2), :]

    def grow_yz(v, grid_y, grid_z, scratch_ref):
        n = grid_y * grid_z
        scratch_ref[pl.ds(0, n, stride=2), :] = v
        scratch_ref[pl.ds(1, n, stride=2), :] = v
        wide = scratch_ref[0 : 2 * n, :].reshape(grid_y, 1, 2 * grid_z, 128)
        return jnp.broadcast_to(wide, (grid_y, 2, 2 * grid_z, 128)).reshape(4 * n, 128)

    def wide_field(cat, plane, first, grid_y, grid_z, turned=False):
        order = (2, 1, 0) if turned else (0, 1, 2)
        pieces = [
            cat[k, plane, first : first + grid_y].reshape(grid_y * grid_z, 128) for k in order
        ]
        return jnp.concatenate(pieces, axis=1)

    row = lax.broadcasted_iota(jnp.int32, (128, 128), 0)
    col = lax.broadcasted_iota(jnp.int32, (128, 128), 1)
    unit = (row == col).astype(f32).astype(bf16)

    def clear(i, carry):
        for k in range(3):
            for p in range(4):
                b.hs[i, k, p, 0] = jnp.zeros((32, 128), bf16)
                b.hs[i, k, p, 9] = jnp.zeros((32, 128), bf16)
            for p in range(3):
                b.hsb[i, k, p, 0] = jnp.zeros((16, 128), bf16)
                b.hsb[i, k, p, 5] = jnp.zeros((16, 128), bf16)
        return carry

    clear(q, 0)
    for ref in (b.ge, b.mp):
        ref[0] = jnp.zeros((16, 128), bf16)
        ref[17] = jnp.zeros((16, 128), bf16)

    hs_own = b.hs.at[q]
    hsb_own = b.hsb.at[q]

    def put_a(plane, h):
        put(hs_own, plane, h, 8, 32)
        b.hraw[q, plane] = h.astype(bf16).reshape(8, 32, 128)

    loads.fv.wait()
    for p in range(2):
        put_a(1 + p, silu(b.fv[p].astype(f32).reshape(256, 128)))

    def taps_a(acc, p, dx):
        for dy in range(3):
            acc = acc + mm(wide_field(hs_own, p + dx, dy, 8, 32), b.wa[3 * dx + dy])
        return acc

    loads.wa.wait()
    acc_a = [jnp.zeros((256, 128), f32), jnp.zeros((256, 128), f32)]
    acc_a[0] = taps_a(taps_a(acc_a[0], 0, 1), 0, 2)
    acc_a[1] = taps_a(taps_a(acc_a[1], 1, 1), 1, 0)
    for p in range(2):
        b.la[p] = acc_a[p]

    loads.cv.wait()
    loads.w1.wait()
    loads.kv.wait()
    flags = b.kv[...].astype(f32)
    flag = [flags[0:1, j : j + 1] for j in range(3)]
    scale = [flag[j] * f32(1.0 / SURVIVAL[j]) for j in range(3)]
    up32 = [b.cv[p].astype(f32).reshape(256, 128) for p in range(2)]
    grad_e1 = pool_yz(up32[0] + up32[1], 8, 32, b.pool_s).astype(bf16)
    grad_d = mm(grad_e1, b.w1[...], NT).astype(bf16)
    b.gd_own[...] = grad_d
    b.bz_buf[z] = pool_yz(grad_d.astype(f32), 4, 16, b.small_s).astype(bf16)
    bz_copies = [
        send(S.bz, k - 1, b.bz_buf.at[z], b.bz_buf.at[z], dev(dz=z_of[k]))
        for k in range(1, NZL)
    ]
    halo_d_copies = [
        send(S.halo_d, 0, b.gd_own, b.halo_d.at[0], nxt),
        send(S.halo_d, 1, b.gd_own, b.halo_d.at[1], prv),
    ]
    for p in range(2):
        turned = mm(unit, (up32[p] * flag[0]).astype(bf16), NT).astype(bf16)
        b.cq[q, :, 256 * p : 256 * p + 256] = turned
    peers = [sibling] + [dev(dy=y_of[k]) for k in range(1, NY)]

    def whole(ref, slot, to_y):
        return ref.at[slot]

    def some(count):
        return lambda ref, slot, to_y: ref.at[slot, pl.ds(to_y // 2, count)]

    def spread(name, ref, part=whole):
        result = []
        for k in range(4):
            piece = part(ref, q, y_of[k])
            result.append(send(name, k, piece, piece, peers[k]))
        return result

    def forward(name, ref, copies, part=whole):
        result = []
        for k in range(1, NY):
            piece = part(ref, y_from[k] * 2 + core, y)
            pltpu.make_async_remote_copy(
                src_ref=piece,
                dst_ref=piece,
                send_sem=send_sem.at[0],
                recv_sem=recv_sem.at[copies[k]],
                device_id=sibling,
                device_id_type=MESH,
            ).wait_recv()
            result.append(send(name, k - 1, piece, piece, sibling))
        return result

    def to_group(name, ref, part=whole):
        result = []
        for k in range(1, 8):
            piece = part(ref, q, group_of[k][0])
            result.append(send(name, k - 1, piece, piece, group_dev[k]))
        return result

    cot_copies = spread(S.cot, b.cq)
    cot_sems = [S.cot + k for k in range(4)]
    hid_sems = [S.hid + k for k in range(4)]

    arrived(halo_a_copies)
    put_a(0, silu(b.halo_a[0].astype(f32).reshape(256, 128)) * has_prev)
    put_a(3, silu(b.halo_a[1].astype(f32).reshape(256, 128)) * has_next)
    hid_copies = spread(S.hid, b.hraw, some(3))
    acc_a[0] = taps_a(b.la[0], 0, 0)
    acc_a[1] = taps_a(b.la[1], 1, 2)
    level_a = []
    for p in range(2):
        value = b.fv[p].astype(f32).reshape(256, 128) + scale[0] * acc_a[p]
        b.la[p] = value
        level_a.append(value)
    pooled = (pool_yz(level_a[0] + level_a[1], 8, 32, b.pool_s) * 0.125).astype(bf16)
    loads.l1.wait()
    lb = mm(pooled, b.l1[...]).astype(bf16).astype(f32)

    hidden_b = silu(lb)
    b.hb_own[...] = hidden_b.astype(bf16)
    halo_b_copies = [
        send(S.halo_b, 0, b.hb_own, b.halo_b.at[0], nxt),
        send(S.halo_b, 1, b.hb_own, b.halo_b.at[1], prv),
    ]

    def put_b(plane, h):
        put(hsb_own, plane, h, 4, 16)
        b.hbraw[q, plane] = h.astype(bf16)

    put_b(1, hidden_b)

    arrived(bz_copies)
    for k in range(4):
        both = b.bz_buf[2 * k].astype(f32) + b.bz_buf[2 * k + 1].astype(f32)
        b.ge[1 + 4 * x + k] = both.astype(bf16)
    own_ge = b.ge.at[pl.ds(1 + 4 * x, 4)]
    bx_copies = [send(S.bx, k - 1, own_ge, own_ge, dev(dx=x_of[k])) for k in range(1, NXC)]

    def taps_b(acc, dx):
        for dy in range(3):
            acc = acc + mm(wide_field(hsb_own, dx, dy, 4, 16), b.wb[3 * dx + dy])
        return acc

    lax.fori_loop(1, 8, lambda k, carry: clear(lax.rem(q + k, 8), carry), 0)
    loads.wb.wait()
    acc_b = taps_b(jnp.zeros((64, 128), f32), 1)
    arrived(halo_b_copies)
    put_b(0, b.halo_b[0].astype(f32) * has_prev)
    put_b(2, b.halo_b[1].astype(f32) * has_next)
    acc_b = taps_b(taps_b(acc_b, 0), 2)
    level_b = lb + scale[1] * acc_b
    b.fz_buf[z] = (pool_yz(level_b, 4, 16, b.small_s) * 0.25).astype(bf16)
    fz_copies = [
        send(S.fz, k - 1, b.fz_buf.at[z], b.fz_buf.at[z], dev(dz=z_of[k]))
        for k in range(1, NZL)
    ]

    for k in range(3):
        for p in range(3):
            b.gbs[k, p, 0] = jnp.zeros((16, 128), bf16)
            b.gbs[k, p, 5] = jnp.zeros((16, 128), bf16)
    for load in (loads.w2, loads.wc, loads.l2):
        load.wait()
    arrived(bx_copies)
    grad_e2 = b.ge[1:17].reshape(256, 128)
    own_rows = b.w2[pl.ds(pl.multiple_of(g * 16, 16), 16), :]
    grad_t = mm(own_rows, grad_e2, NT).astype(bf16).astype(f32)
    lane = lax.broadcasted_iota(jnp.int32, (16, 256), 1)
    pos_p, pos_y, pos_z = lane // 16, (lane // 8) % 2, lane % 8

    def moved(v, pos, length, step, d):
        if d == 0:
            return v
        ok = (pos + d >= 0) & (pos + d < length)
        return jnp.where(ok, pltpu.roll(v, (-d * step) % 256, 1), 0.0)

    for dx in range(3):
        vx = moved(grad_t, pos_p, 16, 16, 1 - dx)
        for dy in range(3):
            vy = moved(vx, pos_y, 2, 8, 1 - dy)
            for dz in range(3):
                tap = 9 * dx + 3 * dy + dz
                b.st[16 * tap : 16 * tap + 16, :] = moved(vy, pos_z, 8, 1, 1 - dz).astype(bf16)
    b.st[432:448, :] = jnp.zeros((16, 256), bf16)
    back_part = mm(b.st[0:432, :], b.wc[...], TN)
    start = z // 2 + z % 2
    two_e2 = b.ge[pl.ds(4 * x + start, 2)].reshape(32, 128)
    two_c = mm(two_e2, b.w2[...], NT).astype(bf16)
    two_m2 = mm(two_c, b.l2[...], NT)

    arrived(fz_copies)
    for k in range(4):
        both = b.fz_buf[2 * k].astype(f32) + b.fz_buf[2 * k + 1].astype(f32)
        b.fx_buf[x, k] = (both * 0.5).astype(bf16)
    fx_copies = [
        send(S.fx, k - 1, b.fx_buf.at[x], b.fx_buf.at[x], dev(dx=x_of[k]))
        for k in range(1, NXC)
    ]
    hb_copies = to_group(S.hb, b.hbraw, some(2))
    cot_forward = forward(S.cot_f, b.cq, cot_sems)
    arrived(fx_copies)
    pooled_two = b.fx_buf[...].reshape(256, 128)
    lc_b = mm(pooled_two, b.l2[...]).astype(bf16)
    lc = lc_b.astype(f32)
    sig = jax.nn.sigmoid(lc)
    hidden_c = (lc * sig).astype(bf16)
    weighted = (scale[2] * (sig * (1.0 + lc * (1.0 - sig))) * back_part).astype(bf16)
    b.mp[1:17] = mm(weighted, b.l2[...], NT).astype(bf16).reshape(16, 16, 128)
    rxb_copies = [
        send(S.rxb, k - 1, b.mp.at[pl.ds(4 * x_of[k], 6)], b.rxb.at[k - 1], dev(dx=x_of[k]))
        for k in range(1, NXC)
    ]
    taps = mm(b.wc[...], hidden_c, NT).reshape(9, 3, 16, 256)

    def folded(v, pos, length, step):
        total = v[:, 1]
        for d in (-1, 1):
            ok = (pos + d >= 0) & (pos + d < length)
            piece = v[:, 1 + d]
            turned = pltpu.roll(piece.reshape(-1, 256), (-d * step) % 256, 1)
            total = total + jnp.where(ok[None], turned.reshape(piece.shape), 0.0)
        return total

    conv_t = folded(taps, pos_z, 8, 1).reshape(3, 3, 16, 256)
    conv_t = folded(conv_t, pos_y, 2, 8).reshape(1, 3, 16, 256)
    conv_t = folded(conv_t, pos_p, 16, 16).reshape(16, 256)
    row16 = lax.broadcasted_iota(jnp.int32, (16, 512), 0)
    lane16 = lax.broadcasted_iota(jnp.int32, (16, 512), 1)
    pick = (lane16 == row16 + g * 16).astype(f32).astype(bf16)
    own_lc = mm(pick, lc_b, NT)
    level_c = (own_lc + scale[2] * conv_t).astype(bf16)
    b.up[...] = mm(level_c, own_rows, TN).astype(bf16).reshape(16, 16, 128)
    rxf_copies = [
        send(S.rxf, k - 1, b.up.at[pl.ds(4 * x_of[k], 4)], b.rxf.at[k - 1], dev(dx=x_of[k]))
        for k in range(1, NXC)
    ]

    arrived(rxb_copies)
    both = b.mp[pl.ds(4 * x, 6)].astype(f32)
    for k in range(3):
        both = both + b.rxb[k].astype(f32)
    b.sb[...] = both.astype(bf16)
    rzb_copies = []
    for k in range(1, NZL):
        first = z_of[k] // 2 + z_of[k] % 2
        rzb_copies.append(
            send(S.rzb, k - 1, b.sb.at[pl.ds(first, 2)], b.rzb.at[k - 1], dev(dz=z_of[k]))
        )
    arrived(rxf_copies)
    both = b.up[pl.ds(4 * x, 4)].astype(f32)
    for k in range(3):
        both = both + b.rxf[k].astype(f32)
    b.sf[...] = both.astype(bf16)
    rzf_copies = [
        send(S.rzf, k - 1, b.sf.at[z_of[k] // 2], b.rzf.at[k - 1], dev(dz=z_of[k]))
        for k in range(1, NZL)
    ]

    grad_w = (scale[2] * mm(b.st[...], hidden_c)).astype(bf16)
    for cc in range(2):
        for yy in range(NY):
            b.dc[cc, yy] = grad_w[224 * cc : 224 * cc + 224, 128 * yy : 128 * yy + 128]
    hid_forward = forward(S.hid_f, b.hraw, hid_sems, some(3))
    c_core = send(S.c_core, 0, b.dc.at[1 - core], b.c_cr, sibling)

    def prepare(slot):
        def one(p, carry):
            put(b.hs.at[slot], p, b.hraw[slot, p].astype(f32).reshape(256, 128), 8, 32)
            return carry

        lax.fori_loop(y // 2, y // 2 + 3, one, 0)

    hid_copies[0].wait_recv()
    prepare(y * 2 + 1 - core)
    for k in range(1, NY):
        prepare(y_of[k] * 2 + core)

    c_core.wait_recv()
    for yy in range(NY):
        b.c_ys[yy] = (b.dc[core, yy].astype(f32) + b.c_cr[yy].astype(f32)).astype(bf16)
    c_y = [
        send(S.c_y, k - 1, b.c_ys.at[y_of[k]], b.c_yr.at[k - 1], dev(dy=y_of[k]))
        for k in range(1, NY)
    ]

    arrived(rzb_copies)
    both = b.sb[pl.ds(start, 2)].astype(f32)
    for k in range(7):
        both = both + b.rzb[k].astype(f32)
    two_m2 = (two_m2.reshape(2, 16, 128) + both).astype(bf16).astype(f32)
    even = (z % 2 == 0).astype(f32)
    lo, hi = two_m2[0], two_m2[1]
    own_m2 = hi * even + lo * (1.0 - even)
    arrived(halo_d_copies)

    def grad_plane(field, m2):
        return (field.astype(f32) + grow_yz(m2, 2, 8, b.small_s) * 0.125).astype(bf16)

    grad_b = grad_plane(b.gd_own[...], own_m2)
    grad_b32 = grad_b.astype(f32)
    b.gbq[q] = (grad_b32 * flag[1]).astype(bf16)
    gb_copies = to_group(S.gb, b.gbq)
    put(b.gbs, 1, grad_b32, 4, 16)
    put(b.gbs, 0, grad_plane(b.halo_d[0], lo).astype(f32) * has_prev, 4, 16)
    put(b.gbs, 2, grad_plane(b.halo_d[1], hi).astype(f32) * has_next, 4, 16)
    back_b = jnp.zeros((64, 128), f32)
    for t in range(9):
        dx, dy = t // 3, t % 3
        for dz in range(3):
            part = b.gbs[2 - dz, 2 - dx, 2 - dy : 6 - dy].reshape(64, 128)
            back_b = back_b + mm(part, b.wb[t, 128 * dz : 128 * dz + 128, :], NT)
    grad_p = (grad_b32 + scale[1] * slope(lb) * back_b).astype(bf16)
    grad_m1 = mm(grad_p, b.l1[...], NT).astype(bf16).astype(f32)
    b.m1q[q] = (grad_m1 * flag[0]).astype(bf16)
    m1_copies = to_group(S.m1, b.m1q)
    early = len(started)

    arrived(c_y)
    total = b.c_ys[y].astype(f32)
    for k in range(3):
        total = total + b.c_yr[k].astype(f32)
    b.c_zs[...] = total.astype(bf16)
    c_zh = send(S.c_zh, 0, b.c_zs, b.c_zr, dev(dzh=1 - zh))
    arrived(hb_copies)
    for k in range(1, 8):
        slot = group_of[k][0] * 2 + group_of[k][1]
        for p in range(2):
            plane = y // 2 + p
            put(b.hsb.at[slot], plane, b.hbraw[slot, plane].astype(f32), 4, 16)
    arrived(gb_copies)
    numbers = [jnp.minimum(4 * q + i, 26) for i in range(4)]
    where = [(t // 9, (t // 3) % 3, t % 3) for t in numbers]

    def keep_sum(kind, i, value):
        for k in range(NXC):
            b.xs[kind, k, i] = value[32 * k : 32 * k + 32].astype(bf16)

    stores = []

    def along_x(kind):
        return [
            send(
                KINDS[kind][0],
                k - 1,
                b.xs.at[kind, x_of[k]],
                b.xr.at[kind, k - 1],
                dev(dx=x_of[k]),
            )
            for k in range(1, NXC)
        ]

    source = ((row // 4) % 4) * 32 + (row // 16) * 4 + row % 4
    shuffle = (col == source).astype(f32).astype(bf16)

    def along_z(kind):
        total = b.xs[kind, x].astype(f32)
        for k in range(3):
            total = total + b.xr[kind, k].astype(f32)
        pieces = mm(shuffle, total.astype(bf16).reshape(128, 128)).astype(bf16)
        b.zs[kind] = pieces.reshape(8, 16, 128)
        copies = []
        for k in sorted(range(1, NZ), key=lambda k: abs(k - NZ // 2)):
            target = dev(dzh=z16_of[k] // NZL, dz=z16_of[k] % NZL)
            src = b.zs.at[kind, z16_of[k] % NZL]
            copies.append(send(KINDS[kind][1], k - 1, src, b.zr.at[kind, z16], target))
        b.zr[kind, z16] = b.zs[kind, z]
        return copies

    def to_all(kind):
        total = b.zr[kind, 0].astype(f32)
        for k in range(1, NZ):
            total = total + b.zr[kind, k].astype(f32)
        b.zt[kind] = total
        own = (fga, fgb)[kind].at[q]
        copies = [
            send(KINDS[kind][2], k - 1, b.zt.at[kind], own, group_dev[k]) for k in range(1, 8)
        ]
        stores.append(pltpu.make_async_copy(b.zt.at[kind], own, local_sem.at[11 + kind]))
        stores[-1].start()
        return copies

    turned_b = mm(unit, b.gbq[...].reshape(512, 128), NT).astype(bf16)
    for i, (dx, dy, dz) in enumerate(where):
        field = b.hsb[:, dz, dx, pl.ds(dy, 4)].reshape(512, 128)
        keep_sum(1, i, mm(turned_b, field) * f32(1.0 / SURVIVAL[1]))
    b_x = along_x(1)
    for k in range(1, NY):
        hid_forward[k - 1].wait_recv()
        prepare(y_from[k] * 2 + 1 - core)
    cot_copies[0].wait_recv()
    arrived(cot_forward)

    coarse = lax.broadcasted_iota(jnp.int32, (64, 512), 0)
    fine = lax.broadcasted_iota(jnp.int32, (64, 512), 1)
    above = ((fine // 64) % 4) * 16 + (fine % 32) // 2
    grow = jnp.where(coarse == above, 0.125, 0.0).astype(bf16)
    arrived(m1_copies)
    for j in range(8):
        b.gt[j] = (b.cq[j].astype(f32) + mm(b.m1q[j], grow, TN)).astype(bf16)
    for pair in range(2):
        acc = jnp.zeros((128, 256), f32)
        for j in range(8):
            pieces = []
            for i in (2 * pair, 2 * pair + 1):
                dx, dy, dz = where[i]
                pieces.append(b.hs[j, dz, pl.ds(dx, 2), pl.ds(dy, 8)].reshape(512, 128))
            acc = acc + mm(b.gt[j], jnp.concatenate(pieces, axis=1))
        acc = acc * f32(1.0 / SURVIVAL[0])
        keep_sum(0, 2 * pair, acc[:, 0:128])
        keep_sum(0, 2 * pair + 1, acc[:, 128:256])
    a_x = along_x(0)

    arrived(b_x)
    b_z = along_z(1)
    c_zh.wait_recv()
    b.fc[y] = (b.c_zs[...].astype(f32) + b.c_zr[...].astype(f32)).astype(bf16)
    own_c = b.fc.at[y]
    c_ay = [send(S.c_ay, k - 1, own_c, own_c, dev(dy=y_of[k])) for k in range(1, NY)]

    arrived(a_x)
    a_z = along_z(0)
    arrived(c_ay)
    stores.append(pltpu.make_async_copy(b.fc, fgc.at[core], local_sem.at[13]))
    stores[-1].start()
    c_ac = send(S.c_ac, 0, b.fc, fgc.at[core], sibling)
    arrived(rzf_copies)
    both = b.sf[z // 2].astype(f32)
    for k in range(7):
        both = both + b.rzf[k].astype(f32)
    level_d = (level_b + grow_yz(both, 2, 8, b.small_s)).astype(bf16)
    wide = grow_yz(mm(level_d, b.w1[...]), 4, 16, b.grow_s)
    for p in range(2):
        b.rv[p] = (b.la[p] + wide).astype(bf16).reshape(8, 32, 128)
    stores.append(pltpu.make_async_copy(b.rv, res.at[0], local_sem.at[10]))
    stores[-1].start()
    arrived(b_z)
    b_all = to_all(1)
    finish(early)

    arrived(a_z)
    a_all = to_all(0)
    finish(len(started) - 7)
    arrived(b_all)
    c_ac.wait_recv()
    for copy in stores:
        copy.wait()
    arrived(a_all)
    finish(len(started))


def finalize(
    res, fga, fgb, fgc, out, out_a, out_b, out_c, res_v, fg_v, fgc_v, tables, wide, sems
):
    parts = [
        pltpu.make_async_copy(fgc.at[part], fgc_v.at[part], sems.at[part]) for part in range(2)
    ]
    loads = [
        pltpu.make_async_copy(res, res_v, sems.at[2]),
        pltpu.make_async_copy(fga, fg_v.at[0], sems.at[3]),
        pltpu.make_async_copy(fgb, fg_v.at[1], sems.at[4]),
    ]
    for load in parts + loads:
        load.start()
    copies = []

    def store(src, dst):
        copies.append(pltpu.make_async_copy(src, dst, sems.at[5 + len(copies)]))
        copies[-1].start()

    for part in range(2):
        parts[part].wait()
        rows = pl.ds(224 * part, 224 - 16 * part)
        for yy in range(NY):
            wide[rows, 128 * yy : 128 * yy + 128] = fgc_v[part, yy, 0 : 224 - 16 * part].astype(f32)
        store(wide.at[rows], out_c.at[rows])
        if part == 0:
            loads[0].wait()
            store(res_v, out)
    for kind, target in enumerate((out_a, out_b)):
        loads[1 + kind].wait()
        for t in range(27):
            first = 4 * (t % 4)
            tables[kind, t] = fg_v[kind, t // 4, first : first + 4]
        store(tables.at[kind], target)
    for copy in copies:
        copy.wait()


def body(
    features,
    cotangent,
    keep_flags,
    conv_a,
    conv_b,
    conv_c,
    lift_one,
    lift_two,
    lower_two,
    lower_one,
):
    hbm = pl.BlockSpec(memory_space=pltpu.HBM)
    result, fga, fgb, fgc = pl.pallas_call(
        kernel,
        out_shape=(
            jax.ShapeDtypeStruct(features.shape, bf16),
            jax.ShapeDtypeStruct((8, 16, 128), f32),
            jax.ShapeDtypeStruct((8, 16, 128), f32),
            jax.ShapeDtypeStruct((2, NY, 224, 128), bf16),
        ),
        in_specs=[hbm] * 10,
        out_specs=(hbm,) * 4,
        scratch_shapes=[pltpu.VMEM(shape, dtype) for shape, dtype in SCRATCH.values()]
        + [
            pltpu.SemaphoreType.DMA((14,)),
            pltpu.SemaphoreType.DMA((TOTAL,)),
            pltpu.SemaphoreType.DMA((TOTAL,)),
        ],
        compiler_params=pltpu.CompilerParams(
            collective_id=0, has_side_effects=True, vmem_limit_bytes=60 * 1024 * 1024
        ),
        cost_estimate=pl.CostEstimate(
            flops=1_400_000_000, bytes_accessed=5_000_000, transcendentals=600_000
        ),
    )(
        features,
        cotangent,
        keep_flags,
        conv_a.reshape(9, 384, 128),
        conv_b.reshape(9, 384, 128),
        conv_c.transpose(0, 2, 1).reshape(432, 512),
        lift_one,
        lift_two,
        lower_two,
        lower_one,
    )

    result, grad_a, grad_b, grad_c = pl.pallas_call(
        finalize,
        out_shape=(
            jax.ShapeDtypeStruct(features.shape, bf16),
            jax.ShapeDtypeStruct((27, 4, 128), f32),
            jax.ShapeDtypeStruct((27, 4, 128), f32),
            jax.ShapeDtypeStruct((432, 512), f32),
        ),
        in_specs=[hbm] * 4,
        out_specs=(hbm,) * 4,
        scratch_shapes=[
            pltpu.VMEM(features.shape, bf16),
            pltpu.VMEM((2, 8, 16, 128), f32),
            pltpu.VMEM((2, NY, 224, 128), bf16),
            pltpu.VMEM((2, 27, 4, 128), f32),
            pltpu.VMEM((432, 512), f32),
            pltpu.SemaphoreType.DMA((10,)),
        ],
        compiler_params=pltpu.CompilerParams(vmem_limit_bytes=60 * 1024 * 1024),
    )(result, fga, fgb, fgc)
    return (
        result,
        grad_a.transpose(0, 2, 1),
        grad_b.transpose(0, 2, 1),
        grad_c.reshape(27, 16, 512).transpose(0, 2, 1),
    )


def solution(mesh):
    return jax.shard_map(
        body,
        mesh=mesh,
        in_specs=(
            P("member", "gx", None, None, None),
            P("member", "gx", None, None, None),
            P("member", None),
            P(),
            P(),
            P(None, None, "gx"),
            P(),
            P(),
            P(),
            P(),
        ),
        out_specs=(
            P("member", "gx", None, None, None),
            P(None, None, "gx"),
            P(None, None, "gx"),
            P(None, None, "gx"),
        ),
        check_vma=False,
    )
```

```python
import jax
import jax.numpy as jnp
from jax import lax
from jax.experimental import pallas as pl
from jax.experimental.pallas import tpu as pltpu
from jax.sharding import PartitionSpec as P

f32 = jnp.float32
bf16 = jnp.bfloat16
MESH = pl.DeviceIdType.MESH

NY, NZH, NCORE, NXC, NZL = 4, 2, 2, 4, 8
NZ = NZH * NZL
SURVIVAL = (0.9, 0.8, 0.7)

COPIES = dict(
    halo_a=2,
    halo_b=2,
    halo_d=2,
    bz=7,
    bx=3,
    fz=7,
    fx=3,
    cot=4,
    cot_f=3,
    hid=4,
    hid_f=3,
    hb=7,
    gb=7,
    m1=7,
    rxb=3,
    rxf=3,
    rzb=7,
    rzf=7,
    a_x=3,
    a_z=15,
    a_all=7,
    b_x=3,
    b_z=15,
    b_all=7,
    c_core=1,
    c_y=3,
    c_zh=1,
    c_ay=3,
    c_ac=1,
)


class S:
    pass


TOTAL = 0
for _name, _count in COPIES.items():
    setattr(S, _name, TOTAL)
    TOTAL += _count
KINDS = ((S.a_x, S.a_z, S.a_all), (S.b_x, S.b_z, S.b_all))

NN = (((1,), (0,)), ((), ()))
NT = (((1,), (1,)), ((), ()))
TN = (((0,), (0,)), ((), ()))


def mm(a, b, dims=NN):
    return lax.dot_general(a, b, dims, preferred_element_type=f32)


def silu(v):
    return v * jax.nn.sigmoid(v)


def slope(v):
    s = jax.nn.sigmoid(v)
    return s * (1.0 + v * (1.0 - s))


SCRATCH = dict(
    fv=((2, 8, 32, 128), bf16),
    cv=((2, 8, 32, 128), bf16),
    kv=((1, 3), jnp.int32),
    wa=((9, 384, 128), bf16),
    wb=((9, 384, 128), bf16),
    wc=((432, 512), bf16),
    l1=((128, 128), bf16),
    l2=((128, 512), bf16),
    w2=((512, 128), bf16),
    w1=((128, 128), bf16),
    rv=((2, 8, 32, 128), bf16),
    halo_a=((2, 8, 32, 128), bf16),
    hs=((8, 3, 4, 10, 32, 128), bf16),
    la=((2, 256, 128), f32),
    pool_s=((128, 128), f32),
    grow_s=((128, 128), f32),
    hb_own=((64, 128), bf16),
    halo_b=((2, 64, 128), bf16),
    hsb=((8, 3, 3, 6, 16, 128), bf16),
    small_s=((32, 128), f32),
    gd_own=((64, 128), bf16),
    halo_d=((2, 64, 128), bf16),
    bz_buf=((8, 16, 128), bf16),
    ge=((18, 16, 128), bf16),
    fz_buf=((8, 16, 128), bf16),
    fx_buf=((4, 4, 16, 128), bf16),
    st=((448, 256), bf16),
    mp=((18, 16, 128), bf16),
    up=((16, 16, 128), bf16),
    rxb=((3, 6, 16, 128), bf16),
    rxf=((3, 4, 16, 128), bf16),
    sb=((6, 16, 128), bf16),
    sf=((4, 16, 128), bf16),
    rzb=((7, 2, 16, 128), bf16),
    rzf=((7, 16, 128), bf16),
    gbs=((3, 3, 6, 16, 128), bf16),
    cq=((8, 128, 512), bf16),
    gbq=((8, 64, 128), bf16),
    m1q=((8, 64, 128), bf16),
    gt=((8, 128, 512), bf16),
    xs=((2, 4, 4, 32, 128), bf16),
    xr=((2, 3, 4, 32, 128), bf16),
    zs=((2, 8, 16, 128), bf16),
    zr=((2, 16, 16, 128), bf16),
    zt=((2, 16, 128), f32),
    fc=((4, 224, 128), bf16),
    dc=((2, 4, 224, 128), bf16),
    c_cr=((4, 224, 128), bf16),
    c_ys=((4, 224, 128), bf16),
    c_yr=((3, 224, 128), bf16),
    c_zs=((224, 128), bf16),
    c_zr=((224, 128), bf16),
)


class Bufs:
    pass


def kernel(
    feat_h,
    cot_h,
    keep_h,
    wa_h,
    wb_h,
    wc_h,
    l1_h,
    l2_h,
    w2_h,
    w1_h,
    res,
    fga,
    fgb,
    fgc,
    *scratch,
):
    b = Bufs()
    for name, ref in zip(SCRATCH, scratch):
        setattr(b, name, ref)
    local_sem, send_sem, recv_sem = scratch[len(SCRATCH) :]

    m = lax.axis_index("member")
    g = lax.axis_index("gx")
    x, z = g // NZL, g % NZL
    core, zh, y = m % NCORE, (m // NCORE) % NZH, m // (NCORE * NZH)
    z16 = zh * NZL + z
    q = y * 2 + core

    def dev(dy=None, dzh=None, dcore=None, dx=None, dz=None):
        yy = y if dy is None else dy
        hh = zh if dzh is None else dzh
        cc = core if dcore is None else dcore
        xx = x if dx is None else dx
        zz = z if dz is None else dz
        return ((yy * NZH + hh) * NCORE + cc, xx * NZL + zz)

    nxt = (m, (g + 1) % (NXC * NZL))
    prv = (m, (g + NXC * NZL - 1) % (NXC * NZL))
    x_of = [(x + k) % NXC for k in range(NXC)]
    z_of = [(z + k) % NZL for k in range(NZL)]
    y_of = [(y + k) % NY for k in range(NY)]
    y_from = [(y + NY - k) % NY for k in range(NY)]
    z16_of = [(z16 + k) % NZ for k in range(NZ)]
    group_of = [(y_of[k // 2], (core + k) % 2) for k in range(8)]
    group_dev = [dev(dy=yy, dcore=cc) for yy, cc in group_of]
    sibling = dev(dcore=1 - core)

    barrier = pltpu.get_barrier_semaphore()
    targets = [prv, nxt]
    targets += [dev(dx=x_of[k]) for k in range(1, NXC)]
    targets += [dev(dzh=z16_of[k] // NZL, dz=z16_of[k] % NZL) for k in range(1, NZ)]
    targets += group_dev[1:]
    for target in targets:
        pl.semaphore_signal(barrier, inc=1, device_id=target, device_id_type=MESH)

    started = []

    def finish(count):
        for copy in started[:count]:
            copy.wait_send()
        del started[:count]

    def send(name, k, src, dst, target):
        index = name + k
        copy = pltpu.make_async_remote_copy(
            src_ref=src,
            dst_ref=dst,
            send_sem=send_sem.at[index],
            recv_sem=recv_sem.at[index],
            device_id=target,
            device_id_type=MESH,
        )
        copy.start()
        started.append(copy)
        return copy

    def arrived(copies):
        for copy in copies:
            copy.wait_recv()

    loads = Bufs()

    def load_all(first, **sources):
        for k, (name, src) in enumerate(sources.items()):
            load = pltpu.make_async_copy(src, getattr(b, name), local_sem.at[first + k])
            load.start()
            setattr(loads, name, load)

    load_all(0, fv=feat_h.at[0], wa=wa_h)
    pl.semaphore_wait(barrier, len(targets))
    halo_a_copies = [
        send(S.halo_a, 0, feat_h.at[0, 1], b.halo_a.at[0], nxt),
        send(S.halo_a, 1, feat_h.at[0, 0], b.halo_a.at[1], prv),
    ]
    load_all(2, cv=cot_h.at[0], w1=w1_h, kv=keep_h, l1=l1_h, wb=wb_h, w2=w2_h, wc=wc_h, l2=l2_h)

    has_prev = (g > 0).astype(f32)
    has_next = (g < NXC * NZL - 1).astype(f32)

    def z_shifts(h, length):
        rows = h.shape[0]
        pos = lax.broadcasted_iota(jnp.int32, h.shape, 0) % length
        before = jnp.where(pos == 0, 0.0, pltpu.roll(h, 1, 0))
        after = jnp.where(pos == length - 1, 0.0, pltpu.roll(h, rows - 1, 0))
        return before, h, after

    def put(cat, plane, h, grid_y, grid_z, shifts=(0, 1, 2)):
        pieces = z_shifts(h, grid_z)
        for k in shifts:
            piece = pieces[k].astype(bf16)
            cat[k, plane, 1 : 1 + grid_y] = piece.reshape(grid_y, grid_z, 128)

    def pool_yz(v, grid_y, grid_z, scratch_ref):
        half = v.reshape(grid_y // 2, 2, grid_z, 128).sum(axis=1)
        n = grid_y // 2 * grid_z
        scratch_ref[0:n, :] = half.reshape(n, 128)
        even = scratch_ref[pl.ds(0, n // 2, stride=2), :]
        return even + scratch_ref[pl.ds(1, n // 2, stride=2), :]

    def grow_yz(v, grid_y, grid_z, scratch_ref):
        n = grid_y * grid_z
        scratch_ref[pl.ds(0, n, stride=2), :] = v
        scratch_ref[pl.ds(1, n, stride=2), :] = v
        wide = scratch_ref[0 : 2 * n, :].reshape(grid_y, 1, 2 * grid_z, 128)
        return jnp.broadcast_to(wide, (grid_y, 2, 2 * grid_z, 128)).reshape(4 * n, 128)

    def wide_field(cat, plane, first, grid_y, grid_z, turned=False):
        order = (2, 1, 0) if turned else (0, 1, 2)
        pieces = [
            cat[k, plane, first : first + grid_y].reshape(grid_y * grid_z, 128) for k in order
        ]
        return jnp.concatenate(pieces, axis=1)

    row = lax.broadcasted_iota(jnp.int32, (128, 128), 0)
    col = lax.broadcasted_iota(jnp.int32, (128, 128), 1)
    unit = (row == col).astype(f32).astype(bf16)

    def clear(i, carry):
        for k in range(3):
            for p in range(4):
                b.hs[i, k, p, 0] = jnp.zeros((32, 128), bf16)
                b.hs[i, k, p, 9] = jnp.zeros((32, 128), bf16)
            for p in range(3):
                b.hsb[i, k, p, 0] = jnp.zeros((16, 128), bf16)
                b.hsb[i, k, p, 5] = jnp.zeros((16, 128), bf16)
        return carry

    clear(q, 0)
    for ref in (b.ge, b.mp):
        ref[0] = jnp.zeros((16, 128), bf16)
        ref[17] = jnp.zeros((16, 128), bf16)

    hs_own = b.hs.at[q]
    hsb_own = b.hsb.at[q]

    def put_a(plane, h):
        put(hs_own, plane, h, 8, 32)

    loads.fv.wait()
    for p in range(2):
        put_a(1 + p, silu(b.fv[p].astype(f32).reshape(256, 128)))

    def taps_a(acc, p, dx):
        for dy in range(3):
            acc = acc + mm(wide_field(hs_own, p + dx, dy, 8, 32), b.wa[3 * dx + dy])
        return acc

    loads.wa.wait()
    acc_a = [jnp.zeros((256, 128), f32), jnp.zeros((256, 128), f32)]
    acc_a[0] = taps_a(taps_a(acc_a[0], 0, 1), 0, 2)
    acc_a[1] = taps_a(taps_a(acc_a[1], 1, 1), 1, 0)
    for p in range(2):
        b.la[p] = acc_a[p]

    loads.cv.wait()
    loads.w1.wait()
    loads.kv.wait()
    flags = b.kv[...].astype(f32)
    flag = [flags[0:1, j : j + 1] for j in range(3)]
    scale = [flag[j] * f32(1.0 / SURVIVAL[j]) for j in range(3)]
    up32 = [b.cv[p].astype(f32).reshape(256, 128) for p in range(2)]
    grad_e1 = pool_yz(up32[0] + up32[1], 8, 32, b.pool_s).astype(bf16)
    grad_d = mm(grad_e1, b.w1[...], NT).astype(bf16)
    b.gd_own[...] = grad_d
    b.bz_buf[z] = pool_yz(grad_d.astype(f32), 4, 16, b.small_s).astype(bf16)
    bz_copies = [
        send(S.bz, k - 1, b.bz_buf.at[z], b.bz_buf.at[z], dev(dz=z_of[k]))
        for k in range(1, NZL)
    ]
    halo_d_copies = [
        send(S.halo_d, 0, b.gd_own, b.halo_d.at[0], nxt),
        send(S.halo_d, 1, b.gd_own, b.halo_d.at[1], prv),
    ]
    for p in range(2):
        turned = mm(unit, (up32[p] * flag[0]).astype(bf16), NT).astype(bf16)
        b.cq[q, :, 256 * p : 256 * p + 256] = turned
    peers = [sibling] + [dev(dy=y_of[k]) for k in range(1, NY)]

    def whole(ref, slot, to_y):
        return ref.at[slot]

    def some(count, grid_y):
        return lambda ref, slot, to_y: ref.at[slot, 1, pl.ds(to_y // 2, count), pl.ds(1, grid_y)]

    def spread(name, ref, part=whole):
        result = []
        for k in range(4):
            piece = part(ref, q, y_of[k])
            result.append(send(name, k, piece, piece, peers[k]))
        return result

    def forward(name, ref, copies, part=whole):
        result = []
        for k in range(1, NY):
            piece = part(ref, y_from[k] * 2 + core, y)
            pltpu.make_async_remote_copy(
                src_ref=piece,
                dst_ref=piece,
                send_sem=send_sem.at[0],
                recv_sem=recv_sem.at[copies[k]],
                device_id=sibling,
                device_id_type=MESH,
            ).wait_recv()
            result.append(send(name, k - 1, piece, piece, sibling))
        return result

    def to_group(name, ref, part=whole):
        result = []
        for k in range(1, 8):
            piece = part(ref, q, group_of[k][0])
            result.append(send(name, k - 1, piece, piece, group_dev[k]))
        return result

    cot_copies = spread(S.cot, b.cq)
    cot_sems = [S.cot + k for k in range(4)]
    hid_sems = [S.hid + k for k in range(4)]

    near = (z == 0).astype(jnp.int32)

    def side_in(name, ref, side):
        pltpu.make_async_remote_copy(
            src_ref=ref.at[side],
            dst_ref=ref.at[side],
            send_sem=send_sem.at[name],
            recv_sem=recv_sem.at[name + side],
            device_id=nxt,
            device_id_type=MESH,
        ).wait_recv()
        return jnp.where(side == 0, has_prev, has_next)

    for side in (near, 1 - near):
        inside = side_in(S.halo_a, b.halo_a, side)
        put_a(3 * side, silu(b.halo_a[side].astype(f32).reshape(256, 128)) * inside)
        acc = b.la[side]
        for dy in range(3):
            acc = acc + mm(wide_field(hs_own, 3 * side, dy, 8, 32), b.wa[6 * side + dy])
        b.la[side] = acc
    hid_copies = spread(S.hid, b.hs, some(3, 8))
    level_a = []
    for p in range(2):
        value = b.fv[p].astype(f32).reshape(256, 128) + scale[0] * b.la[p]
        b.la[p] = value
        level_a.append(value)
    pooled = (pool_yz(level_a[0] + level_a[1], 8, 32, b.pool_s) * 0.125).astype(bf16)
    loads.l1.wait()
    lb = mm(pooled, b.l1[...]).astype(bf16).astype(f32)

    hidden_b = silu(lb)
    b.hb_own[...] = hidden_b.astype(bf16)
    halo_b_copies = [
        send(S.halo_b, 0, b.hb_own, b.halo_b.at[0], nxt),
        send(S.halo_b, 1, b.hb_own, b.halo_b.at[1], prv),
    ]

    def put_b(plane, h):
        put(hsb_own, plane, h, 4, 16)

    put_b(1, hidden_b)

    arrived(bz_copies)
    for k in range(4):
        both = b.bz_buf[2 * k].astype(f32) + b.bz_buf[2 * k + 1].astype(f32)
        b.ge[1 + 4 * x + k] = both.astype(bf16)
    own_ge = b.ge.at[pl.ds(1 + 4 * x, 4)]
    bx_copies = [send(S.bx, k - 1, own_ge, own_ge, dev(dx=x_of[k])) for k in range(1, NXC)]

    def taps_b(acc, dx):
        for dy in range(3):
            acc = acc + mm(wide_field(hsb_own, dx, dy, 4, 16), b.wb[3 * dx + dy])
        return acc

    lax.fori_loop(1, 8, lambda k, carry: clear(lax.rem(q + k, 8), carry), 0)
    loads.wb.wait()
    acc_b = taps_b(jnp.zeros((64, 128), f32), 1)
    for side in (near, 1 - near):
        inside = side_in(S.halo_b, b.halo_b, side)
        put_b(2 * side, b.halo_b[side].astype(f32) * inside)
        for dy in range(3):
            acc_b = acc_b + mm(wide_field(hsb_own, 2 * side, dy, 4, 16), b.wb[6 * side + dy])
    level_b = lb + scale[1] * acc_b
    b.fz_buf[z] = (pool_yz(level_b, 4, 16, b.small_s) * 0.25).astype(bf16)
    fz_copies = [
        send(S.fz, k - 1, b.fz_buf.at[z], b.fz_buf.at[z], dev(dz=z_of[k]))
        for k in range(1, NZL)
    ]

    for k in range(3):
        for p in range(3):
            b.gbs[k, p, 0] = jnp.zeros((16, 128), bf16)
            b.gbs[k, p, 5] = jnp.zeros((16, 128), bf16)
    for load in (loads.w2, loads.wc, loads.l2):
        load.wait()
    arrived(bx_copies)
    grad_e2 = b.ge[1:17].reshape(256, 128)
    own_rows = b.w2[pl.ds(pl.multiple_of(g * 16, 16), 16), :]
    grad_t = mm(own_rows, grad_e2, NT).astype(bf16).astype(f32)
    lane = lax.broadcasted_iota(jnp.int32, (16, 256), 1)
    pos_p, pos_y, pos_z = lane // 16, (lane // 8) % 2, lane % 8

    def moved(v, pos, length, step, d):
        if d == 0:
            return v
        ok = (pos + d >= 0) & (pos + d < length)
        return jnp.where(ok, pltpu.roll(v, (-d * step) % 256, 1), 0.0)

    for dx in range(3):
        vx = moved(grad_t, pos_p, 16, 16, 1 - dx)
        for dy in range(3):
            vy = moved(vx, pos_y, 2, 8, 1 - dy)
            for dz in range(3):
                tap = 9 * dx + 3 * dy + dz
                b.st[16 * tap : 16 * tap + 16, :] = moved(vy, pos_z, 8, 1, 1 - dz).astype(bf16)
    b.st[432:448, :] = jnp.zeros((16, 256), bf16)
    back_part = mm(b.st[0:432, :], b.wc[...], TN)
    start = z // 2 + z % 2
    two_e2 = b.ge[pl.ds(4 * x + start, 2)].reshape(32, 128)
    two_c = mm(two_e2, b.w2[...], NT).astype(bf16)
    two_m2 = mm(two_c, b.l2[...], NT)

    arrived(fz_copies)
    for k in range(4):
        both = b.fz_buf[2 * k].astype(f32) + b.fz_buf[2 * k + 1].astype(f32)
        b.fx_buf[x, k] = (both * 0.5).astype(bf16)
    fx_copies = [
        send(S.fx, k - 1, b.fx_buf.at[x], b.fx_buf.at[x], dev(dx=x_of[k]))
        for k in range(1, NXC)
    ]
    hb_copies = to_group(S.hb, b.hsb, some(2, 4))
    cot_forward = forward(S.cot_f, b.cq, cot_sems)
    arrived(fx_copies)
    pooled_two = b.fx_buf[...].reshape(256, 128)
    lc_b = mm(pooled_two, b.l2[...]).astype(bf16)
    lc = lc_b.astype(f32)
    sig = jax.nn.sigmoid(lc)
    hidden_c = (lc * sig).astype(bf16)
    weighted = (scale[2] * (sig * (1.0 + lc * (1.0 - sig))) * back_part).astype(bf16)
    b.mp[1:17] = mm(weighted, b.l2[...], NT).astype(bf16).reshape(16, 16, 128)
    rxb_copies = [
        send(S.rxb, k - 1, b.mp.at[pl.ds(4 * x_of[k], 6)], b.rxb.at[k - 1], dev(dx=x_of[k]))
        for k in range(1, NXC)
    ]
    taps = mm(b.wc[...], hidden_c, NT).reshape(9, 3, 16, 256)

    def folded(v, pos, length, step):
        total = v[:, 1]
        for d in (-1, 1):
            ok = (pos + d >= 0) & (pos + d < length)
            piece = v[:, 1 + d]
            turned = pltpu.roll(piece.reshape(-1, 256), (-d * step) % 256, 1)
            total = total + jnp.where(ok[None], turned.reshape(piece.shape), 0.0)
        return total

    conv_t = folded(taps, pos_z, 8, 1).reshape(3, 3, 16, 256)
    conv_t = folded(conv_t, pos_y, 2, 8).reshape(1, 3, 16, 256)
    conv_t = folded(conv_t, pos_p, 16, 16).reshape(16, 256)
    row16 = lax.broadcasted_iota(jnp.int32, (16, 512), 0)
    lane16 = lax.broadcasted_iota(jnp.int32, (16, 512), 1)
    pick = (lane16 == row16 + g * 16).astype(f32).astype(bf16)
    own_lc = mm(pick, lc_b, NT)
    level_c = (own_lc + scale[2] * conv_t).astype(bf16)
    b.up[...] = mm(level_c, own_rows, TN).astype(bf16).reshape(16, 16, 128)
    rxf_copies = [
        send(S.rxf, k - 1, b.up.at[pl.ds(4 * x_of[k], 4)], b.rxf.at[k - 1], dev(dx=x_of[k]))
        for k in range(1, NXC)
    ]

    arrived(rxb_copies)
    both = b.mp[pl.ds(4 * x, 6)].astype(f32)
    for k in range(3):
        both = both + b.rxb[k].astype(f32)
    b.sb[...] = both.astype(bf16)
    rzb_copies = []
    for k in range(1, NZL):
        first = z_of[k] // 2 + z_of[k] % 2
        rzb_copies.append(
            send(S.rzb, k - 1, b.sb.at[pl.ds(first, 2)], b.rzb.at[k - 1], dev(dz=z_of[k]))
        )
    grad_w = (scale[2] * mm(b.st[...], hidden_c)).astype(bf16)
    for cc in range(2):
        for yy in range(NY):
            b.dc[cc, yy] = grad_w[224 * cc : 224 * cc + 224, 128 * yy : 128 * yy + 128]
    hid_forward = forward(S.hid_f, b.hs, hid_sems, some(3, 8))
    c_core = send(S.c_core, 0, b.dc.at[1 - core], b.c_cr, sibling)

    def prepare(slot):
        def one(p, carry):
            field = b.hs[slot, 1, p, 1:9].astype(f32).reshape(256, 128)
            put(b.hs.at[slot], p, field, 8, 32, (0, 2))
            return carry

        lax.fori_loop(y // 2, y // 2 + 3, one, 0)

    hid_copies[0].wait_recv()
    prepare(y * 2 + 1 - core)
    for k in range(1, NY):
        prepare(y_of[k] * 2 + core)

    c_core.wait_recv()
    for yy in range(NY):
        b.c_ys[yy] = (b.dc[core, yy].astype(f32) + b.c_cr[yy].astype(f32)).astype(bf16)
    c_y = [
        send(S.c_y, k - 1, b.c_ys.at[y_of[k]], b.c_yr.at[k - 1], dev(dy=y_of[k]))
        for k in range(1, NY)
    ]

    arrived(rzb_copies)
    both = b.sb[pl.ds(start, 2)].astype(f32)
    for k in range(7):
        both = both + b.rzb[k].astype(f32)
    two_m2 = (two_m2.reshape(2, 16, 128) + both).astype(bf16).astype(f32)
    even = (z % 2 == 0).astype(f32)
    lo, hi = two_m2[0], two_m2[1]
    own_m2 = hi * even + lo * (1.0 - even)
    arrived(halo_d_copies)

    def grad_plane(field, m2):
        return (field.astype(f32) + grow_yz(m2, 2, 8, b.small_s) * 0.125).astype(bf16)

    grad_b = grad_plane(b.gd_own[...], own_m2)
    grad_b32 = grad_b.astype(f32)
    b.gbq[q] = (grad_b32 * flag[1]).astype(bf16)
    gb_copies = to_group(S.gb, b.gbq)
    put(b.gbs, 1, grad_b32, 4, 16)
    put(b.gbs, 0, grad_plane(b.halo_d[0], lo).astype(f32) * has_prev, 4, 16)
    put(b.gbs, 2, grad_plane(b.halo_d[1], hi).astype(f32) * has_next, 4, 16)
    back_b = jnp.zeros((64, 128), f32)
    for t in range(9):
        dx, dy = t // 3, t % 3
        for dz in range(3):
            part = b.gbs[2 - dz, 2 - dx, 2 - dy : 6 - dy].reshape(64, 128)
            back_b = back_b + mm(part, b.wb[t, 128 * dz : 128 * dz + 128, :], NT)
    grad_p = (grad_b32 + scale[1] * slope(lb) * back_b).astype(bf16)
    grad_m1 = mm(grad_p, b.l1[...], NT).astype(bf16).astype(f32)
    b.m1q[q] = (grad_m1 * flag[0]).astype(bf16)
    m1_copies = to_group(S.m1, b.m1q)
    early = len(started)

    arrived(c_y)
    total = b.c_ys[y].astype(f32)
    for k in range(3):
        total = total + b.c_yr[k].astype(f32)
    b.c_zs[...] = total.astype(bf16)
    c_zh = send(S.c_zh, 0, b.c_zs, b.c_zr, dev(dzh=1 - zh))
    arrived(hb_copies)
    for k in range(1, 8):
        slot = group_of[k][0] * 2 + group_of[k][1]
        for p in range(2):
            plane = y // 2 + p
            field = b.hsb[slot, 1, plane, 1:5].astype(f32).reshape(64, 128)
            put(b.hsb.at[slot], plane, field, 4, 16, (0, 2))
    arrived(gb_copies)
    numbers = [jnp.minimum(4 * q + i, 26) for i in range(4)]
    where = [(t // 9, (t // 3) % 3, t % 3) for t in numbers]

    def keep_sum(kind, i, value):
        for k in range(NXC):
            b.xs[kind, k, i] = value[32 * k : 32 * k + 32].astype(bf16)

    stores = []

    def along_x(kind):
        return [
            send(
                KINDS[kind][0],
                k - 1,
                b.xs.at[kind, x_of[k]],
                b.xr.at[kind, k - 1],
                dev(dx=x_of[k]),
            )
            for k in range(1, NXC)
        ]

    source = ((row // 4) % 4) * 32 + (row // 16) * 4 + row % 4
    shuffle = (col == source).astype(f32).astype(bf16)

    def along_z(kind):
        total = b.xs[kind, x].astype(f32)
        for k in range(3):
            total = total + b.xr[kind, k].astype(f32)
        pieces = mm(shuffle, total.astype(bf16).reshape(128, 128)).astype(bf16)
        b.zs[kind] = pieces.reshape(8, 16, 128)
        copies = []
        for k in sorted(range(1, NZ), key=lambda k: abs(k - NZ // 2)):
            target = dev(dzh=z16_of[k] // NZL, dz=z16_of[k] % NZL)
            src = b.zs.at[kind, z16_of[k] % NZL]
            copies.append(send(KINDS[kind][1], k - 1, src, b.zr.at[kind, z16], target))
        b.zr[kind, z16] = b.zs[kind, z]
        return copies

    def to_all(kind):
        total = b.zr[kind, 0].astype(f32)
        for k in range(1, NZ):
            total = total + b.zr[kind, k].astype(f32)
        b.zt[kind] = total
        own = (fga, fgb)[kind].at[q]
        copies = [
            send(KINDS[kind][2], k - 1, b.zt.at[kind], own, group_dev[k]) for k in range(1, 8)
        ]
        stores.append(pltpu.make_async_copy(b.zt.at[kind], own, local_sem.at[11 + kind]))
        stores[-1].start()
        return copies

    turned_b = mm(unit, b.gbq[...].reshape(512, 128), NT).astype(bf16)
    for i, (dx, dy, dz) in enumerate(where):
        field = b.hsb[:, dz, dx, pl.ds(dy, 4)].reshape(512, 128)
        keep_sum(1, i, mm(turned_b, field) * f32(1.0 / SURVIVAL[1]))
    b_x = along_x(1)
    for k in range(1, NY):
        hid_forward[k - 1].wait_recv()
        prepare(y_from[k] * 2 + 1 - core)
    cot_copies[0].wait_recv()
    arrived(cot_forward)

    coarse = lax.broadcasted_iota(jnp.int32, (64, 512), 0)
    fine = lax.broadcasted_iota(jnp.int32, (64, 512), 1)
    above = ((fine // 64) % 4) * 16 + (fine % 32) // 2
    grow = jnp.where(coarse == above, 0.125, 0.0).astype(bf16)
    arrived(m1_copies)
    for j in range(8):
        b.gt[j] = (b.cq[j].astype(f32) + mm(b.m1q[j], grow, TN)).astype(bf16)
    for pair in range(2):
        acc = jnp.zeros((128, 256), f32)
        for j in range(8):
            pieces = []
            for i in (2 * pair, 2 * pair + 1):
                dx, dy, dz = where[i]
                pieces.append(b.hs[j, dz, pl.ds(dx, 2), pl.ds(dy, 8)].reshape(512, 128))
            acc = acc + mm(b.gt[j], jnp.concatenate(pieces, axis=1))
        acc = acc * f32(1.0 / SURVIVAL[0])
        keep_sum(0, 2 * pair, acc[:, 0:128])
        keep_sum(0, 2 * pair + 1, acc[:, 128:256])
    a_x = along_x(0)

    arrived(b_x)
    b_z = along_z(1)
    c_zh.wait_recv()
    b.fc[y] = (b.c_zs[...].astype(f32) + b.c_zr[...].astype(f32)).astype(bf16)
    own_c = b.fc.at[y]
    c_ay = [send(S.c_ay, k - 1, own_c, own_c, dev(dy=y_of[k])) for k in range(1, NY)]

    arrived(a_x)
    a_z = along_z(0)
    arrived(rxf_copies)
    both = b.up[pl.ds(4 * x, 4)].astype(f32)
    for k in range(3):
        both = both + b.rxf[k].astype(f32)
    b.sf[...] = both.astype(bf16)
    rzf_copies = [
        send(S.rzf, k - 1, b.sf.at[z_of[k] // 2], b.rzf.at[k - 1], dev(dz=z_of[k]))
        for k in range(1, NZL)
    ]

    arrived(c_ay)
    stores.append(pltpu.make_async_copy(b.fc, fgc.at[core], local_sem.at[13]))
    stores[-1].start()
    c_ac = send(S.c_ac, 0, b.fc, fgc.at[core], sibling)
    arrived(b_z)
    b_all = to_all(1)
    finish(early)

    arrived(a_z)
    a_all = to_all(0)
    arrived(rzf_copies)
    both = b.sf[z // 2].astype(f32)
    for k in range(7):
        both = both + b.rzf[k].astype(f32)
    level_d = (level_b + grow_yz(both, 2, 8, b.small_s)).astype(bf16)
    wide = grow_yz(mm(level_d, b.w1[...]), 4, 16, b.grow_s)
    for p in range(2):
        b.rv[p] = (b.la[p] + wide).astype(bf16).reshape(8, 32, 128)
    stores.append(pltpu.make_async_copy(b.rv, res.at[0], local_sem.at[10]))
    stores[-1].start()
    arrived(b_all)
    finish(len(started) - 7)
    c_ac.wait_recv()
    for copy in stores:
        copy.wait()
    arrived(a_all)
    finish(len(started))


def finalize(
    res, fga, fgb, fgc, out, out_a, out_b, out_c, res_v, fg_v, fgc_v, tables, wide, sems
):
    parts = [
        pltpu.make_async_copy(fgc.at[part], fgc_v.at[part], sems.at[part]) for part in range(2)
    ]
    loads = [
        pltpu.make_async_copy(res, res_v, sems.at[2]),
        pltpu.make_async_copy(fga, fg_v.at[0], sems.at[3]),
        pltpu.make_async_copy(fgb, fg_v.at[1], sems.at[4]),
    ]
    for load in parts + loads:
        load.start()
    copies = []

    def store(src, dst):
        copies.append(pltpu.make_async_copy(src, dst, sems.at[5 + len(copies)]))
        copies[-1].start()

    for part in range(2):
        parts[part].wait()
        rows = pl.ds(224 * part, 224 - 16 * part)
        for yy in range(NY):
            wide[rows, 128 * yy : 128 * yy + 128] = fgc_v[part, yy, 0 : 224 - 16 * part].astype(f32)
        store(wide.at[rows], out_c.at[rows])
        if part == 0:
            loads[0].wait()
            store(res_v, out)
    for kind, target in enumerate((out_a, out_b)):
        loads[1 + kind].wait()
        for t in range(27):
            first = 4 * (t % 4)
            tables[kind, t] = fg_v[kind, t // 4, first : first + 4]
        store(tables.at[kind], target)
    for copy in copies:
        copy.wait()


def body(
    features,
    cotangent,
    keep_flags,
    conv_a,
    conv_b,
    conv_c,
    lift_one,
    lift_two,
    lower_two,
    lower_one,
):
    hbm = pl.BlockSpec(memory_space=pltpu.HBM)
    result, fga, fgb, fgc = pl.pallas_call(
        kernel,
        out_shape=(
            jax.ShapeDtypeStruct(features.shape, bf16),
            jax.ShapeDtypeStruct((8, 16, 128), f32),
            jax.ShapeDtypeStruct((8, 16, 128), f32),
            jax.ShapeDtypeStruct((2, NY, 224, 128), bf16),
        ),
        in_specs=[hbm] * 10,
        out_specs=(hbm,) * 4,
        scratch_shapes=[pltpu.VMEM(shape, dtype) for shape, dtype in SCRATCH.values()]
        + [
            pltpu.SemaphoreType.DMA((14,)),
            pltpu.SemaphoreType.DMA((TOTAL,)),
            pltpu.SemaphoreType.DMA((TOTAL,)),
        ],
        compiler_params=pltpu.CompilerParams(
            collective_id=0, has_side_effects=True, vmem_limit_bytes=60 * 1024 * 1024
        ),
        cost_estimate=pl.CostEstimate(
            flops=1_400_000_000, bytes_accessed=5_000_000, transcendentals=600_000
        ),
    )(
        features,
        cotangent,
        keep_flags,
        conv_a.reshape(9, 384, 128),
        conv_b.reshape(9, 384, 128),
        conv_c.transpose(0, 2, 1).reshape(432, 512),
        lift_one,
        lift_two,
        lower_two,
        lower_one,
    )

    result, grad_a, grad_b, grad_c = pl.pallas_call(
        finalize,
        out_shape=(
            jax.ShapeDtypeStruct(features.shape, bf16),
            jax.ShapeDtypeStruct((27, 4, 128), f32),
            jax.ShapeDtypeStruct((27, 4, 128), f32),
            jax.ShapeDtypeStruct((432, 512), f32),
        ),
        in_specs=[hbm] * 4,
        out_specs=(hbm,) * 4,
        scratch_shapes=[
            pltpu.VMEM(features.shape, bf16),
            pltpu.VMEM((2, 8, 16, 128), f32),
            pltpu.VMEM((2, NY, 224, 128), bf16),
            pltpu.VMEM((2, 27, 4, 128), f32),
            pltpu.VMEM((432, 512), f32),
            pltpu.SemaphoreType.DMA((10,)),
        ],
        compiler_params=pltpu.CompilerParams(vmem_limit_bytes=60 * 1024 * 1024),
    )(result, fga, fgb, fgc)
    return (
        result,
        grad_a.transpose(0, 2, 1),
        grad_b.transpose(0, 2, 1),
        grad_c.reshape(27, 16, 512).transpose(0, 2, 1),
    )


def solution(mesh):
    return jax.shard_map(
        body,
        mesh=mesh,
        in_specs=(
            P("member", "gx", None, None, None),
            P("member", "gx", None, None, None),
            P("member", None),
            P(),
            P(),
            P(None, None, "gx"),
            P(),
            P(),
            P(),
            P(),
        ),
        out_specs=(
            P("member", "gx", None, None, None),
            P(None, None, "gx"),
            P(None, None, "gx"),
            P(None, None, "gx"),
        ),
        check_vma=False,
    )
```

```python
import jax
import jax.numpy as jnp
from jax import lax
from jax.experimental import pallas as pl
from jax.experimental.pallas import tpu as pltpu
from jax.sharding import PartitionSpec as P

f32 = jnp.float32
bf16 = jnp.bfloat16
MESH = pl.DeviceIdType.MESH

NY, NZH, NCORE, NXC, NZL = 4, 2, 2, 4, 8
NZ = NZH * NZL
SURVIVAL = (0.9, 0.8, 0.7)

COPIES = dict(
    halo_a=2,
    halo_b=2,
    halo_d=2,
    bz=7,
    bx=3,
    fz=7,
    fx=3,
    cot=4,
    cot_f=3,
    hid=4,
    hid_f=3,
    hb=7,
    gb=7,
    m1=7,
    rxb=3,
    rxf=3,
    rzb=7,
    rzf=7,
    a_x=3,
    a_z=15,
    a_all=7,
    b_x=3,
    b_z=15,
    b_all=7,
    c_core=1,
    c_y=3,
    c_zh=1,
    c_ay=3,
    c_ac=1,
)


class S:
    pass


TOTAL = 0
for _name, _count in COPIES.items():
    setattr(S, _name, TOTAL)
    TOTAL += _count
KINDS = ((S.a_x, S.a_z, S.a_all), (S.b_x, S.b_z, S.b_all))

NN = (((1,), (0,)), ((), ()))
NT = (((1,), (1,)), ((), ()))
TN = (((0,), (0,)), ((), ()))


def mm(a, b, dims=NN):
    return lax.dot_general(a, b, dims, preferred_element_type=f32)


def silu(v):
    return v * jax.nn.sigmoid(v)


def slope(v):
    s = jax.nn.sigmoid(v)
    return s * (1.0 + v * (1.0 - s))


SCRATCH = dict(
    fv=((2, 8, 32, 128), bf16),
    cv=((2, 8, 32, 128), bf16),
    kv=((1, 3), jnp.int32),
    wa=((9, 384, 128), bf16),
    wb=((9, 384, 128), bf16),
    wc=((432, 512), bf16),
    l1=((128, 128), bf16),
    l2=((128, 512), bf16),
    w2=((512, 128), bf16),
    w1=((128, 128), bf16),
    rv=((2, 8, 32, 128), bf16),
    halo_a=((2, 8, 32, 128), bf16),
    hs=((8, 3, 4, 10, 32, 128), bf16),
    la=((2, 256, 128), f32),
    pool_s=((128, 128), f32),
    grow_s=((128, 128), f32),
    hb_own=((64, 128), bf16),
    halo_b=((2, 64, 128), bf16),
    hsb=((8, 3, 3, 6, 16, 128), bf16),
    small_s=((32, 128), f32),
    gd_own=((64, 128), bf16),
    halo_d=((2, 64, 128), bf16),
    bz_buf=((8, 16, 128), bf16),
    ge=((18, 16, 128), bf16),
    fz_buf=((8, 16, 128), bf16),
    fx_buf=((4, 4, 16, 128), bf16),
    st=((448, 256), bf16),
    mp=((18, 16, 128), bf16),
    up=((16, 16, 128), bf16),
    rxb=((3, 6, 16, 128), bf16),
    rxf=((3, 4, 16, 128), bf16),
    sb=((6, 16, 128), bf16),
    sf=((4, 16, 128), bf16),
    rzb=((7, 2, 16, 128), bf16),
    rzf=((7, 16, 128), bf16),
    gbs=((3, 3, 6, 16, 128), bf16),
    cq=((8, 128, 512), bf16),
    gbq=((8, 64, 128), bf16),
    m1q=((8, 64, 128), bf16),
    gt=((8, 128, 512), bf16),
    xs=((2, 4, 4, 32, 128), bf16),
    xr=((2, 3, 4, 32, 128), bf16),
    zs=((2, 8, 16, 128), bf16),
    zr=((2, 16, 16, 128), bf16),
    zt=((2, 16, 128), f32),
    fc=((4, 224, 128), bf16),
    dc=((2, 4, 224, 128), bf16),
    c_cr=((4, 224, 128), bf16),
    c_ys=((4, 224, 128), bf16),
    c_yr=((3, 224, 128), bf16),
    c_zs=((224, 128), bf16),
    c_zr=((224, 128), bf16),
)


class Bufs:
    pass


def kernel(
    feat_h,
    cot_h,
    keep_h,
    wa_h,
    wb_h,
    wc_h,
    l1_h,
    l2_h,
    w2_h,
    w1_h,
    res,
    fga,
    fgb,
    fgc,
    *scratch,
):
    b = Bufs()
    for name, ref in zip(SCRATCH, scratch):
        setattr(b, name, ref)
    local_sem, send_sem, recv_sem = scratch[len(SCRATCH) :]

    m = lax.axis_index("member")
    g = lax.axis_index("gx")
    x, z = g // NZL, g % NZL
    core, zh, y = m % NCORE, (m // NCORE) % NZH, m // (NCORE * NZH)
    z16 = zh * NZL + z
    q = y * 2 + core

    def chosen(*values):
        return sum((y == k).astype(jnp.int32) * value for k, value in enumerate(values))

    share = chosen(0, 4, 2, 1) * (1 - core) + chosen(3, 5, 6, 7) * core

    def dev(dy=None, dzh=None, dcore=None, dx=None, dz=None):
        yy = y if dy is None else dy
        hh = zh if dzh is None else dzh
        cc = core if dcore is None else dcore
        xx = x if dx is None else dx
        zz = z if dz is None else dz
        return ((yy * NZH + hh) * NCORE + cc, xx * NZL + zz)

    nxt = (m, (g + 1) % (NXC * NZL))
    prv = (m, (g + NXC * NZL - 1) % (NXC * NZL))
    x_of = [(x + k) % NXC for k in range(NXC)]
    z_of = [(z + k) % NZL for k in range(NZL)]
    y_of = [(y + k) % NY for k in range(NY)]
    y_from = [(y + NY - k) % NY for k in range(NY)]
    z16_of = [(z16 + k) % NZ for k in range(NZ)]
    group_of = [(y_of[k // 2], (core + k) % 2) for k in range(8)]
    group_dev = [dev(dy=yy, dcore=cc) for yy, cc in group_of]
    sibling = dev(dcore=1 - core)

    barrier = pltpu.get_barrier_semaphore()
    targets = [prv, nxt]
    targets += [dev(dx=x_of[k]) for k in range(1, NXC)]
    targets += [dev(dzh=z16_of[k] // NZL, dz=z16_of[k] % NZL) for k in range(1, NZ)]
    targets += group_dev[1:]
    for target in targets:
        pl.semaphore_signal(barrier, inc=1, device_id=target, device_id_type=MESH)

    started = []

    def finish(count):
        for copy in started[:count]:
            copy.wait_send()
        del started[:count]

    def send(name, k, src, dst, target):
        index = name + k
        copy = pltpu.make_async_remote_copy(
            src_ref=src,
            dst_ref=dst,
            send_sem=send_sem.at[index],
            recv_sem=recv_sem.at[index],
            device_id=target,
            device_id_type=MESH,
        )
        copy.start()
        started.append(copy)
        return copy

    def arrived(copies):
        for copy in copies:
            copy.wait_recv()

    loads = Bufs()

    def load_all(first, **sources):
        for k, (name, src) in enumerate(sources.items()):
            load = pltpu.make_async_copy(src, getattr(b, name), local_sem.at[first + k])
            load.start()
            setattr(loads, name, load)

    load_all(0, fv=feat_h.at[0], wa=wa_h)
    pl.semaphore_wait(barrier, len(targets))
    halo_a_copies = [
        send(S.halo_a, 0, feat_h.at[0, 1], b.halo_a.at[0], nxt),
        send(S.halo_a, 1, feat_h.at[0, 0], b.halo_a.at[1], prv),
    ]
    load_all(2, cv=cot_h.at[0], w1=w1_h, kv=keep_h, l1=l1_h, wb=wb_h, w2=w2_h, wc=wc_h, l2=l2_h)

    has_prev = (g > 0).astype(f32)
    has_next = (g < NXC * NZL - 1).astype(f32)

    def z_shifts(h, length):
        rows = h.shape[0]
        pos = lax.broadcasted_iota(jnp.int32, h.shape, 0) % length
        before = jnp.where(pos == 0, 0.0, pltpu.roll(h, 1, 0))
        after = jnp.where(pos == length - 1, 0.0, pltpu.roll(h, rows - 1, 0))
        return before, h, after

    def put(cat, plane, h, grid_y, grid_z, shifts=(0, 1, 2)):
        pieces = z_shifts(h, grid_z)
        for k in shifts:
            piece = pieces[k].astype(bf16)
            cat[k, plane, 1 : 1 + grid_y] = piece.reshape(grid_y, grid_z, 128)

    def pool_yz(v, grid_y, grid_z, scratch_ref):
        half = v.reshape(grid_y // 2, 2, grid_z, 128).sum(axis=1)
        n = grid_y // 2 * grid_z
        scratch_ref[0:n, :] = half.reshape(n, 128)
        even = scratch_ref[pl.ds(0, n // 2, stride=2), :]
        return even + scratch_ref[pl.ds(1, n // 2, stride=2), :]

    def grow_yz(v, grid_y, grid_z, scratch_ref):
        n = grid_y * grid_z
        scratch_ref[pl.ds(0, n, stride=2), :] = v
        scratch_ref[pl.ds(1, n, stride=2), :] = v
        wide = scratch_ref[0 : 2 * n, :].reshape(grid_y, 1, 2 * grid_z, 128)
        return jnp.broadcast_to(wide, (grid_y, 2, 2 * grid_z, 128)).reshape(4 * n, 128)

    def wide_field(cat, plane, first, grid_y, grid_z, turned=False):
        order = (2, 1, 0) if turned else (0, 1, 2)
        pieces = [
            cat[k, plane, first : first + grid_y].reshape(grid_y * grid_z, 128) for k in order
        ]
        return jnp.concatenate(pieces, axis=1)

    row = lax.broadcasted_iota(jnp.int32, (128, 128), 0)
    col = lax.broadcasted_iota(jnp.int32, (128, 128), 1)
    unit = (row == col).astype(f32).astype(bf16)

    def clear(i, carry):
        for k in range(3):
            for p in range(4):
                b.hs[i, k, p, 0] = jnp.zeros((32, 128), bf16)
                b.hs[i, k, p, 9] = jnp.zeros((32, 128), bf16)
            for p in range(3):
                b.hsb[i, k, p, 0] = jnp.zeros((16, 128), bf16)
                b.hsb[i, k, p, 5] = jnp.zeros((16, 128), bf16)
        return carry

    clear(q, 0)
    for ref in (b.ge, b.mp):
        ref[0] = jnp.zeros((16, 128), bf16)
        ref[17] = jnp.zeros((16, 128), bf16)

    hs_own = b.hs.at[q]
    hsb_own = b.hsb.at[q]

    def put_a(plane, h):
        put(hs_own, plane, h, 8, 32)

    loads.fv.wait()
    for p in range(2):
        put_a(1 + p, silu(b.fv[p].astype(f32).reshape(256, 128)))

    def taps_a(acc, p, dx):
        for dy in range(3):
            acc = acc + mm(wide_field(hs_own, p + dx, dy, 8, 32), b.wa[3 * dx + dy])
        return acc

    loads.wa.wait()
    acc_a = [jnp.zeros((256, 128), f32), jnp.zeros((256, 128), f32)]
    acc_a[0] = taps_a(taps_a(acc_a[0], 0, 1), 0, 2)
    acc_a[1] = taps_a(taps_a(acc_a[1], 1, 1), 1, 0)
    for p in range(2):
        b.la[p] = acc_a[p]

    loads.cv.wait()
    loads.w1.wait()
    loads.kv.wait()
    flags = b.kv[...].astype(f32)
    flag = [flags[0:1, j : j + 1] for j in range(3)]
    scale = [flag[j] * f32(1.0 / SURVIVAL[j]) for j in range(3)]
    up32 = [b.cv[p].astype(f32).reshape(256, 128) for p in range(2)]
    grad_e1 = pool_yz(up32[0] + up32[1], 8, 32, b.pool_s).astype(bf16)
    grad_d = mm(grad_e1, b.w1[...], NT).astype(bf16)
    b.gd_own[...] = grad_d
    b.bz_buf[z] = pool_yz(grad_d.astype(f32), 4, 16, b.small_s).astype(bf16)
    bz_copies = [
        send(S.bz, k - 1, b.bz_buf.at[z], b.bz_buf.at[z], dev(dz=z_of[k]))
        for k in range(1, NZL)
    ]
    halo_d_copies = [
        send(S.halo_d, 0, b.gd_own, b.halo_d.at[0], nxt),
        send(S.halo_d, 1, b.gd_own, b.halo_d.at[1], prv),
    ]
    for p in range(2):
        turned = mm(unit, (up32[p] * flag[0]).astype(bf16), NT).astype(bf16)
        b.cq[q, :, 256 * p : 256 * p + 256] = turned
    peers = [sibling] + [dev(dy=y_of[k]) for k in range(1, NY)]

    def whole(ref, slot, to_y):
        return ref.at[slot]

    def some(count, grid_y):
        return lambda ref, slot, to_y: ref.at[slot, 1, pl.ds(to_y // 2, count), pl.ds(1, grid_y)]

    def spread(name, ref, part=whole):
        result = []
        for k in range(4):
            piece = part(ref, q, y_of[k])
            result.append(send(name, k, piece, piece, peers[k]))
        return result

    def forward(name, ref, copies, part=whole):
        result = []
        for k in range(1, NY):
            piece = part(ref, y_from[k] * 2 + core, y)
            pltpu.make_async_remote_copy(
                src_ref=piece,
                dst_ref=piece,
                send_sem=send_sem.at[0],
                recv_sem=recv_sem.at[copies[k]],
                device_id=sibling,
                device_id_type=MESH,
            ).wait_recv()
            result.append(send(name, k - 1, piece, piece, sibling))
        return result

    def to_group(name, ref, part=whole):
        result = []
        for k in range(1, 8):
            piece = part(ref, q, group_of[k][0])
            result.append(send(name, k - 1, piece, piece, group_dev[k]))
        return result

    cot_copies = spread(S.cot, b.cq)
    cot_sems = [S.cot + k for k in range(4)]
    hid_sems = [S.hid + k for k in range(4)]

    near = (z == 0).astype(jnp.int32)

    def side_in(name, ref, side):
        pltpu.make_async_remote_copy(
            src_ref=ref.at[side],
            dst_ref=ref.at[side],
            send_sem=send_sem.at[name],
            recv_sem=recv_sem.at[name + side],
            device_id=nxt,
            device_id_type=MESH,
        ).wait_recv()
        return jnp.where(side == 0, has_prev, has_next)

    for side in (near, 1 - near):
        inside = side_in(S.halo_a, b.halo_a, side)
        put_a(3 * side, silu(b.halo_a[side].astype(f32).reshape(256, 128)) * inside)
        acc = b.la[side]
        for dy in range(3):
            acc = acc + mm(wide_field(hs_own, 3 * side, dy, 8, 32), b.wa[6 * side + dy])
        b.la[side] = acc
    hid_copies = spread(S.hid, b.hs, some(3, 8))
    level_a = []
    for p in range(2):
        value = b.fv[p].astype(f32).reshape(256, 128) + scale[0] * b.la[p]
        b.la[p] = value
        level_a.append(value)
    pooled = (pool_yz(level_a[0] + level_a[1], 8, 32, b.pool_s) * 0.125).astype(bf16)
    loads.l1.wait()
    lb = mm(pooled, b.l1[...]).astype(bf16).astype(f32)

    hidden_b = silu(lb)
    b.hb_own[...] = hidden_b.astype(bf16)
    halo_b_copies = [
        send(S.halo_b, 0, b.hb_own, b.halo_b.at[0], nxt),
        send(S.halo_b, 1, b.hb_own, b.halo_b.at[1], prv),
    ]

    def put_b(plane, h):
        put(hsb_own, plane, h, 4, 16)

    put_b(1, hidden_b)

    arrived(bz_copies)
    for k in range(4):
        both = b.bz_buf[2 * k].astype(f32) + b.bz_buf[2 * k + 1].astype(f32)
        b.ge[1 + 4 * x + k] = both.astype(bf16)
    own_ge = b.ge.at[pl.ds(1 + 4 * x, 4)]
    bx_copies = [send(S.bx, k - 1, own_ge, own_ge, dev(dx=x_of[k])) for k in range(1, NXC)]

    def taps_b(acc, dx):
        for dy in range(3):
            acc = acc + mm(wide_field(hsb_own, dx, dy, 4, 16), b.wb[3 * dx + dy])
        return acc

    lax.fori_loop(1, 8, lambda k, carry: clear(lax.rem(q + k, 8), carry), 0)
    loads.wb.wait()
    acc_b = taps_b(jnp.zeros((64, 128), f32), 1)
    for side in (near, 1 - near):
        inside = side_in(S.halo_b, b.halo_b, side)
        put_b(2 * side, b.halo_b[side].astype(f32) * inside)
        for dy in range(3):
            acc_b = acc_b + mm(wide_field(hsb_own, 2 * side, dy, 4, 16), b.wb[6 * side + dy])
    level_b = lb + scale[1] * acc_b
    b.fz_buf[z] = (pool_yz(level_b, 4, 16, b.small_s) * 0.25).astype(bf16)
    fz_copies = [
        send(S.fz, k - 1, b.fz_buf.at[z], b.fz_buf.at[z], dev(dz=z_of[k]))
        for k in range(1, NZL)
    ]

    for k in range(3):
        for p in range(3):
            b.gbs[k, p, 0] = jnp.zeros((16, 128), bf16)
            b.gbs[k, p, 5] = jnp.zeros((16, 128), bf16)
    for load in (loads.w2, loads.wc, loads.l2):
        load.wait()
    arrived(bx_copies)
    grad_e2 = b.ge[1:17].reshape(256, 128)
    own_rows = b.w2[pl.ds(pl.multiple_of(g * 16, 16), 16), :]
    grad_t = mm(own_rows, grad_e2, NT).astype(bf16).astype(f32)
    lane = lax.broadcasted_iota(jnp.int32, (16, 256), 1)
    pos_p, pos_y, pos_z = lane // 16, (lane // 8) % 2, lane % 8

    def moved(v, pos, length, step, d):
        if d == 0:
            return v
        ok = (pos + d >= 0) & (pos + d < length)
        return jnp.where(ok, pltpu.roll(v, (-d * step) % 256, 1), 0.0)

    for dx in range(3):
        vx = moved(grad_t, pos_p, 16, 16, 1 - dx)
        for dy in range(3):
            vy = moved(vx, pos_y, 2, 8, 1 - dy)
            for dz in range(3):
                tap = 9 * dx + 3 * dy + dz
                b.st[16 * tap : 16 * tap + 16, :] = moved(vy, pos_z, 8, 1, 1 - dz).astype(bf16)
    b.st[432:448, :] = jnp.zeros((16, 256), bf16)
    back_part = mm(b.st[0:432, :], b.wc[...], TN)
    start = z // 2 + z % 2
    two_e2 = b.ge[pl.ds(4 * x + start, 2)].reshape(32, 128)
    two_c = mm(two_e2, b.w2[...], NT).astype(bf16)
    two_m2 = mm(two_c, b.l2[...], NT)

    arrived(fz_copies)
    for k in range(4):
        both = b.fz_buf[2 * k].astype(f32) + b.fz_buf[2 * k + 1].astype(f32)
        b.fx_buf[x, k] = (both * 0.5).astype(bf16)
    fx_copies = [
        send(S.fx, k - 1, b.fx_buf.at[x], b.fx_buf.at[x], dev(dx=x_of[k]))
        for k in range(1, NXC)
    ]
    hb_copies = to_group(S.hb, b.hsb, some(2, 4))
    cot_forward = forward(S.cot_f, b.cq, cot_sems)
    arrived(fx_copies)
    pooled_two = b.fx_buf[...].reshape(256, 128)
    lc_b = mm(pooled_two, b.l2[...]).astype(bf16)
    lc = lc_b.astype(f32)
    sig = jax.nn.sigmoid(lc)
    hidden_c = (lc * sig).astype(bf16)
    weighted = (scale[2] * (sig * (1.0 + lc * (1.0 - sig))) * back_part).astype(bf16)
    b.mp[1:17] = mm(weighted, b.l2[...], NT).astype(bf16).reshape(16, 16, 128)
    rxb_copies = [
        send(S.rxb, k - 1, b.mp.at[pl.ds(4 * x_of[k], 6)], b.rxb.at[k - 1], dev(dx=x_of[k]))
        for k in range(1, NXC)
    ]
    taps = mm(b.wc[...], hidden_c, NT).reshape(9, 3, 16, 256)

    def folded(v, pos, length, step):
        total = v[:, 1]
        for d in (-1, 1):
            ok = (pos + d >= 0) & (pos + d < length)
            piece = v[:, 1 + d]
            turned = pltpu.roll(piece.reshape(-1, 256), (-d * step) % 256, 1)
            total = total + jnp.where(ok[None], turned.reshape(piece.shape), 0.0)
        return total

    conv_t = folded(taps, pos_z, 8, 1).reshape(3, 3, 16, 256)
    conv_t = folded(conv_t, pos_y, 2, 8).reshape(1, 3, 16, 256)
    conv_t = folded(conv_t, pos_p, 16, 16).reshape(16, 256)
    row16 = lax.broadcasted_iota(jnp.int32, (16, 512), 0)
    lane16 = lax.broadcasted_iota(jnp.int32, (16, 512), 1)
    pick = (lane16 == row16 + g * 16).astype(f32).astype(bf16)
    own_lc = mm(pick, lc_b, NT)
    level_c = (own_lc + scale[2] * conv_t).astype(bf16)
    b.up[...] = mm(level_c, own_rows, TN).astype(bf16).reshape(16, 16, 128)
    rxf_copies = [
        send(S.rxf, k - 1, b.up.at[pl.ds(4 * x_of[k], 4)], b.rxf.at[k - 1], dev(dx=x_of[k]))
        for k in range(1, NXC)
    ]

    arrived(rxb_copies)
    both = b.mp[pl.ds(4 * x, 6)].astype(f32)
    for k in range(3):
        both = both + b.rxb[k].astype(f32)
    b.sb[...] = both.astype(bf16)
    rzb_copies = []
    for k in range(1, NZL):
        first = z_of[k] // 2 + z_of[k] % 2
        rzb_copies.append(
            send(S.rzb, k - 1, b.sb.at[pl.ds(first, 2)], b.rzb.at[k - 1], dev(dz=z_of[k]))
        )
    grad_w = (scale[2] * mm(b.st[...], hidden_c)).astype(bf16)
    for cc in range(2):
        for yy in range(NY):
            b.dc[cc, yy] = grad_w[224 * cc : 224 * cc + 224, 128 * yy : 128 * yy + 128]
    hid_forward = forward(S.hid_f, b.hs, hid_sems, some(3, 8))
    c_core = send(S.c_core, 0, b.dc.at[1 - core], b.c_cr, sibling)

    def shifted(work):
        for shift, used in ((0, share <= 2), (2, share >= 4)):
            pl.when(used)(lambda: work((shift,)))

    def prepare(slots):
        def work(shifts):
            for slot in slots:

                def one(p, carry):
                    field = b.hs[slot, 1, p, 1:9].astype(f32).reshape(256, 128)
                    put(b.hs.at[slot], p, field, 8, 32, shifts)
                    return carry

                lax.fori_loop(y // 2, y // 2 + 3, one, 0)

        shifted(work)

    hid_copies[0].wait_recv()
    prepare([y * 2 + 1 - core] + [y_of[k] * 2 + core for k in range(1, NY)])

    c_core.wait_recv()
    for yy in range(NY):
        b.c_ys[yy] = (b.dc[core, yy].astype(f32) + b.c_cr[yy].astype(f32)).astype(bf16)
    c_y = [
        send(S.c_y, k - 1, b.c_ys.at[y_of[k]], b.c_yr.at[k - 1], dev(dy=y_of[k]))
        for k in range(1, NY)
    ]

    arrived(rzb_copies)
    both = b.sb[pl.ds(start, 2)].astype(f32)
    for k in range(7):
        both = both + b.rzb[k].astype(f32)
    two_m2 = (two_m2.reshape(2, 16, 128) + both).astype(bf16).astype(f32)
    even = (z % 2 == 0).astype(f32)
    lo, hi = two_m2[0], two_m2[1]
    own_m2 = hi * even + lo * (1.0 - even)
    arrived(halo_d_copies)

    def grad_plane(field, m2):
        return (field.astype(f32) + grow_yz(m2, 2, 8, b.small_s) * 0.125).astype(bf16)

    grad_b = grad_plane(b.gd_own[...], own_m2)
    grad_b32 = grad_b.astype(f32)
    b.gbq[q] = (grad_b32 * flag[1]).astype(bf16)
    put(b.gbs, 1, grad_b32, 4, 16)
    put(b.gbs, 0, grad_plane(b.halo_d[0], lo).astype(f32) * has_prev, 4, 16)
    put(b.gbs, 2, grad_plane(b.halo_d[1], hi).astype(f32) * has_next, 4, 16)
    back_b = jnp.zeros((64, 128), f32)
    for t in range(9):
        dx, dy = t // 3, t % 3
        for dz in range(3):
            part = b.gbs[2 - dz, 2 - dx, 2 - dy : 6 - dy].reshape(64, 128)
            back_b = back_b + mm(part, b.wb[t, 128 * dz : 128 * dz + 128, :], NT)
    grad_p = (grad_b32 + scale[1] * slope(lb) * back_b).astype(bf16)
    grad_m1 = mm(grad_p, b.l1[...], NT).astype(bf16).astype(f32)
    b.m1q[q] = (grad_m1 * flag[0]).astype(bf16)
    m1_copies = to_group(S.m1, b.m1q)
    gb_copies = to_group(S.gb, b.gbq)
    early = len(started)

    arrived(c_y)
    total = b.c_ys[y].astype(f32)
    for k in range(3):
        total = total + b.c_yr[k].astype(f32)
    b.c_zs[...] = total.astype(bf16)
    c_zh = send(S.c_zh, 0, b.c_zs, b.c_zr, dev(dzh=1 - zh))
    arrived(hb_copies)

    def prepare_b(shifts):
        for k in range(1, 8):
            slot = group_of[k][0] * 2 + group_of[k][1]
            for p in range(2):
                plane = y // 2 + p
                field = b.hsb[slot, 1, plane, 1:5].astype(f32).reshape(64, 128)
                put(b.hsb.at[slot], plane, field, 4, 16, shifts)

    shifted(prepare_b)
    arrived(hid_forward)
    prepare([y_from[k] * 2 + 1 - core for k in range(1, NY)])
    arrived(gb_copies)
    where = []
    for i in range(4):
        place = jnp.minimum(4 * share + i, 26)
        dz, e = place // 9, place % 9
        odd = dz % 2
        e = e * (1 - odd) + (8 - e) * odd
        where.append((e // 3, e % 3, dz))

    def keep_sum(kind, i, value):
        for k in range(NXC):
            b.xs[kind, k, i] = value[32 * k : 32 * k + 32].astype(bf16)

    stores = []

    def along_x(kind):
        return [
            send(
                KINDS[kind][0],
                k - 1,
                b.xs.at[kind, x_of[k]],
                b.xr.at[kind, k - 1],
                dev(dx=x_of[k]),
            )
            for k in range(1, NXC)
        ]

    source = ((row // 4) % 4) * 32 + (row // 16) * 4 + row % 4
    shuffle = (col == source).astype(f32).astype(bf16)

    def along_z(kind):
        total = b.xs[kind, x].astype(f32)
        for k in range(3):
            total = total + b.xr[kind, k].astype(f32)
        pieces = mm(shuffle, total.astype(bf16).reshape(128, 128)).astype(bf16)
        b.zs[kind] = pieces.reshape(8, 16, 128)
        copies = []
        for k in sorted(range(1, NZ), key=lambda k: abs(k - NZ // 2)):
            target = dev(dzh=z16_of[k] // NZL, dz=z16_of[k] % NZL)
            src = b.zs.at[kind, z16_of[k] % NZL]
            copies.append(send(KINDS[kind][1], k - 1, src, b.zr.at[kind, z16], target))
        b.zr[kind, z16] = b.zs[kind, z]
        return copies

    def to_all(kind):
        total = b.zr[kind, 0].astype(f32)
        for k in range(1, NZ):
            total = total + b.zr[kind, k].astype(f32)
        b.zt[kind] = total
        own = (fga, fgb)[kind].at[q]
        copies = [
            send(KINDS[kind][2], k - 1, b.zt.at[kind], own, group_dev[k]) for k in range(1, 8)
        ]
        stores.append(pltpu.make_async_copy(b.zt.at[kind], own, local_sem.at[11 + kind]))
        stores[-1].start()
        return copies

    turned_b = mm(unit, b.gbq[...].reshape(512, 128), NT).astype(bf16)
    for i, (dx, dy, dz) in enumerate(where):
        field = b.hsb[:, dz, dx, pl.ds(dy, 4)].reshape(512, 128)
        keep_sum(1, i, mm(turned_b, field) * f32(1.0 / SURVIVAL[1]))
    b_x = along_x(1)
    cot_copies[0].wait_recv()
    arrived(cot_forward)

    coarse = lax.broadcasted_iota(jnp.int32, (64, 512), 0)
    fine = lax.broadcasted_iota(jnp.int32, (64, 512), 1)
    above = ((fine // 64) % 4) * 16 + (fine % 32) // 2
    grow = jnp.where(coarse == above, 0.125, 0.0).astype(bf16)
    for k in (0, 1, 2, 3, 6, 7, 4, 5):
        if k:
            m1_copies[k - 1].wait_recv()
        j = y_from[k // 2] * 2 + (core + k) % 2
        b.gt[j] = (b.cq[j].astype(f32) + mm(b.m1q[j], grow, TN)).astype(bf16)
    for pair in range(2):
        acc = jnp.zeros((128, 256), f32)
        for j in range(8):
            pieces = []
            for i in (2 * pair, 2 * pair + 1):
                dx, dy, dz = where[i]
                pieces.append(b.hs[j, dz, pl.ds(dx, 2), pl.ds(dy, 8)].reshape(512, 128))
            acc = acc + mm(b.gt[j], jnp.concatenate(pieces, axis=1))
        acc = acc * f32(1.0 / SURVIVAL[0])
        keep_sum(0, 2 * pair, acc[:, 0:128])
        keep_sum(0, 2 * pair + 1, acc[:, 128:256])
    a_x = along_x(0)

    arrived(b_x)
    b_z = along_z(1)
    c_zh.wait_recv()
    b.fc[y] = (b.c_zs[...].astype(f32) + b.c_zr[...].astype(f32)).astype(bf16)
    own_c = b.fc.at[y]
    c_ay = [send(S.c_ay, k - 1, own_c, own_c, dev(dy=y_of[k])) for k in range(1, NY)]

    arrived(a_x)
    a_z = along_z(0)
    arrived(rxf_copies)
    both = b.up[pl.ds(4 * x, 4)].astype(f32)
    for k in range(3):
        both = both + b.rxf[k].astype(f32)
    b.sf[...] = both.astype(bf16)
    rzf_copies = [
        send(S.rzf, k - 1, b.sf.at[z_of[k] // 2], b.rzf.at[k - 1], dev(dz=z_of[k]))
        for k in range(1, NZL)
    ]

    arrived(c_ay)
    stores.append(pltpu.make_async_copy(b.fc, fgc.at[core], local_sem.at[13]))
    stores[-1].start()
    c_ac = send(S.c_ac, 0, b.fc, fgc.at[core], sibling)
    arrived(b_z)
    b_all = to_all(1)
    finish(early)

    arrived(a_z)
    a_all = to_all(0)
    arrived(rzf_copies)
    both = b.sf[z // 2].astype(f32)
    for k in range(7):
        both = both + b.rzf[k].astype(f32)
    level_d = (level_b + grow_yz(both, 2, 8, b.small_s)).astype(bf16)
    wide = grow_yz(mm(level_d, b.w1[...]), 4, 16, b.grow_s)
    for p in range(2):
        b.rv[p] = (b.la[p] + wide).astype(bf16).reshape(8, 32, 128)
    stores.append(pltpu.make_async_copy(b.rv, res.at[0], local_sem.at[10]))
    stores[-1].start()
    arrived(b_all)
    finish(len(started) - 7)
    c_ac.wait_recv()
    for copy in stores:
        copy.wait()
    arrived(a_all)
    finish(len(started))


OWNER = (0, 6, 4, 1, 2, 3, 5, 7)


def finalize(
    res, fga, fgb, fgc, out, out_a, out_b, out_c, res_v, fg_v, fgc_v, tables, wide, sems
):
    parts = [
        pltpu.make_async_copy(fgc.at[part], fgc_v.at[part], sems.at[part]) for part in range(2)
    ]
    loads = [
        pltpu.make_async_copy(res, res_v, sems.at[2]),
        pltpu.make_async_copy(fga, fg_v.at[0], sems.at[3]),
        pltpu.make_async_copy(fgb, fg_v.at[1], sems.at[4]),
    ]
    for load in parts + loads:
        load.start()
    copies = []

    def store(src, dst):
        copies.append(pltpu.make_async_copy(src, dst, sems.at[5 + len(copies)]))
        copies[-1].start()

    for part in range(2):
        parts[part].wait()
        rows = pl.ds(224 * part, 224 - 16 * part)
        for yy in range(NY):
            wide[rows, 128 * yy : 128 * yy + 128] = fgc_v[part, yy, 0 : 224 - 16 * part].astype(f32)
        store(wide.at[rows], out_c.at[rows])
        if part == 0:
            loads[0].wait()
            store(res_v, out)
    for kind, target in enumerate((out_a, out_b)):
        loads[1 + kind].wait()
        for t in range(27):
            e, dz = t // 3, t % 3
            place = 9 * dz + (8 - e if dz == 1 else e)
            first = 4 * (place % 4)
            tables[kind, t] = fg_v[kind, OWNER[place // 4], first : first + 4]
        store(tables.at[kind], target)
    for copy in copies:
        copy.wait()


def body(
    features,
    cotangent,
    keep_flags,
    conv_a,
    conv_b,
    conv_c,
    lift_one,
    lift_two,
    lower_two,
    lower_one,
):
    hbm = pl.BlockSpec(memory_space=pltpu.HBM)
    result, fga, fgb, fgc = pl.pallas_call(
        kernel,
        out_shape=(
            jax.ShapeDtypeStruct(features.shape, bf16),
            jax.ShapeDtypeStruct((8, 16, 128), f32),
            jax.ShapeDtypeStruct((8, 16, 128), f32),
            jax.ShapeDtypeStruct((2, NY, 224, 128), bf16),
        ),
        in_specs=[hbm] * 10,
        out_specs=(hbm,) * 4,
        scratch_shapes=[pltpu.VMEM(shape, dtype) for shape, dtype in SCRATCH.values()]
        + [
            pltpu.SemaphoreType.DMA((14,)),
            pltpu.SemaphoreType.DMA((TOTAL,)),
            pltpu.SemaphoreType.DMA((TOTAL,)),
        ],
        compiler_params=pltpu.CompilerParams(
            collective_id=0, has_side_effects=True, vmem_limit_bytes=60 * 1024 * 1024
        ),
        cost_estimate=pl.CostEstimate(
            flops=1_400_000_000, bytes_accessed=5_000_000, transcendentals=600_000
        ),
    )(
        features,
        cotangent,
        keep_flags,
        conv_a.reshape(9, 384, 128),
        conv_b.reshape(9, 384, 128),
        conv_c.transpose(0, 2, 1).reshape(432, 512),
        lift_one,
        lift_two,
        lower_two,
        lower_one,
    )

    result, grad_a, grad_b, grad_c = pl.pallas_call(
        finalize,
        out_shape=(
            jax.ShapeDtypeStruct(features.shape, bf16),
            jax.ShapeDtypeStruct((27, 4, 128), f32),
            jax.ShapeDtypeStruct((27, 4, 128), f32),
            jax.ShapeDtypeStruct((432, 512), f32),
        ),
        in_specs=[hbm] * 4,
        out_specs=(hbm,) * 4,
        scratch_shapes=[
            pltpu.VMEM(features.shape, bf16),
            pltpu.VMEM((2, 8, 16, 128), f32),
            pltpu.VMEM((2, NY, 224, 128), bf16),
            pltpu.VMEM((2, 27, 4, 128), f32),
            pltpu.VMEM((432, 512), f32),
            pltpu.SemaphoreType.DMA((10,)),
        ],
        compiler_params=pltpu.CompilerParams(vmem_limit_bytes=60 * 1024 * 1024),
    )(result, fga, fgb, fgc)
    return (
        result,
        grad_a.transpose(0, 2, 1),
        grad_b.transpose(0, 2, 1),
        grad_c.reshape(27, 16, 512).transpose(0, 2, 1),
    )


def solution(mesh):
    return jax.shard_map(
        body,
        mesh=mesh,
        in_specs=(
            P("member", "gx", None, None, None),
            P("member", "gx", None, None, None),
            P("member", None),
            P(),
            P(),
            P(None, None, "gx"),
            P(),
            P(),
            P(),
            P(),
        ),
        out_specs=(
            P("member", "gx", None, None, None),
            P(None, None, "gx"),
            P(None, None, "gx"),
            P(None, None, "gx"),
        ),
        check_vma=False,
    )
```

```python
import jax
import jax.numpy as jnp
from jax import lax
from jax.experimental import pallas as pl
from jax.experimental.pallas import tpu as pltpu
from jax.sharding import PartitionSpec as P

f32 = jnp.float32
bf16 = jnp.bfloat16
MESH = pl.DeviceIdType.MESH

NY, NZH, NCORE, NXC, NZL = 4, 2, 2, 4, 8
NZ = NZH * NZL
SURVIVAL = (0.9, 0.8, 0.7)

COPIES = dict(
    halo_a=2,
    halo_b=2,
    halo_d=2,
    bz=7,
    bx=3,
    fz=7,
    fx=3,
    cot=4,
    cot_f=3,
    hid=4,
    hid_f=3,
    hb=7,
    gb=7,
    m1=7,
    rxb=3,
    rxf=3,
    rzb=7,
    rzf=7,
    a_x=3,
    a_z=15,
    a_all=7,
    b_x=3,
    b_z=15,
    b_all=7,
    c_core=1,
    c_y=3,
    c_zh=1,
    c_ay=3,
    c_ac=1,
)


class S:
    pass


TOTAL = 0
for _name, _count in COPIES.items():
    setattr(S, _name, TOTAL)
    TOTAL += _count
KINDS = ((S.a_x, S.a_z, S.a_all), (S.b_x, S.b_z, S.b_all))

NN = (((1,), (0,)), ((), ()))
NT = (((1,), (1,)), ((), ()))
TN = (((0,), (0,)), ((), ()))


def mm(a, b, dims=NN):
    return lax.dot_general(a, b, dims, preferred_element_type=f32)


def silu(v):
    return v * jax.nn.sigmoid(v)


def slope(v):
    s = jax.nn.sigmoid(v)
    return s * (1.0 + v * (1.0 - s))


SCRATCH = dict(
    fv=((2, 8, 32, 128), bf16),
    cv=((2, 8, 32, 128), bf16),
    kv=((1, 3), jnp.int32),
    wa=((9, 384, 128), bf16),
    wb=((9, 384, 128), bf16),
    wc=((432, 512), bf16),
    l1=((128, 128), bf16),
    l2=((128, 512), bf16),
    w2=((512, 128), bf16),
    w1=((128, 128), bf16),
    rv=((2, 8, 32, 128), bf16),
    halo_a=((2, 8, 32, 128), bf16),
    hs=((8, 3, 4, 10, 32, 128), bf16),
    la=((2, 256, 128), f32),
    pool_s=((128, 128), f32),
    grow_s=((128, 128), f32),
    hb_own=((64, 128), bf16),
    halo_b=((2, 64, 128), bf16),
    hsb=((8, 3, 3, 6, 16, 128), bf16),
    small_s=((32, 128), f32),
    gd_own=((64, 128), bf16),
    halo_d=((2, 64, 128), bf16),
    bz_buf=((8, 16, 128), bf16),
    ge=((18, 16, 128), bf16),
    fz_buf=((8, 16, 128), bf16),
    fx_buf=((4, 4, 16, 128), bf16),
    st=((448, 256), bf16),
    mp=((18, 16, 128), bf16),
    up=((16, 16, 128), bf16),
    rxb=((3, 6, 16, 128), bf16),
    rxf=((3, 4, 16, 128), bf16),
    sb=((6, 16, 128), bf16),
    sf=((4, 16, 128), bf16),
    rzb=((7, 2, 16, 128), bf16),
    rzf=((7, 16, 128), bf16),
    gbs=((3, 3, 6, 16, 128), bf16),
    cq=((8, 128, 512), bf16),
    gbq=((8, 64, 128), bf16),
    m1q=((8, 64, 128), bf16),
    gt=((8, 128, 512), bf16),
    xs=((2, 4, 4, 32, 128), bf16),
    xr=((2, 3, 4, 32, 128), bf16),
    zs=((2, 8, 16, 128), bf16),
    zr=((2, 16, 16, 128), bf16),
    zt=((2, 16, 128), f32),
    fc=((4, 224, 128), bf16),
    dc=((2, 4, 224, 128), bf16),
    c_cr=((4, 224, 128), bf16),
    c_ys=((4, 224, 128), bf16),
    c_yr=((3, 224, 128), bf16),
    c_zs=((224, 128), bf16),
    c_zr=((224, 128), bf16),
)


class Bufs:
    pass


def kernel(
    feat_h,
    cot_h,
    keep_h,
    wa_h,
    wb_h,
    wc_h,
    l1_h,
    l2_h,
    w2_h,
    w1_h,
    res,
    fga,
    fgb,
    fgc,
    *scratch,
):
    b = Bufs()
    for name, ref in zip(SCRATCH, scratch):
        setattr(b, name, ref)
    local_sem, send_sem, recv_sem = scratch[len(SCRATCH) :]

    m = lax.axis_index("member")
    g = lax.axis_index("gx")
    x, z = g // NZL, g % NZL
    core, zh, y = m % NCORE, (m // NCORE) % NZH, m // (NCORE * NZH)
    z16 = zh * NZL + z
    q = y * 2 + core

    def chosen(*values):
        return sum((y == k).astype(jnp.int32) * value for k, value in enumerate(values))

    share = chosen(0, 4, 2, 1) * (1 - core) + chosen(3, 5, 6, 7) * core

    def dev(dy=None, dzh=None, dcore=None, dx=None, dz=None):
        yy = y if dy is None else dy
        hh = zh if dzh is None else dzh
        cc = core if dcore is None else dcore
        xx = x if dx is None else dx
        zz = z if dz is None else dz
        return ((yy * NZH + hh) * NCORE + cc, xx * NZL + zz)

    nxt = (m, (g + 1) % (NXC * NZL))
    prv = (m, (g + NXC * NZL - 1) % (NXC * NZL))
    x_of = [(x + k) % NXC for k in range(NXC)]
    z_of = [(z + k) % NZL for k in range(NZL)]
    y_of = [(y + k) % NY for k in range(NY)]
    y_from = [(y + NY - k) % NY for k in range(NY)]
    z16_of = [(z16 + k) % NZ for k in range(NZ)]
    group_of = [(y_of[k // 2], (core + k) % 2) for k in range(8)]
    group_dev = [dev(dy=yy, dcore=cc) for yy, cc in group_of]
    sibling = dev(dcore=1 - core)

    barrier = pltpu.get_barrier_semaphore()
    targets = [prv, nxt]
    targets += [dev(dx=x_of[k]) for k in range(1, NXC)]
    targets += [dev(dzh=z16_of[k] // NZL, dz=z16_of[k] % NZL) for k in range(1, NZ)]
    targets += group_dev[1:]
    for target in targets:
        pl.semaphore_signal(barrier, inc=1, device_id=target, device_id_type=MESH)

    started = []

    def finish(count):
        for copy in started[:count]:
            copy.wait_send()
        del started[:count]

    def send(name, k, src, dst, target):
        index = name + k
        copy = pltpu.make_async_remote_copy(
            src_ref=src,
            dst_ref=dst,
            send_sem=send_sem.at[index],
            recv_sem=recv_sem.at[index],
            device_id=target,
            device_id_type=MESH,
        )
        copy.start()
        started.append(copy)
        return copy

    def arrived(copies):
        for copy in copies:
            copy.wait_recv()

    loads = Bufs()

    def load_all(first, **sources):
        for k, (name, src) in enumerate(sources.items()):
            load = pltpu.make_async_copy(src, getattr(b, name), local_sem.at[first + k])
            load.start()
            setattr(loads, name, load)

    load_all(0, fv=feat_h.at[0], wa=wa_h)
    pl.semaphore_wait(barrier, len(targets))
    halo_a_copies = [
        send(S.halo_a, 0, feat_h.at[0, 1], b.halo_a.at[0], nxt),
        send(S.halo_a, 1, feat_h.at[0, 0], b.halo_a.at[1], prv),
    ]
    load_all(2, cv=cot_h.at[0], w1=w1_h, kv=keep_h, l1=l1_h, wb=wb_h, w2=w2_h, wc=wc_h, l2=l2_h)

    has_prev = (g > 0).astype(f32)
    has_next = (g < NXC * NZL - 1).astype(f32)

    def z_shifts(h, length):
        rows = h.shape[0]
        pos = lax.broadcasted_iota(jnp.int32, h.shape, 0) % length
        before = jnp.where(pos == 0, 0.0, pltpu.roll(h, 1, 0))
        after = jnp.where(pos == length - 1, 0.0, pltpu.roll(h, rows - 1, 0))
        return before, h, after

    def put(cat, plane, h, grid_y, grid_z, shifts=(0, 1, 2)):
        pieces = z_shifts(h, grid_z)
        for k in shifts:
            piece = pieces[k].astype(bf16)
            cat[k, plane, 1 : 1 + grid_y] = piece.reshape(grid_y, grid_z, 128)

    def pool_yz(v, grid_y, grid_z, scratch_ref):
        half = v.reshape(grid_y // 2, 2, grid_z, 128).sum(axis=1)
        n = grid_y // 2 * grid_z
        scratch_ref[0:n, :] = half.reshape(n, 128)
        even = scratch_ref[pl.ds(0, n // 2, stride=2), :]
        return even + scratch_ref[pl.ds(1, n // 2, stride=2), :]

    def grow_yz(v, grid_y, grid_z, scratch_ref):
        n = grid_y * grid_z
        scratch_ref[pl.ds(0, n, stride=2), :] = v
        scratch_ref[pl.ds(1, n, stride=2), :] = v
        wide = scratch_ref[0 : 2 * n, :].reshape(grid_y, 1, 2 * grid_z, 128)
        return jnp.broadcast_to(wide, (grid_y, 2, 2 * grid_z, 128)).reshape(4 * n, 128)

    def wide_field(cat, plane, first, grid_y, grid_z, turned=False):
        order = (2, 1, 0) if turned else (0, 1, 2)
        pieces = [
            cat[k, plane, first : first + grid_y].reshape(grid_y * grid_z, 128) for k in order
        ]
        return jnp.concatenate(pieces, axis=1)

    row = lax.broadcasted_iota(jnp.int32, (128, 128), 0)
    col = lax.broadcasted_iota(jnp.int32, (128, 128), 1)
    unit = (row == col).astype(f32).astype(bf16)

    def clear(i, carry):
        for k in range(3):
            for p in range(4):
                b.hs[i, k, p, 0] = jnp.zeros((32, 128), bf16)
                b.hs[i, k, p, 9] = jnp.zeros((32, 128), bf16)
            for p in range(3):
                b.hsb[i, k, p, 0] = jnp.zeros((16, 128), bf16)
                b.hsb[i, k, p, 5] = jnp.zeros((16, 128), bf16)
        return carry

    clear(q, 0)
    for ref in (b.ge, b.mp):
        ref[0] = jnp.zeros((16, 128), bf16)
        ref[17] = jnp.zeros((16, 128), bf16)

    hs_own = b.hs.at[q]
    hsb_own = b.hsb.at[q]

    def put_a(plane, h):
        put(hs_own, plane, h, 8, 32)

    loads.fv.wait()
    for p in range(2):
        put_a(1 + p, silu(b.fv[p].astype(f32).reshape(256, 128)))

    def taps_a(acc, p, dx):
        for dy in range(3):
            acc = acc + mm(wide_field(hs_own, p + dx, dy, 8, 32), b.wa[3 * dx + dy])
        return acc

    loads.wa.wait()
    acc_a = [jnp.zeros((256, 128), f32), jnp.zeros((256, 128), f32)]
    acc_a[0] = taps_a(taps_a(acc_a[0], 0, 1), 0, 2)
    acc_a[1] = taps_a(taps_a(acc_a[1], 1, 1), 1, 0)
    for p in range(2):
        b.la[p] = acc_a[p]

    loads.cv.wait()
    loads.w1.wait()
    loads.kv.wait()
    flags = b.kv[...].astype(f32)
    flag = [flags[0:1, j : j + 1] for j in range(3)]
    scale = [flag[j] * f32(1.0 / SURVIVAL[j]) for j in range(3)]
    up32 = [b.cv[p].astype(f32).reshape(256, 128) for p in range(2)]
    grad_e1 = pool_yz(up32[0] + up32[1], 8, 32, b.pool_s).astype(bf16)
    grad_d = mm(grad_e1, b.w1[...], NT).astype(bf16)
    b.gd_own[...] = grad_d
    b.bz_buf[z] = pool_yz(grad_d.astype(f32), 4, 16, b.small_s).astype(bf16)
    bz_copies = [
        send(S.bz, k - 1, b.bz_buf.at[z], b.bz_buf.at[z], dev(dz=z_of[k]))
        for k in range(1, NZL)
    ]
    halo_d_copies = [
        send(S.halo_d, 0, b.gd_own, b.halo_d.at[0], nxt),
        send(S.halo_d, 1, b.gd_own, b.halo_d.at[1], prv),
    ]
    for p in range(2):
        turned = mm(unit, (up32[p] * flag[0]).astype(bf16), NT).astype(bf16)
        b.cq[q, :, 256 * p : 256 * p + 256] = turned
    peers = [sibling] + [dev(dy=y_of[k]) for k in range(1, NY)]

    def whole(ref, slot, to_y):
        return ref.at[slot]

    def some(count, grid_y):
        return lambda ref, slot, to_y: ref.at[slot, 1, pl.ds(to_y // 2, count), pl.ds(1, grid_y)]

    def spread(name, ref, part=whole):
        result = []
        for k in range(4):
            piece = part(ref, q, y_of[k])
            result.append(send(name, k, piece, piece, peers[k]))
        return result

    def forward(name, ref, copies, part=whole):
        result = []
        for k in range(1, NY):
            piece = part(ref, y_from[k] * 2 + core, y)
            pltpu.make_async_remote_copy(
                src_ref=piece,
                dst_ref=piece,
                send_sem=send_sem.at[0],
                recv_sem=recv_sem.at[copies[k]],
                device_id=sibling,
                device_id_type=MESH,
            ).wait_recv()
            result.append(send(name, k - 1, piece, piece, sibling))
        return result

    def to_group(name, ref, part=whole):
        result = []
        for k in range(1, 8):
            piece = part(ref, q, group_of[k][0])
            result.append(send(name, k - 1, piece, piece, group_dev[k]))
        return result

    cot_copies = spread(S.cot, b.cq)
    cot_sems = [S.cot + k for k in range(4)]
    hid_sems = [S.hid + k for k in range(4)]

    near = (z == 0).astype(jnp.int32)

    def side_in(name, ref, side):
        pltpu.make_async_remote_copy(
            src_ref=ref.at[side],
            dst_ref=ref.at[side],
            send_sem=send_sem.at[name],
            recv_sem=recv_sem.at[name + side],
            device_id=nxt,
            device_id_type=MESH,
        ).wait_recv()
        return jnp.where(side == 0, has_prev, has_next)

    for side in (near, 1 - near):
        inside = side_in(S.halo_a, b.halo_a, side)
        put_a(3 * side, silu(b.halo_a[side].astype(f32).reshape(256, 128)) * inside)
        acc = b.la[side]
        for dy in range(3):
            acc = acc + mm(wide_field(hs_own, 3 * side, dy, 8, 32), b.wa[6 * side + dy])
        b.la[side] = acc
    hid_copies = spread(S.hid, b.hs, some(3, 8))
    level_a = []
    for p in range(2):
        value = b.fv[p].astype(f32).reshape(256, 128) + scale[0] * b.la[p]
        b.la[p] = value
        level_a.append(value)
    pooled = (pool_yz(level_a[0] + level_a[1], 8, 32, b.pool_s) * 0.125).astype(bf16)
    loads.l1.wait()
    lb = mm(pooled, b.l1[...]).astype(bf16).astype(f32)

    hidden_b = silu(lb)
    b.hb_own[...] = hidden_b.astype(bf16)
    halo_b_copies = [
        send(S.halo_b, 0, b.hb_own, b.halo_b.at[0], nxt),
        send(S.halo_b, 1, b.hb_own, b.halo_b.at[1], prv),
    ]

    def put_b(plane, h):
        put(hsb_own, plane, h, 4, 16)

    put_b(1, hidden_b)

    arrived(bz_copies)
    for k in range(4):
        both = b.bz_buf[2 * k].astype(f32) + b.bz_buf[2 * k + 1].astype(f32)
        b.ge[1 + 4 * x + k] = both.astype(bf16)
    own_ge = b.ge.at[pl.ds(1 + 4 * x, 4)]
    bx_copies = [send(S.bx, k - 1, own_ge, own_ge, dev(dx=x_of[k])) for k in range(1, NXC)]

    def taps_b(acc, dx):
        for dy in range(3):
            acc = acc + mm(wide_field(hsb_own, dx, dy, 4, 16), b.wb[3 * dx + dy])
        return acc

    lax.fori_loop(1, 8, lambda k, carry: clear(lax.rem(q + k, 8), carry), 0)
    loads.wb.wait()
    acc_b = taps_b(jnp.zeros((64, 128), f32), 1)
    for side in (near, 1 - near):
        inside = side_in(S.halo_b, b.halo_b, side)
        put_b(2 * side, b.halo_b[side].astype(f32) * inside)
        for dy in range(3):
            acc_b = acc_b + mm(wide_field(hsb_own, 2 * side, dy, 4, 16), b.wb[6 * side + dy])
    level_b = lb + scale[1] * acc_b
    b.fz_buf[z] = (pool_yz(level_b, 4, 16, b.small_s) * 0.25).astype(bf16)
    fz_copies = [
        send(S.fz, k - 1, b.fz_buf.at[z], b.fz_buf.at[z], dev(dz=z_of[k]))
        for k in range(1, NZL)
    ]

    for k in range(3):
        for p in range(3):
            b.gbs[k, p, 0] = jnp.zeros((16, 128), bf16)
            b.gbs[k, p, 5] = jnp.zeros((16, 128), bf16)
    for load in (loads.w2, loads.wc, loads.l2):
        load.wait()
    arrived(bx_copies)
    grad_e2 = b.ge[1:17].reshape(256, 128)
    own_rows = b.w2[pl.ds(pl.multiple_of(g * 16, 16), 16), :]
    grad_t = mm(own_rows, grad_e2, NT).astype(bf16).astype(f32)
    lane = lax.broadcasted_iota(jnp.int32, (16, 256), 1)
    pos_p, pos_y, pos_z = lane // 16, (lane // 8) % 2, lane % 8

    def moved(v, pos, length, step, d):
        if d == 0:
            return v
        ok = (pos + d >= 0) & (pos + d < length)
        return jnp.where(ok, pltpu.roll(v, (-d * step) % 256, 1), 0.0)

    for dx in range(3):
        vx = moved(grad_t, pos_p, 16, 16, 1 - dx)
        for dy in range(3):
            vy = moved(vx, pos_y, 2, 8, 1 - dy)
            for dz in range(3):
                tap = 9 * dx + 3 * dy + dz
                b.st[16 * tap : 16 * tap + 16, :] = moved(vy, pos_z, 8, 1, 1 - dz).astype(bf16)
    b.st[432:448, :] = jnp.zeros((16, 256), bf16)
    back_part = mm(b.st[0:432, :], b.wc[...], TN)
    start = z // 2 + z % 2
    two_e2 = b.ge[pl.ds(4 * x + start, 2)].reshape(32, 128)
    two_c = mm(two_e2, b.w2[...], NT).astype(bf16)
    two_m2 = mm(two_c, b.l2[...], NT)

    arrived(fz_copies)
    for k in range(4):
        both = b.fz_buf[2 * k].astype(f32) + b.fz_buf[2 * k + 1].astype(f32)
        b.fx_buf[x, k] = (both * 0.5).astype(bf16)
    fx_copies = [
        send(S.fx, k - 1, b.fx_buf.at[x], b.fx_buf.at[x], dev(dx=x_of[k]))
        for k in range(1, NXC)
    ]
    hb_copies = to_group(S.hb, b.hsb, some(2, 4))
    cot_forward = forward(S.cot_f, b.cq, cot_sems)
    arrived(fx_copies)
    pooled_two = b.fx_buf[...].reshape(256, 128)
    lc_b = mm(pooled_two, b.l2[...]).astype(bf16)
    lc = lc_b.astype(f32)
    sig = jax.nn.sigmoid(lc)
    hidden_c = (lc * sig).astype(bf16)
    weighted = (scale[2] * (sig * (1.0 + lc * (1.0 - sig))) * back_part).astype(bf16)
    b.mp[1:17] = mm(weighted, b.l2[...], NT).astype(bf16).reshape(16, 16, 128)
    rxb_copies = [
        send(S.rxb, k - 1, b.mp.at[pl.ds(4 * x_of[k], 6)], b.rxb.at[k - 1], dev(dx=x_of[k]))
        for k in range(1, NXC)
    ]
    taps = mm(b.wc[...], hidden_c, NT).reshape(9, 3, 16, 256)

    def folded(v, pos, length, step):
        total = v[:, 1]
        for d in (-1, 1):
            ok = (pos + d >= 0) & (pos + d < length)
            piece = v[:, 1 + d]
            turned = pltpu.roll(piece.reshape(-1, 256), (-d * step) % 256, 1)
            total = total + jnp.where(ok[None], turned.reshape(piece.shape), 0.0)
        return total

    conv_t = folded(taps, pos_z, 8, 1).reshape(3, 3, 16, 256)
    conv_t = folded(conv_t, pos_y, 2, 8).reshape(1, 3, 16, 256)
    conv_t = folded(conv_t, pos_p, 16, 16).reshape(16, 256)
    row16 = lax.broadcasted_iota(jnp.int32, (16, 512), 0)
    lane16 = lax.broadcasted_iota(jnp.int32, (16, 512), 1)
    pick = (lane16 == row16 + g * 16).astype(f32).astype(bf16)
    own_lc = mm(pick, lc_b, NT)
    level_c = (own_lc + scale[2] * conv_t).astype(bf16)
    b.up[...] = mm(level_c, own_rows, TN).astype(bf16).reshape(16, 16, 128)
    rxf_copies = [
        send(S.rxf, k - 1, b.up.at[pl.ds(4 * x_of[k], 4)], b.rxf.at[k - 1], dev(dx=x_of[k]))
        for k in range(1, NXC)
    ]

    arrived(rxb_copies)
    both = b.mp[pl.ds(4 * x, 6)].astype(f32)
    for k in range(3):
        both = both + b.rxb[k].astype(f32)
    b.sb[...] = both.astype(bf16)
    rzb_copies = []
    for k in range(1, NZL):
        first = z_of[k] // 2 + z_of[k] % 2
        rzb_copies.append(
            send(S.rzb, k - 1, b.sb.at[pl.ds(first, 2)], b.rzb.at[k - 1], dev(dz=z_of[k]))
        )
    grad_w = (scale[2] * mm(b.st[...], hidden_c)).astype(bf16)
    for cc in range(2):
        for yy in range(NY):
            b.dc[cc, yy] = grad_w[224 * cc : 224 * cc + 224, 128 * yy : 128 * yy + 128]
    hid_forward = forward(S.hid_f, b.hs, hid_sems, some(3, 8))
    c_core = send(S.c_core, 0, b.dc.at[1 - core], b.c_cr, sibling)

    def shifted(work):
        for shift, used in ((0, share <= 2), (2, share >= 4)):
            pl.when(used)(lambda: work((shift,)))

    def prepare(slots):
        def work(shifts):
            for slot in slots:

                def one(p, carry):
                    field = b.hs[slot, 1, p, 1:9].astype(f32).reshape(256, 128)
                    put(b.hs.at[slot], p, field, 8, 32, shifts)
                    return carry

                lax.fori_loop(y // 2, y // 2 + 3, one, 0)

        shifted(work)

    hid_copies[0].wait_recv()
    prepare([y * 2 + 1 - core] + [y_of[k] * 2 + core for k in range(1, NY)])

    c_core.wait_recv()
    for yy in range(NY):
        b.c_ys[yy] = (b.dc[core, yy].astype(f32) + b.c_cr[yy].astype(f32)).astype(bf16)
    c_y = [
        send(S.c_y, k - 1, b.c_ys.at[y_of[k]], b.c_yr.at[k - 1], dev(dy=y_of[k]))
        for k in range(1, NY)
    ]

    arrived(rzb_copies)
    both = b.sb[pl.ds(start, 2)].astype(f32)
    for k in range(7):
        both = both + b.rzb[k].astype(f32)
    two_m2 = (two_m2.reshape(2, 16, 128) + both).astype(bf16).astype(f32)
    even = (z % 2 == 0).astype(f32)
    lo, hi = two_m2[0], two_m2[1]
    own_m2 = hi * even + lo * (1.0 - even)
    arrived(halo_d_copies)

    def grad_plane(field, m2):
        return (field.astype(f32) + grow_yz(m2, 2, 8, b.small_s) * 0.125).astype(bf16)

    grad_b = grad_plane(b.gd_own[...], own_m2)
    grad_b32 = grad_b.astype(f32)
    b.gbq[q] = (grad_b32 * flag[1]).astype(bf16)
    gb_copies = to_group(S.gb, b.gbq)
    put(b.gbs, 1, grad_b32, 4, 16)
    put(b.gbs, 0, grad_plane(b.halo_d[0], lo).astype(f32) * has_prev, 4, 16)
    put(b.gbs, 2, grad_plane(b.halo_d[1], hi).astype(f32) * has_next, 4, 16)
    back_b = jnp.zeros((64, 128), f32)
    for t in range(9):
        dx, dy = t // 3, t % 3
        for dz in range(3):
            part = b.gbs[2 - dz, 2 - dx, 2 - dy : 6 - dy].reshape(64, 128)
            back_b = back_b + mm(part, b.wb[t, 128 * dz : 128 * dz + 128, :], NT)
    grad_p = (grad_b32 + scale[1] * slope(lb) * back_b).astype(bf16)
    grad_m1 = mm(grad_p, b.l1[...], NT).astype(bf16).astype(f32)
    b.m1q[q] = (grad_m1 * flag[0]).astype(bf16)
    m1_copies = to_group(S.m1, b.m1q)
    early = len(started)

    arrived(hb_copies)

    def prepare_b(shifts):
        for k in range(1, 8):
            slot = group_of[k][0] * 2 + group_of[k][1]
            for p in range(2):
                plane = y // 2 + p
                field = b.hsb[slot, 1, plane, 1:5].astype(f32).reshape(64, 128)
                put(b.hsb.at[slot], plane, field, 4, 16, shifts)

    shifted(prepare_b)
    arrived(hid_forward)
    prepare([y_from[k] * 2 + 1 - core for k in range(1, NY)])
    arrived(c_y)
    total = b.c_ys[y].astype(f32)
    for k in range(3):
        total = total + b.c_yr[k].astype(f32)
    b.c_zs[...] = total.astype(bf16)
    c_zh = send(S.c_zh, 0, b.c_zs, b.c_zr, dev(dzh=1 - zh))
    arrived(gb_copies)
    where = []
    for i in range(4):
        place = jnp.minimum(4 * share + i, 26)
        dz, e = place // 9, place % 9
        odd = dz % 2
        e = e * (1 - odd) + (8 - e) * odd
        where.append((e // 3, e % 3, dz))

    def keep_sum(kind, i, value):
        for k in range(NXC):
            b.xs[kind, k, i] = value[32 * k : 32 * k + 32].astype(bf16)

    stores = []

    def along_x(kind):
        return [
            send(
                KINDS[kind][0],
                k - 1,
                b.xs.at[kind, x_of[k]],
                b.xr.at[kind, k - 1],
                dev(dx=x_of[k]),
            )
            for k in range(1, NXC)
        ]

    source = ((row // 4) % 4) * 32 + (row // 16) * 4 + row % 4
    shuffle = (col == source).astype(f32).astype(bf16)

    def along_z(kind):
        total = b.xs[kind, x].astype(f32)
        for k in range(3):
            total = total + b.xr[kind, k].astype(f32)
        pieces = mm(shuffle, total.astype(bf16).reshape(128, 128)).astype(bf16)
        b.zs[kind] = pieces.reshape(8, 16, 128)
        copies = []
        for k in sorted(range(1, NZ), key=lambda k: abs(k - NZ // 2)):
            target = dev(dzh=z16_of[k] // NZL, dz=z16_of[k] % NZL)
            src = b.zs.at[kind, z16_of[k] % NZL]
            copies.append(send(KINDS[kind][1], k - 1, src, b.zr.at[kind, z16], target))
        b.zr[kind, z16] = b.zs[kind, z]
        return copies

    def to_all(kind):
        total = b.zr[kind, 0].astype(f32)
        for k in range(1, NZ):
            total = total + b.zr[kind, k].astype(f32)
        b.zt[kind] = total
        own = (fga, fgb)[kind].at[q]
        copies = [
            send(KINDS[kind][2], k - 1, b.zt.at[kind], own, group_dev[k]) for k in range(1, 8)
        ]
        stores.append(pltpu.make_async_copy(b.zt.at[kind], own, local_sem.at[11 + kind]))
        stores[-1].start()
        return copies

    turned_b = mm(unit, b.gbq[...].reshape(512, 128), NT).astype(bf16)
    for i, (dx, dy, dz) in enumerate(where):
        field = b.hsb[:, dz, dx, pl.ds(dy, 4)].reshape(512, 128)
        keep_sum(1, i, mm(turned_b, field) * f32(1.0 / SURVIVAL[1]))
    b_x = along_x(1)
    cot_copies[0].wait_recv()
    arrived(cot_forward)

    coarse = lax.broadcasted_iota(jnp.int32, (64, 512), 0)
    fine = lax.broadcasted_iota(jnp.int32, (64, 512), 1)
    above = ((fine // 64) % 4) * 16 + (fine % 32) // 2
    grow = jnp.where(coarse == above, 0.125, 0.0).astype(bf16)
    for k in (0, 1, 2, 3, 6, 7, 4, 5):
        if k:
            m1_copies[k - 1].wait_recv()
        j = y_from[k // 2] * 2 + (core + k) % 2
        b.gt[j] = (b.cq[j].astype(f32) + mm(b.m1q[j], grow, TN)).astype(bf16)
    for pair in range(2):
        acc = jnp.zeros((128, 256), f32)
        for j in range(8):
            pieces = []
            for i in (2 * pair, 2 * pair + 1):
                dx, dy, dz = where[i]
                pieces.append(b.hs[j, dz, pl.ds(dx, 2), pl.ds(dy, 8)].reshape(512, 128))
            acc = acc + mm(b.gt[j], jnp.concatenate(pieces, axis=1))
        acc = acc * f32(1.0 / SURVIVAL[0])
        keep_sum(0, 2 * pair, acc[:, 0:128])
        keep_sum(0, 2 * pair + 1, acc[:, 128:256])
    a_x = along_x(0)

    arrived(b_x)
    b_z = along_z(1)
    arrived(a_x)
    a_z = along_z(0)
    arrived(rxf_copies)
    both = b.up[pl.ds(4 * x, 4)].astype(f32)
    for k in range(3):
        both = both + b.rxf[k].astype(f32)
    b.sf[...] = both.astype(bf16)
    rzf_copies = [
        send(S.rzf, k - 1, b.sf.at[z_of[k] // 2], b.rzf.at[k - 1], dev(dz=z_of[k]))
        for k in range(1, NZL)
    ]

    c_zh.wait_recv()
    b.fc[y] = (b.c_zs[...].astype(f32) + b.c_zr[...].astype(f32)).astype(bf16)
    own_c = b.fc.at[y]
    c_ay = [send(S.c_ay, k - 1, own_c, own_c, dev(dy=y_of[k])) for k in range(1, NY)]
    arrived(b_z)
    b_all = to_all(1)
    finish(early)

    arrived(a_z)
    a_all = to_all(0)
    arrived(c_ay)
    stores.append(pltpu.make_async_copy(b.fc, fgc.at[core], local_sem.at[13]))
    stores[-1].start()
    c_ac = send(S.c_ac, 0, b.fc, fgc.at[core], sibling)
    arrived(rzf_copies)
    both = b.sf[z // 2].astype(f32)
    for k in range(7):
        both = both + b.rzf[k].astype(f32)
    level_d = (level_b + grow_yz(both, 2, 8, b.small_s)).astype(bf16)
    wide = grow_yz(mm(level_d, b.w1[...]), 4, 16, b.grow_s)
    for p in range(2):
        b.rv[p] = (b.la[p] + wide).astype(bf16).reshape(8, 32, 128)
    stores.append(pltpu.make_async_copy(b.rv, res.at[0], local_sem.at[10]))
    stores[-1].start()
    arrived(b_all)
    finish(len(started) - 8)
    c_ac.wait_recv()
    for copy in stores:
        copy.wait()
    arrived(a_all)
    finish(len(started))


OWNER = (0, 6, 4, 1, 2, 3, 5, 7)


def finalize(
    res, fga, fgb, fgc, out, out_a, out_b, out_c, res_v, fg_v, fgc_v, tables, wide, sems
):
    parts = [
        pltpu.make_async_copy(fgc.at[part], fgc_v.at[part], sems.at[part]) for part in range(2)
    ]
    loads = [
        pltpu.make_async_copy(res, res_v, sems.at[2]),
        pltpu.make_async_copy(fga, fg_v.at[0], sems.at[3]),
        pltpu.make_async_copy(fgb, fg_v.at[1], sems.at[4]),
    ]
    for load in parts + loads:
        load.start()
    copies = []

    def store(src, dst):
        copies.append(pltpu.make_async_copy(src, dst, sems.at[5 + len(copies)]))
        copies[-1].start()

    for part in range(2):
        parts[part].wait()
        rows = pl.ds(224 * part, 224 - 16 * part)
        for yy in range(NY):
            wide[rows, 128 * yy : 128 * yy + 128] = fgc_v[part, yy, 0 : 224 - 16 * part].astype(f32)
        store(wide.at[rows], out_c.at[rows])
        if part == 0:
            loads[0].wait()
            store(res_v, out)
    for kind, target in enumerate((out_a, out_b)):
        loads[1 + kind].wait()
        for t in range(27):
            e, dz = t // 3, t % 3
            place = 9 * dz + (8 - e if dz == 1 else e)
            first = 4 * (place % 4)
            tables[kind, t] = fg_v[kind, OWNER[place // 4], first : first + 4]
        store(tables.at[kind], target)
    for copy in copies:
        copy.wait()


def body(
    features,
    cotangent,
    keep_flags,
    conv_a,
    conv_b,
    conv_c,
    lift_one,
    lift_two,
    lower_two,
    lower_one,
):
    hbm = pl.BlockSpec(memory_space=pltpu.HBM)
    result, fga, fgb, fgc = pl.pallas_call(
        kernel,
        out_shape=(
            jax.ShapeDtypeStruct(features.shape, bf16),
            jax.ShapeDtypeStruct((8, 16, 128), f32),
            jax.ShapeDtypeStruct((8, 16, 128), f32),
            jax.ShapeDtypeStruct((2, NY, 224, 128), bf16),
        ),
        in_specs=[hbm] * 10,
        out_specs=(hbm,) * 4,
        scratch_shapes=[pltpu.VMEM(shape, dtype) for shape, dtype in SCRATCH.values()]
        + [
            pltpu.SemaphoreType.DMA((14,)),
            pltpu.SemaphoreType.DMA((TOTAL,)),
            pltpu.SemaphoreType.DMA((TOTAL,)),
        ],
        compiler_params=pltpu.CompilerParams(
            collective_id=0, has_side_effects=True, vmem_limit_bytes=60 * 1024 * 1024
        ),
        cost_estimate=pl.CostEstimate(
            flops=1_400_000_000, bytes_accessed=5_000_000, transcendentals=600_000
        ),
    )(
        features,
        cotangent,
        keep_flags,
        conv_a.reshape(9, 384, 128),
        conv_b.reshape(9, 384, 128),
        conv_c.transpose(0, 2, 1).reshape(432, 512),
        lift_one,
        lift_two,
        lower_two,
        lower_one,
    )

    result, grad_a, grad_b, grad_c = pl.pallas_call(
        finalize,
        out_shape=(
            jax.ShapeDtypeStruct(features.shape, bf16),
            jax.ShapeDtypeStruct((27, 4, 128), f32),
            jax.ShapeDtypeStruct((27, 4, 128), f32),
            jax.ShapeDtypeStruct((432, 512), f32),
        ),
        in_specs=[hbm] * 4,
        out_specs=(hbm,) * 4,
        scratch_shapes=[
            pltpu.VMEM(features.shape, bf16),
            pltpu.VMEM((2, 8, 16, 128), f32),
            pltpu.VMEM((2, NY, 224, 128), bf16),
            pltpu.VMEM((2, 27, 4, 128), f32),
            pltpu.VMEM((432, 512), f32),
            pltpu.SemaphoreType.DMA((10,)),
        ],
        compiler_params=pltpu.CompilerParams(vmem_limit_bytes=60 * 1024 * 1024),
    )(result, fga, fgb, fgc)
    return (
        result,
        grad_a.transpose(0, 2, 1),
        grad_b.transpose(0, 2, 1),
        grad_c.reshape(27, 16, 512).transpose(0, 2, 1),
    )


def solution(mesh):
    return jax.shard_map(
        body,
        mesh=mesh,
        in_specs=(
            P("member", "gx", None, None, None),
            P("member", "gx", None, None, None),
            P("member", None),
            P(),
            P(),
            P(None, None, "gx"),
            P(),
            P(),
            P(),
            P(),
        ),
        out_specs=(
            P("member", "gx", None, None, None),
            P(None, None, "gx"),
            P(None, None, "gx"),
            P(None, None, "gx"),
        ),
        check_vma=False,
    )
```

```python
import jax
import jax.numpy as jnp
from jax import lax
from jax.experimental import pallas as pl
from jax.experimental.pallas import tpu as pltpu
from jax.sharding import PartitionSpec as P

f32 = jnp.float32
bf16 = jnp.bfloat16
MESH = pl.DeviceIdType.MESH

NY, NZH, NCORE, NXC, NZL = 4, 2, 2, 4, 8
NZ = NZH * NZL
SURVIVAL = (0.9, 0.8, 0.7)

COPIES = dict(
    halo_a=2,
    halo_b=2,
    halo_d=2,
    bz=7,
    bx=3,
    fz=7,
    fx=3,
    cot=4,
    cot_f=3,
    hid=4,
    hid_f=3,
    hb=7,
    gb=7,
    m1=7,
    rxb=3,
    rxf=3,
    rzb=7,
    rzf=7,
    a_x=3,
    a_z=15,
    a_all=7,
    b_x=3,
    b_z=15,
    b_all=7,
    c_core=1,
    c_y=3,
    c_zh=1,
    c_ay=3,
    c_ac=1,
)


class S:
    pass


TOTAL = 0
for _name, _count in COPIES.items():
    setattr(S, _name, TOTAL)
    TOTAL += _count
KINDS = ((S.a_x, S.a_z, S.a_all), (S.b_x, S.b_z, S.b_all))

NN = (((1,), (0,)), ((), ()))
NT = (((1,), (1,)), ((), ()))
TN = (((0,), (0,)), ((), ()))


def mm(a, b, dims=NN):
    return lax.dot_general(a, b, dims, preferred_element_type=f32)


def silu(v):
    return v * jax.nn.sigmoid(v)


def slope(v):
    s = jax.nn.sigmoid(v)
    return s * (1.0 + v * (1.0 - s))


SCRATCH = dict(
    fv=((2, 8, 32, 128), bf16),
    cv=((2, 8, 32, 128), bf16),
    kv=((1, 3), jnp.int32),
    wa=((9, 384, 128), bf16),
    wb=((9, 384, 128), bf16),
    wc=((432, 512), bf16),
    l1=((128, 128), bf16),
    l2=((128, 512), bf16),
    w2=((512, 128), bf16),
    w1=((128, 128), bf16),
    rv=((2, 8, 32, 128), bf16),
    halo_a=((2, 8, 32, 128), bf16),
    hs=((8, 3, 4, 10, 32, 128), bf16),
    la=((2, 256, 128), f32),
    pool_s=((128, 128), f32),
    grow_s=((128, 128), f32),
    hb_own=((64, 128), bf16),
    halo_b=((2, 64, 128), bf16),
    hsb=((8, 3, 3, 6, 16, 128), bf16),
    small_s=((32, 128), f32),
    gd_own=((64, 128), bf16),
    halo_d=((2, 64, 128), bf16),
    bz_buf=((8, 16, 128), bf16),
    ge=((18, 16, 128), bf16),
    fz_buf=((8, 16, 128), bf16),
    fx_buf=((4, 4, 16, 128), bf16),
    st=((448, 256), bf16),
    mp=((18, 16, 128), bf16),
    up=((16, 16, 128), bf16),
    rxb=((3, 6, 16, 128), bf16),
    rxf=((3, 4, 16, 128), bf16),
    sb=((6, 16, 128), bf16),
    sf=((4, 16, 128), bf16),
    rzb=((7, 2, 16, 128), bf16),
    rzf=((7, 16, 128), bf16),
    gbs=((3, 3, 6, 16, 128), bf16),
    cq=((8, 128, 512), bf16),
    gbq=((8, 64, 128), bf16),
    m1q=((8, 64, 128), bf16),
    gt=((8, 128, 512), bf16),
    xs=((2, 4, 4, 32, 128), bf16),
    xr=((2, 3, 4, 32, 128), bf16),
    zs=((2, 8, 16, 128), bf16),
    zr=((2, 16, 16, 128), bf16),
    zt=((2, 16, 128), f32),
    fc=((4, 224, 128), bf16),
    dc=((2, 4, 224, 128), bf16),
    c_cr=((4, 224, 128), bf16),
    c_ys=((4, 224, 128), bf16),
    c_yr=((3, 224, 128), bf16),
    c_zs=((224, 128), bf16),
    c_zr=((224, 128), bf16),
)


class Bufs:
    pass


def kernel(
    feat_h,
    cot_h,
    keep_h,
    wa_h,
    wb_h,
    wc_h,
    l1_h,
    l2_h,
    w2_h,
    w1_h,
    res,
    fga,
    fgb,
    fgc,
    *scratch,
):
    b = Bufs()
    for name, ref in zip(SCRATCH, scratch):
        setattr(b, name, ref)
    local_sem, send_sem, recv_sem = scratch[len(SCRATCH) :]

    m = lax.axis_index("member")
    g = lax.axis_index("gx")
    x, z = g // NZL, g % NZL
    core, zh, y = m % NCORE, (m // NCORE) % NZH, m // (NCORE * NZH)
    z16 = zh * NZL + z
    q = y * 2 + core

    def chosen(*values):
        return sum((y == k).astype(jnp.int32) * value for k, value in enumerate(values))

    share = chosen(0, 4, 2, 1) * (1 - core) + chosen(3, 5, 6, 7) * core

    def dev(dy=None, dzh=None, dcore=None, dx=None, dz=None):
        yy = y if dy is None else dy
        hh = zh if dzh is None else dzh
        cc = core if dcore is None else dcore
        xx = x if dx is None else dx
        zz = z if dz is None else dz
        return ((yy * NZH + hh) * NCORE + cc, xx * NZL + zz)

    nxt = (m, (g + 1) % (NXC * NZL))
    prv = (m, (g + NXC * NZL - 1) % (NXC * NZL))
    x_of = [(x + k) % NXC for k in range(NXC)]
    z_of = [(z + k) % NZL for k in range(NZL)]
    y_of = [(y + k) % NY for k in range(NY)]
    y_from = [(y + NY - k) % NY for k in range(NY)]
    z16_of = [(z16 + k) % NZ for k in range(NZ)]
    group_of = [(y_of[k // 2], (core + k) % 2) for k in range(8)]
    group_dev = [dev(dy=yy, dcore=cc) for yy, cc in group_of]
    sibling = dev(dcore=1 - core)

    barrier = pltpu.get_barrier_semaphore()
    targets = [prv, nxt]
    targets += [dev(dx=x_of[k]) for k in range(1, NXC)]
    targets += [dev(dzh=z16_of[k] // NZL, dz=z16_of[k] % NZL) for k in range(1, NZ)]
    targets += group_dev[1:]
    for target in targets:
        pl.semaphore_signal(barrier, inc=1, device_id=target, device_id_type=MESH)

    started = []

    def finish(count):
        for copy in started[:count]:
            copy.wait_send()
        del started[:count]

    def send(name, k, src, dst, target):
        index = name + k
        copy = pltpu.make_async_remote_copy(
            src_ref=src,
            dst_ref=dst,
            send_sem=send_sem.at[index],
            recv_sem=recv_sem.at[index],
            device_id=target,
            device_id_type=MESH,
        )
        copy.start()
        started.append(copy)
        return copy

    def arrived(copies):
        for copy in copies:
            copy.wait_recv()

    loads = Bufs()

    def load_all(first, **sources):
        for k, (name, src) in enumerate(sources.items()):
            load = pltpu.make_async_copy(src, getattr(b, name), local_sem.at[first + k])
            load.start()
            setattr(loads, name, load)

    load_all(0, fv=feat_h.at[0], wa=wa_h)
    pl.semaphore_wait(barrier, len(targets))
    halo_a_copies = [
        send(S.halo_a, 0, feat_h.at[0, 1], b.halo_a.at[0], nxt),
        send(S.halo_a, 1, feat_h.at[0, 0], b.halo_a.at[1], prv),
    ]
    load_all(2, cv=cot_h.at[0], w1=w1_h, kv=keep_h, l1=l1_h, wb=wb_h, w2=w2_h, wc=wc_h, l2=l2_h)

    has_prev = (g > 0).astype(f32)
    has_next = (g < NXC * NZL - 1).astype(f32)

    def z_shifts(h, length):
        rows = h.shape[0]
        pos = lax.broadcasted_iota(jnp.int32, h.shape, 0) % length
        before = jnp.where(pos == 0, 0.0, pltpu.roll(h, 1, 0))
        after = jnp.where(pos == length - 1, 0.0, pltpu.roll(h, rows - 1, 0))
        return before, h, after

    def put(cat, plane, h, grid_y, grid_z, shifts=(0, 1, 2)):
        pieces = z_shifts(h, grid_z)
        for k in shifts:
            piece = pieces[k].astype(bf16)
            cat[k, plane, 1 : 1 + grid_y] = piece.reshape(grid_y, grid_z, 128)

    def pool_yz(v, grid_y, grid_z, scratch_ref):
        half = v.reshape(grid_y // 2, 2, grid_z, 128).sum(axis=1)
        n = grid_y // 2 * grid_z
        scratch_ref[0:n, :] = half.reshape(n, 128)
        even = scratch_ref[pl.ds(0, n // 2, stride=2), :]
        return even + scratch_ref[pl.ds(1, n // 2, stride=2), :]

    def grow_yz(v, grid_y, grid_z, scratch_ref):
        n = grid_y * grid_z
        scratch_ref[pl.ds(0, n, stride=2), :] = v
        scratch_ref[pl.ds(1, n, stride=2), :] = v
        wide = scratch_ref[0 : 2 * n, :].reshape(grid_y, 1, 2 * grid_z, 128)
        return jnp.broadcast_to(wide, (grid_y, 2, 2 * grid_z, 128)).reshape(4 * n, 128)

    def wide_field(cat, plane, first, grid_y, grid_z, turned=False):
        order = (2, 1, 0) if turned else (0, 1, 2)
        pieces = [
            cat[k, plane, first : first + grid_y].reshape(grid_y * grid_z, 128) for k in order
        ]
        return jnp.concatenate(pieces, axis=1)

    row = lax.broadcasted_iota(jnp.int32, (128, 128), 0)
    col = lax.broadcasted_iota(jnp.int32, (128, 128), 1)
    unit = (row == col).astype(f32).astype(bf16)

    def clear(i, carry):
        for k in range(3):
            for p in range(4):
                b.hs[i, k, p, 0] = jnp.zeros((32, 128), bf16)
                b.hs[i, k, p, 9] = jnp.zeros((32, 128), bf16)
            for p in range(3):
                b.hsb[i, k, p, 0] = jnp.zeros((16, 128), bf16)
                b.hsb[i, k, p, 5] = jnp.zeros((16, 128), bf16)
        return carry

    clear(q, 0)
    for ref in (b.ge, b.mp):
        ref[0] = jnp.zeros((16, 128), bf16)
        ref[17] = jnp.zeros((16, 128), bf16)

    hs_own = b.hs.at[q]
    hsb_own = b.hsb.at[q]

    def put_a(plane, h):
        put(hs_own, plane, h, 8, 32)

    loads.fv.wait()
    for p in range(2):
        put_a(1 + p, silu(b.fv[p].astype(f32).reshape(256, 128)))

    def taps_a(acc, p, dx):
        for dy in range(3):
            acc = acc + mm(wide_field(hs_own, p + dx, dy, 8, 32), b.wa[3 * dx + dy])
        return acc

    loads.wa.wait()
    acc_a = [jnp.zeros((256, 128), f32), jnp.zeros((256, 128), f32)]
    acc_a[0] = taps_a(taps_a(acc_a[0], 0, 1), 0, 2)
    acc_a[1] = taps_a(taps_a(acc_a[1], 1, 1), 1, 0)
    for p in range(2):
        b.la[p] = acc_a[p]

    loads.cv.wait()
    loads.w1.wait()
    loads.kv.wait()
    flags = b.kv[...].astype(f32)
    flag = [flags[0:1, j : j + 1] for j in range(3)]
    scale = [flag[j] * f32(1.0 / SURVIVAL[j]) for j in range(3)]
    up32 = [b.cv[p].astype(f32).reshape(256, 128) for p in range(2)]
    grad_e1 = pool_yz(up32[0] + up32[1], 8, 32, b.pool_s).astype(bf16)
    grad_d = mm(grad_e1, b.w1[...], NT).astype(bf16)
    b.gd_own[...] = grad_d
    b.bz_buf[z] = pool_yz(grad_d.astype(f32), 4, 16, b.small_s).astype(bf16)
    bz_copies = [
        send(S.bz, k - 1, b.bz_buf.at[z], b.bz_buf.at[z], dev(dz=z_of[k]))
        for k in range(1, NZL)
    ]
    halo_d_copies = [
        send(S.halo_d, 0, b.gd_own, b.halo_d.at[0], nxt),
        send(S.halo_d, 1, b.gd_own, b.halo_d.at[1], prv),
    ]
    for p in range(2):
        turned = mm(unit, (up32[p] * flag[0]).astype(bf16), NT).astype(bf16)
        b.cq[q, :, 256 * p : 256 * p + 256] = turned
    peers = [sibling] + [dev(dy=y_of[k]) for k in range(1, NY)]

    def whole(ref, slot, to_y):
        return ref.at[slot]

    def some(count, grid_y):
        return lambda ref, slot, to_y: ref.at[slot, 1, pl.ds(to_y // 2, count), pl.ds(1, grid_y)]

    def spread(name, ref, part=whole):
        result = []
        for k in range(4):
            piece = part(ref, q, y_of[k])
            result.append(send(name, k, piece, piece, peers[k]))
        return result

    def forward(name, ref, copies, part=whole):
        result = []
        for k in range(1, NY):
            piece = part(ref, y_from[k] * 2 + core, y)
            pltpu.make_async_remote_copy(
                src_ref=piece,
                dst_ref=piece,
                send_sem=send_sem.at[0],
                recv_sem=recv_sem.at[copies[k]],
                device_id=sibling,
                device_id_type=MESH,
            ).wait_recv()
            result.append(send(name, k - 1, piece, piece, sibling))
        return result

    def to_group(name, ref, part=whole):
        result = {}
        for k in (4, 5, 2, 3, 6, 7, 1):
            piece = part(ref, q, group_of[k][0])
            result[k - 1] = send(name, k - 1, piece, piece, group_dev[k])
        return [result[k] for k in range(7)]

    cot_copies = spread(S.cot, b.cq)
    cot_sems = [S.cot + k for k in range(4)]
    hid_sems = [S.hid + k for k in range(4)]

    near = (z == 0).astype(jnp.int32)

    def side_in(name, ref, side):
        pltpu.make_async_remote_copy(
            src_ref=ref.at[side],
            dst_ref=ref.at[side],
            send_sem=send_sem.at[name],
            recv_sem=recv_sem.at[name + side],
            device_id=nxt,
            device_id_type=MESH,
        ).wait_recv()
        return jnp.where(side == 0, has_prev, has_next)

    for side in (near, 1 - near):
        inside = side_in(S.halo_a, b.halo_a, side)
        put_a(3 * side, silu(b.halo_a[side].astype(f32).reshape(256, 128)) * inside)
        acc = b.la[side]
        for dy in range(3):
            acc = acc + mm(wide_field(hs_own, 3 * side, dy, 8, 32), b.wa[6 * side + dy])
        b.la[side] = acc
    hid_copies = spread(S.hid, b.hs, some(3, 8))
    level_a = []
    for p in range(2):
        value = b.fv[p].astype(f32).reshape(256, 128) + scale[0] * b.la[p]
        b.la[p] = value
        level_a.append(value)
    pooled = (pool_yz(level_a[0] + level_a[1], 8, 32, b.pool_s) * 0.125).astype(bf16)
    loads.l1.wait()
    lb = mm(pooled, b.l1[...]).astype(bf16).astype(f32)

    hidden_b = silu(lb)
    b.hb_own[...] = hidden_b.astype(bf16)
    halo_b_copies = [
        send(S.halo_b, 0, b.hb_own, b.halo_b.at[0], nxt),
        send(S.halo_b, 1, b.hb_own, b.halo_b.at[1], prv),
    ]

    def put_b(plane, h):
        put(hsb_own, plane, h, 4, 16)

    put_b(1, hidden_b)

    arrived(bz_copies)
    for k in range(4):
        both = b.bz_buf[2 * k].astype(f32) + b.bz_buf[2 * k + 1].astype(f32)
        b.ge[1 + 4 * x + k] = both.astype(bf16)
    own_ge = b.ge.at[pl.ds(1 + 4 * x, 4)]
    bx_copies = [send(S.bx, k - 1, own_ge, own_ge, dev(dx=x_of[k])) for k in range(1, NXC)]

    def taps_b(acc, dx):
        for dy in range(3):
            acc = acc + mm(wide_field(hsb_own, dx, dy, 4, 16), b.wb[3 * dx + dy])
        return acc

    lax.fori_loop(1, 8, lambda k, carry: clear(lax.rem(q + k, 8), carry), 0)
    loads.wb.wait()
    acc_b = taps_b(jnp.zeros((64, 128), f32), 1)
    for side in (near, 1 - near):
        inside = side_in(S.halo_b, b.halo_b, side)
        put_b(2 * side, b.halo_b[side].astype(f32) * inside)
        for dy in range(3):
            acc_b = acc_b + mm(wide_field(hsb_own, 2 * side, dy, 4, 16), b.wb[6 * side + dy])
    level_b = lb + scale[1] * acc_b
    b.fz_buf[z] = (pool_yz(level_b, 4, 16, b.small_s) * 0.25).astype(bf16)
    fz_copies = [
        send(S.fz, k - 1, b.fz_buf.at[z], b.fz_buf.at[z], dev(dz=z_of[k]))
        for k in range(1, NZL)
    ]

    for k in range(3):
        for p in range(3):
            b.gbs[k, p, 0] = jnp.zeros((16, 128), bf16)
            b.gbs[k, p, 5] = jnp.zeros((16, 128), bf16)
    for load in (loads.w2, loads.wc, loads.l2):
        load.wait()
    arrived(bx_copies)
    grad_e2 = b.ge[1:17].reshape(256, 128)
    own_rows = b.w2[pl.ds(pl.multiple_of(g * 16, 16), 16), :]
    grad_t = mm(own_rows, grad_e2, NT).astype(bf16).astype(f32)
    lane = lax.broadcasted_iota(jnp.int32, (16, 256), 1)
    pos_p, pos_y, pos_z = lane // 16, (lane // 8) % 2, lane % 8

    def moved(v, pos, length, step, d):
        if d == 0:
            return v
        ok = (pos + d >= 0) & (pos + d < length)
        return jnp.where(ok, pltpu.roll(v, (-d * step) % 256, 1), 0.0)

    for dx in range(3):
        vx = moved(grad_t, pos_p, 16, 16, 1 - dx)
        for dy in range(3):
            vy = moved(vx, pos_y, 2, 8, 1 - dy)
            for dz in range(3):
                tap = 9 * dx + 3 * dy + dz
                b.st[16 * tap : 16 * tap + 16, :] = moved(vy, pos_z, 8, 1, 1 - dz).astype(bf16)
    b.st[432:448, :] = jnp.zeros((16, 256), bf16)
    back_part = mm(b.st[0:432, :], b.wc[...], TN)
    start = z // 2 + z % 2
    two_e2 = b.ge[pl.ds(4 * x + start, 2)].reshape(32, 128)
    two_c = mm(two_e2, b.w2[...], NT).astype(bf16)
    two_m2 = mm(two_c, b.l2[...], NT)

    arrived(fz_copies)
    for k in range(4):
        both = b.fz_buf[2 * k].astype(f32) + b.fz_buf[2 * k + 1].astype(f32)
        b.fx_buf[x, k] = (both * 0.5).astype(bf16)
    fx_copies = [
        send(S.fx, k - 1, b.fx_buf.at[x], b.fx_buf.at[x], dev(dx=x_of[k]))
        for k in range(1, NXC)
    ]
    hb_copies = to_group(S.hb, b.hsb, some(2, 4))
    cot_forward = forward(S.cot_f, b.cq, cot_sems)
    arrived(fx_copies)
    pooled_two = b.fx_buf[...].reshape(256, 128)
    lc_b = mm(pooled_two, b.l2[...]).astype(bf16)
    lc = lc_b.astype(f32)
    sig = jax.nn.sigmoid(lc)
    hidden_c = (lc * sig).astype(bf16)
    weighted = (scale[2] * (sig * (1.0 + lc * (1.0 - sig))) * back_part).astype(bf16)
    b.mp[1:17] = mm(weighted, b.l2[...], NT).astype(bf16).reshape(16, 16, 128)
    rxb_copies = [
        send(S.rxb, k - 1, b.mp.at[pl.ds(4 * x_of[k], 6)], b.rxb.at[k - 1], dev(dx=x_of[k]))
        for k in range(1, NXC)
    ]
    taps = mm(b.wc[...], hidden_c, NT).reshape(9, 3, 16, 256)

    def folded(v, pos, length, step):
        total = v[:, 1]
        for d in (-1, 1):
            ok = (pos + d >= 0) & (pos + d < length)
            piece = v[:, 1 + d]
            turned = pltpu.roll(piece.reshape(-1, 256), (-d * step) % 256, 1)
            total = total + jnp.where(ok[None], turned.reshape(piece.shape), 0.0)
        return total

    conv_t = folded(taps, pos_z, 8, 1).reshape(3, 3, 16, 256)
    conv_t = folded(conv_t, pos_y, 2, 8).reshape(1, 3, 16, 256)
    conv_t = folded(conv_t, pos_p, 16, 16).reshape(16, 256)
    row16 = lax.broadcasted_iota(jnp.int32, (16, 512), 0)
    lane16 = lax.broadcasted_iota(jnp.int32, (16, 512), 1)
    pick = (lane16 == row16 + g * 16).astype(f32).astype(bf16)
    own_lc = mm(pick, lc_b, NT)
    level_c = (own_lc + scale[2] * conv_t).astype(bf16)
    b.up[...] = mm(level_c, own_rows, TN).astype(bf16).reshape(16, 16, 128)
    rxf_copies = [
        send(S.rxf, k - 1, b.up.at[pl.ds(4 * x_of[k], 4)], b.rxf.at[k - 1], dev(dx=x_of[k]))
        for k in range(1, NXC)
    ]

    arrived(rxb_copies)
    both = b.mp[pl.ds(4 * x, 6)].astype(f32)
    for k in range(3):
        both = both + b.rxb[k].astype(f32)
    b.sb[...] = both.astype(bf16)
    rzb_copies = []
    for k in range(1, NZL):
        first = z_of[k] // 2 + z_of[k] % 2
        rzb_copies.append(
            send(S.rzb, k - 1, b.sb.at[pl.ds(first, 2)], b.rzb.at[k - 1], dev(dz=z_of[k]))
        )
    arrived(rxf_copies)
    both = b.up[pl.ds(4 * x, 4)].astype(f32)
    for k in range(3):
        both = both + b.rxf[k].astype(f32)
    b.sf[...] = both.astype(bf16)
    rzf_copies = [
        send(S.rzf, k - 1, b.sf.at[z_of[k] // 2], b.rzf.at[k - 1], dev(dz=z_of[k]))
        for k in range(1, NZL)
    ]

    grad_w = (scale[2] * mm(b.st[...], hidden_c)).astype(bf16)
    for cc in range(2):
        for yy in range(NY):
            b.dc[cc, yy] = grad_w[224 * cc : 224 * cc + 224, 128 * yy : 128 * yy + 128]
    hid_forward = forward(S.hid_f, b.hs, hid_sems, some(3, 8))
    c_core = send(S.c_core, 0, b.dc.at[1 - core], b.c_cr, sibling)

    def shifted(work):
        for shift, used in ((0, share <= 2), (2, share >= 4)):
            pl.when(used)(lambda: work((shift,)))

    def prepare(slots):
        def work(shifts):
            for slot in slots:

                def one(p, carry):
                    field = b.hs[slot, 1, p, 1:9].astype(f32).reshape(256, 128)
                    put(b.hs.at[slot], p, field, 8, 32, shifts)
                    return carry

                lax.fori_loop(y // 2, y // 2 + 3, one, 0)

        shifted(work)

    hid_copies[0].wait_recv()
    prepare([y * 2 + 1 - core] + [y_of[k] * 2 + core for k in range(1, NY)])

    c_core.wait_recv()
    for yy in range(NY):
        b.c_ys[yy] = (b.dc[core, yy].astype(f32) + b.c_cr[yy].astype(f32)).astype(bf16)
    c_y = [
        send(S.c_y, k - 1, b.c_ys.at[y_of[k]], b.c_yr.at[k - 1], dev(dy=y_of[k]))
        for k in range(1, NY)
    ]

    arrived(rzb_copies)
    both = b.sb[pl.ds(start, 2)].astype(f32)
    for k in range(7):
        both = both + b.rzb[k].astype(f32)
    two_m2 = (two_m2.reshape(2, 16, 128) + both).astype(bf16).astype(f32)
    even = (z % 2 == 0).astype(f32)
    lo, hi = two_m2[0], two_m2[1]
    own_m2 = hi * even + lo * (1.0 - even)
    arrived(halo_d_copies)

    def grad_plane(field, m2):
        return (field.astype(f32) + grow_yz(m2, 2, 8, b.small_s) * 0.125).astype(bf16)

    grad_b = grad_plane(b.gd_own[...], own_m2)
    grad_b32 = grad_b.astype(f32)
    b.gbq[q] = (grad_b32 * flag[1]).astype(bf16)
    gb_copies = to_group(S.gb, b.gbq)
    put(b.gbs, 1, grad_b32, 4, 16)
    put(b.gbs, 0, grad_plane(b.halo_d[0], lo).astype(f32) * has_prev, 4, 16)
    put(b.gbs, 2, grad_plane(b.halo_d[1], hi).astype(f32) * has_next, 4, 16)
    back_b = jnp.zeros((64, 128), f32)
    for t in range(9):
        dx, dy = t // 3, t % 3
        for dz in range(3):
            part = b.gbs[2 - dz, 2 - dx, 2 - dy : 6 - dy].reshape(64, 128)
            back_b = back_b + mm(part, b.wb[t, 128 * dz : 128 * dz + 128, :], NT)
    grad_p = (grad_b32 + scale[1] * slope(lb) * back_b).astype(bf16)
    grad_m1 = mm(grad_p, b.l1[...], NT).astype(bf16).astype(f32)
    b.m1q[q] = (grad_m1 * flag[0]).astype(bf16)
    m1_copies = to_group(S.m1, b.m1q)
    early = len(started)

    arrived(hb_copies)

    def prepare_b(shifts):
        for k in range(1, 8):
            slot = group_of[k][0] * 2 + group_of[k][1]
            for p in range(2):
                plane = y // 2 + p
                field = b.hsb[slot, 1, plane, 1:5].astype(f32).reshape(64, 128)
                put(b.hsb.at[slot], plane, field, 4, 16, shifts)

    shifted(prepare_b)
    arrived(hid_forward)
    prepare([y_from[k] * 2 + 1 - core for k in range(1, NY)])
    arrived(c_y)
    total = b.c_ys[y].astype(f32)
    for k in range(3):
        total = total + b.c_yr[k].astype(f32)
    b.c_zs[...] = total.astype(bf16)
    c_zh = send(S.c_zh, 0, b.c_zs, b.c_zr, dev(dzh=1 - zh))
    arrived(gb_copies)
    where = []
    for i in range(4):
        place = jnp.minimum(4 * share + i, 26)
        dz, e = place // 9, place % 9
        odd = dz % 2
        e = e * (1 - odd) + (8 - e) * odd
        where.append((e // 3, e % 3, dz))

    def keep_sum(kind, i, value):
        for k in range(NXC):
            b.xs[kind, k, i] = value[32 * k : 32 * k + 32].astype(bf16)

    stores = []

    def along_x(kind):
        return [
            send(
                KINDS[kind][0],
                k - 1,
                b.xs.at[kind, x_of[k]],
                b.xr.at[kind, k - 1],
                dev(dx=x_of[k]),
            )
            for k in range(1, NXC)
        ]

    source = ((row // 4) % 4) * 32 + (row // 16) * 4 + row % 4
    shuffle = (col == source).astype(f32).astype(bf16)

    def along_z(kind):
        total = b.xs[kind, x].astype(f32)
        for k in range(3):
            total = total + b.xr[kind, k].astype(f32)
        pieces = mm(shuffle, total.astype(bf16).reshape(128, 128)).astype(bf16)
        b.zs[kind] = pieces.reshape(8, 16, 128)
        copies = []
        for k in sorted(range(1, NZ), key=lambda k: abs(k - NZ // 2)):
            target = dev(dzh=z16_of[k] // NZL, dz=z16_of[k] % NZL)
            src = b.zs.at[kind, z16_of[k] % NZL]
            copies.append(send(KINDS[kind][1], k - 1, src, b.zr.at[kind, z16], target))
        b.zr[kind, z16] = b.zs[kind, z]
        return copies

    def to_all(kind):
        total = b.zr[kind, 0].astype(f32)
        for k in range(1, NZ):
            total = total + b.zr[kind, k].astype(f32)
        b.zt[kind] = total
        own = (fga, fgb)[kind].at[q]
        copies = [
            send(KINDS[kind][2], k - 1, b.zt.at[kind], own, group_dev[k]) for k in range(1, 8)
        ]
        stores.append(pltpu.make_async_copy(b.zt.at[kind], own, local_sem.at[11 + kind]))
        stores[-1].start()
        return copies

    turned_b = mm(unit, b.gbq[...].reshape(512, 128), NT).astype(bf16)
    for i, (dx, dy, dz) in enumerate(where):
        field = b.hsb[:, dz, dx, pl.ds(dy, 4)].reshape(512, 128)
        keep_sum(1, i, mm(turned_b, field) * f32(1.0 / SURVIVAL[1]))
    b_x = along_x(1)
    cot_copies[0].wait_recv()
    arrived(cot_forward)

    coarse = lax.broadcasted_iota(jnp.int32, (64, 512), 0)
    fine = lax.broadcasted_iota(jnp.int32, (64, 512), 1)
    above = ((fine // 64) % 4) * 16 + (fine % 32) // 2
    grow = jnp.where(coarse == above, 0.125, 0.0).astype(bf16)
    for k in (0, 1, 2, 3, 6, 7, 4, 5):
        if k:
            m1_copies[k - 1].wait_recv()
        j = y_from[k // 2] * 2 + (core + k) % 2
        b.gt[j] = (b.cq[j].astype(f32) + mm(b.m1q[j], grow, TN)).astype(bf16)
    for pair in range(2):
        acc = jnp.zeros((128, 256), f32)
        for j in range(8):
            pieces = []
            for i in (2 * pair, 2 * pair + 1):
                dx, dy, dz = where[i]
                pieces.append(b.hs[j, dz, pl.ds(dx, 2), pl.ds(dy, 8)].reshape(512, 128))
            acc = acc + mm(b.gt[j], jnp.concatenate(pieces, axis=1))
        acc = acc * f32(1.0 / SURVIVAL[0])
        keep_sum(0, 2 * pair, acc[:, 0:128])
        keep_sum(0, 2 * pair + 1, acc[:, 128:256])
    a_x = along_x(0)

    arrived(b_x)
    b_z = along_z(1)
    arrived(a_x)
    a_z = along_z(0)
    c_zh.wait_recv()
    b.fc[y] = (b.c_zs[...].astype(f32) + b.c_zr[...].astype(f32)).astype(bf16)
    own_c = b.fc.at[y]
    c_ay = [send(S.c_ay, k - 1, own_c, own_c, dev(dy=y_of[k])) for k in range(1, NY)]
    arrived(rzf_copies)
    both = b.sf[z // 2].astype(f32)
    for k in range(7):
        both = both + b.rzf[k].astype(f32)
    level_d = (level_b + grow_yz(both, 2, 8, b.small_s)).astype(bf16)
    wide = grow_yz(mm(level_d, b.w1[...]), 4, 16, b.grow_s)
    for p in range(2):
        b.rv[p] = (b.la[p] + wide).astype(bf16).reshape(8, 32, 128)
    stores.append(pltpu.make_async_copy(b.rv, res.at[0], local_sem.at[10]))
    stores[-1].start()
    arrived(b_z)
    b_all = to_all(1)
    finish(early)

    arrived(a_z)
    a_all = to_all(0)
    arrived(c_ay)
    stores.append(pltpu.make_async_copy(b.fc, fgc.at[core], local_sem.at[13]))
    stores[-1].start()
    c_ac = send(S.c_ac, 0, b.fc, fgc.at[core], sibling)
    arrived(b_all)
    finish(len(started) - 8)
    c_ac.wait_recv()
    for copy in stores:
        copy.wait()
    arrived(a_all)
    finish(len(started))


OWNER = (0, 6, 4, 1, 2, 3, 5, 7)


def finalize(
    res, fga, fgb, fgc, out, out_a, out_b, out_c, res_v, fg_v, fgc_v, tables, wide, sems
):
    parts = [
        pltpu.make_async_copy(fgc.at[part], fgc_v.at[part], sems.at[part]) for part in range(2)
    ]
    loads = [
        pltpu.make_async_copy(res, res_v, sems.at[2]),
        pltpu.make_async_copy(fga, fg_v.at[0], sems.at[3]),
        pltpu.make_async_copy(fgb, fg_v.at[1], sems.at[4]),
    ]
    for load in parts + loads:
        load.start()
    copies = []

    def store(src, dst):
        copies.append(pltpu.make_async_copy(src, dst, sems.at[5 + len(copies)]))
        copies[-1].start()

    for part in range(2):
        parts[part].wait()
        rows = pl.ds(224 * part, 224 - 16 * part)
        for yy in range(NY):
            wide[rows, 128 * yy : 128 * yy + 128] = fgc_v[part, yy, 0 : 224 - 16 * part].astype(f32)
        store(wide.at[rows], out_c.at[rows])
        if part == 0:
            loads[0].wait()
            store(res_v, out)
    for kind, target in enumerate((out_a, out_b)):
        loads[1 + kind].wait()
        for t in range(27):
            e, dz = t // 3, t % 3
            place = 9 * dz + (8 - e if dz == 1 else e)
            first = 4 * (place % 4)
            tables[kind, t] = fg_v[kind, OWNER[place // 4], first : first + 4]
        store(tables.at[kind], target)
    for copy in copies:
        copy.wait()


def body(
    features,
    cotangent,
    keep_flags,
    conv_a,
    conv_b,
    conv_c,
    lift_one,
    lift_two,
    lower_two,
    lower_one,
):
    hbm = pl.BlockSpec(memory_space=pltpu.HBM)
    result, fga, fgb, fgc = pl.pallas_call(
        kernel,
        out_shape=(
            jax.ShapeDtypeStruct(features.shape, bf16),
            jax.ShapeDtypeStruct((8, 16, 128), f32),
            jax.ShapeDtypeStruct((8, 16, 128), f32),
            jax.ShapeDtypeStruct((2, NY, 224, 128), bf16),
        ),
        in_specs=[hbm] * 10,
        out_specs=(hbm,) * 4,
        scratch_shapes=[pltpu.VMEM(shape, dtype) for shape, dtype in SCRATCH.values()]
        + [
            pltpu.SemaphoreType.DMA((14,)),
            pltpu.SemaphoreType.DMA((TOTAL,)),
            pltpu.SemaphoreType.DMA((TOTAL,)),
        ],
        compiler_params=pltpu.CompilerParams(
            collective_id=0, has_side_effects=True, vmem_limit_bytes=60 * 1024 * 1024
        ),
        cost_estimate=pl.CostEstimate(
            flops=1_400_000_000, bytes_accessed=5_000_000, transcendentals=600_000
        ),
    )(
        features,
        cotangent,
        keep_flags,
        conv_a.reshape(9, 384, 128),
        conv_b.reshape(9, 384, 128),
        conv_c.transpose(0, 2, 1).reshape(432, 512),
        lift_one,
        lift_two,
        lower_two,
        lower_one,
    )

    result, grad_a, grad_b, grad_c = pl.pallas_call(
        finalize,
        out_shape=(
            jax.ShapeDtypeStruct(features.shape, bf16),
            jax.ShapeDtypeStruct((27, 4, 128), f32),
            jax.ShapeDtypeStruct((27, 4, 128), f32),
            jax.ShapeDtypeStruct((432, 512), f32),
        ),
        in_specs=[hbm] * 4,
        out_specs=(hbm,) * 4,
        scratch_shapes=[
            pltpu.VMEM(features.shape, bf16),
            pltpu.VMEM((2, 8, 16, 128), f32),
            pltpu.VMEM((2, NY, 224, 128), bf16),
            pltpu.VMEM((2, 27, 4, 128), f32),
            pltpu.VMEM((432, 512), f32),
            pltpu.SemaphoreType.DMA((10,)),
        ],
        compiler_params=pltpu.CompilerParams(vmem_limit_bytes=60 * 1024 * 1024),
    )(result, fga, fgb, fgc)
    return (
        result,
        grad_a.transpose(0, 2, 1),
        grad_b.transpose(0, 2, 1),
        grad_c.reshape(27, 16, 512).transpose(0, 2, 1),
    )


def solution(mesh):
    return jax.shard_map(
        body,
        mesh=mesh,
        in_specs=(
            P("member", "gx", None, None, None),
            P("member", "gx", None, None, None),
            P("member", None),
            P(),
            P(),
            P(None, None, "gx"),
            P(),
            P(),
            P(),
            P(),
        ),
        out_specs=(
            P("member", "gx", None, None, None),
            P(None, None, "gx"),
            P(None, None, "gx"),
            P(None, None, "gx"),
        ),
        check_vma=False,
    )
```
